128 devices in a mesh: seq: 4 (over x), shard: 8 (over z_lo, y), replica: 4 (over z_hi, core).
Axes of the slice: x: 4, y: 4, z: 4 (z_hi: 2, z_lo: 2; z = z_hi * 2 + z_lo), core: 2. Of those that a mesh axis runs over, the one named last changes fastest.
Arguments:
- tokens: bfloat16 [32, 1024, 1024], P(('shard', 'replica'), 'seq'), may hold values from -6 to 6
- cotangent: bfloat16 [32, 1024, 1024], P(('shard', 'replica'), 'seq'), may hold values from -6 to 6
- w_qkv: float32 [1024, 4096], P(('seq', 'shard')), may hold values from -0.1875 to 0.1875
- w_out: float32 [2048, 1024], P(('seq', 'shard')), may hold values from -0.75 to 0.75
- w_gu: float32 [1024, 6144], P(('seq', 'shard')), may hold values from -0.1875 to 0.1875
- w_down: float32 [3072, 1024], P(('seq', 'shard')), may hold values from -0.109375 to 0.109375
- gains: float32 [2304], P(('seq', 'shard')), may hold values from 0.5 to 2, as said below
- first_qkv: float32 [1024, 4096], P(('seq', 'shard')), may hold values from -64 to 64
- first_out: float32 [2048, 1024], P(('seq', 'shard')), may hold values from -16 to 16
- first_gu: float32 [1024, 6144], P(('seq', 'shard')), may hold values from -40 to 40
- first_down: float32 [3072, 1024], P(('seq', 'shard')), may hold values from -64 to 64
- first_gains: float32 [2304], P(('seq', 'shard')), may hold values from -192 to 192
- second_qkv: float32 [1024, 4096], P(('seq', 'shard')), may hold values from 425.984 to 1736.704
- second_out: float32 [2048, 1024], P(('seq', 'shard')), may hold values from 29.4912 to 117.9648
- second_gu: float32 [1024, 6144], P(('seq', 'shard')), may hold values from 209.7152 to 851.968
- second_down: float32 [3072, 1024], P(('seq', 'shard')), may hold values from 622.592 to 2490.368
- second_gains: float32 [2304], P(('seq', 'shard')), may hold values from 3932.16 to 15400.96
Outputs:
- mixed: bfloat16 [32, 1024, 1024], P(('shard', 'replica'), 'seq')
- input_grad: float32 [32, 1024, 1024], P(('shard', 'replica'), 'seq')
- new_qkv: float32 [1024, 4096], P(('seq', 'shard'))
- new_first_qkv: float32 [1024, 4096], P(('seq', 'shard'))
- new_second_qkv: float32 [1024, 4096], P(('seq', 'shard'))
- new_out: float32 [2048, 1024], P(('seq', 'shard'))
- new_first_out: float32 [2048, 1024], P(('seq', 'shard'))
- new_second_out: float32 [2048, 1024], P(('seq', 'shard'))
- new_gu: float32 [1024, 6144], P(('seq', 'shard'))
- new_first_gu: float32 [1024, 6144], P(('seq', 'shard'))
- new_second_gu: float32 [1024, 6144], P(('seq', 'shard'))
- new_down: float32 [3072, 1024], P(('seq', 'shard'))
- new_first_down: float32 [3072, 1024], P(('seq', 'shard'))
- new_second_down: float32 [3072, 1024], P(('seq', 'shard'))
- new_gains: float32 [2304], P(('seq', 'shard'))
- new_first_gains: float32 [2304], P(('seq', 'shard'))
- new_second_gains: float32 [2304], P(('seq', 'shard'))
The draws below stay inside these ranges and needn't reach their ends.
Inputs may be any that keep to these rules, and one draw needn't show every extreme that they name: Positive gains.
All inputs are finite; a program needn't handle non-finite values.
Results may differ from the reference program's by a relative error of at most 0.015.
The reference program's roundings to bfloat16 on the way count: a program that leaves them out, or rounds other values in their place, can miss the bound.
Values may be sent and summed in bfloat16 or wider, within the bound.
No kernel may reach another device: no remote copies, remote signals or barrier semaphores. Data moves between devices by JAX's collectives and lax.ppermute only.
A program may use at most 384 MiB of HBM per device.

```python
import math
import jax
import jax.numpy as jnp
from jax import lax

D = 1024
HEADS = 16
KVH = 8
HD = 128
FF = 3072
STEP = 10
QW = 2048
QKV = 4096
GN = 2304
LENGTH = 1024
SEQS = 32


def draw_gains(key, part):
    key = jax.random.fold_in(key, 11)
    norm_key, head_key = jax.random.split(key)
    norm_part = jax.random.uniform(norm_key, (2 * D,), jnp.float32, 0.5, 1.5)
    head_part = jax.random.uniform(head_key, (2 * HD,), jnp.float32, 1.0, 2.0)
    return jnp.concatenate([norm_part, head_part])


def block_levels(key, dims, cuts, smallest, top_value):
    def one(axis_at, blocks):
        draws = jax.random.uniform(jax.random.fold_in(jax.random.fold_in(key, 6), axis_at), (blocks,), jnp.float32, smallest / len(cuts), top_value / len(cuts))
        return jnp.repeat(jnp.exp(draws), dims[axis_at] // blocks).reshape((-1,) + (1,) * (len(dims) - axis_at - 1))

    factor_of = one(*cuts[0])
    for cut in cuts[1:]:
        factor_of = factor_of * one(*cut)
    return factor_of


def noise(own_key, dims, scale, reach, shards=(), kind=jnp.bfloat16):
    values = jax.random.normal(own_key, dims, jnp.float32) * scale
    if len(shards) > 0:
        values = block_levels(own_key, dims, shards, -0.22, 0.18) * values
    return jnp.clip(values, min=-reach, max=reach).astype(kind)


def setup_inputs(seed: int = 0) -> dict:
    key_of = jax.random.split(jax.random.key(seed), 18)
    return {
        "tokens": noise(key_of[0], (SEQS, LENGTH, D), 1.0, 6.0, ((0, 32), (1, 4))),
        "cotangent": noise(key_of[1], (SEQS, LENGTH, D), 1.0, 6.0, ((0, 32), (1, 4))),
        "w_qkv": noise(key_of[2], (D, QKV), D ** -0.5, 0.1875, ((0, 32),), jnp.float32),
        "w_out": noise(key_of[3], (QW, D), 64 ** -0.5, 0.75, ((0, 32),), jnp.float32),
        "w_gu": noise(key_of[4], (D, 2 * FF), D ** -0.5, 0.1875, ((0, 32),), jnp.float32),
        "w_down": noise(key_of[5], (FF, D), FF ** -0.5, 0.109375, ((0, 32),), jnp.float32),
        "gains": draw_gains(jax.random.fold_in(key_of[17], 71), 0),
        "first_qkv": noise(key_of[7], (D, QKV), (0.056 * (SEQS * LENGTH) ** 0.5), 64.0, ((0, 32),), jnp.float32),
        "first_out": noise(key_of[8], (QW, D), (0.0144 * (SEQS * LENGTH) ** 0.5), 16.0, ((0, 32),), jnp.float32),
        "first_gu": noise(key_of[9], (D, 2 * FF), (0.039 * (SEQS * LENGTH) ** 0.5), 40.0, ((0, 32),), jnp.float32),
        "first_down": noise(key_of[10], (FF, D), (0.067 * (SEQS * LENGTH) ** 0.5), 64.0, ((0, 32),), jnp.float32),
        "first_gains": noise(key_of[11], (GN,), (0.17 * (SEQS * LENGTH) ** 0.5), 192.0, ((0, 32),), jnp.float32),
        "second_qkv": jnp.clip(jnp.exp(math.log(1736.704) - 1.40534252 * jax.random.uniform(key_of[12], (D, QKV), jnp.float32) ** block_levels(key_of[12], (D, QKV), ((0, 32),), -0.2, 0.2)), 425.984, 1736.704),
        "second_out": jnp.clip(jnp.exp(math.log(117.9648) - 1.3862944 * jax.random.uniform(key_of[13], (QW, D), jnp.float32) ** block_levels(key_of[13], (QW, D), ((0, 32),), -0.2, 0.2)), 29.4912, 117.9648),
        "second_gu": jnp.clip(jnp.exp(math.log(851.968) - 1.4017986 * jax.random.uniform(key_of[14], (D, 2 * FF), jnp.float32) ** block_levels(key_of[14], (D, 2 * FF), ((0, 32),), -0.2, 0.2)), 209.7152, 851.968),
        "second_down": jnp.clip(jnp.exp(math.log(2490.368) - 1.3862944 * jax.random.uniform(key_of[15], (FF, D), jnp.float32) ** block_levels(key_of[15], (FF, D), ((0, 32),), -0.2, 0.2)), 622.592, 2490.368),
        "second_gains": jnp.clip(jnp.exp(math.log(15400.96) - 1.36524097 * jax.random.uniform(key_of[16], (GN,), jnp.float32) ** block_levels(key_of[16], (GN,), ((0, 32),), -0.2, 0.2)), 3932.16, 15400.96),
    }


@jax.custom_vjp
def low(v):
    return lax.optimization_barrier(v.astype(jnp.bfloat16)).astype(jnp.float32)

@jax.custom_vjp
def low_back(v):
    return v

def low_keep(v):
    return (low(v), None)

def low_pass(kept, grad):
    return (grad,)

def back_keep(v):
    return (v, None)

def back_low(kept, grad):
    return (low(grad),)
low.defvjp(low_keep, low_pass)
low_back.defvjp(back_keep, back_low)
EPS = 1e-06
THETA = 1000000.0
BETA_ONE = 0.9
BETA_TWO = 0.95
ADAM_EPS = 1e-08
RATES = (0.04, 0.2, 0.04, 0.03, 0.4)
DECAYS = (0.1, 0.1, 0.1, 0.1, 0.0)
NEG_FILL = -1e+30
HIGHEST = lax.Precision.HIGHEST

def matmul_high(left, right):
    return jnp.matmul(left, right, precision=HIGHEST)

def rms_scale(value, gain):
    return value * lax.rsqrt(lax.optimization_barrier(jnp.mean(value * value, axis=-1, keepdims=True)) + EPS) * gain

def rotary(positions, half_dim):
    frequency = THETA ** (-jnp.arange(half_dim, dtype=jnp.float32) / half_dim)
    angles = positions[:, None] * frequency[None, :]
    return (jnp.cos(angles)[:, None, :], jnp.sin(angles)[:, None, :])

def rotate(value, cos_table, sin_table):
    half_dim = value.shape[-1] // 2
    lower = value[..., :half_dim]
    upper = value[..., half_dim:]
    return jnp.concatenate([lower * cos_table - upper * sin_table, upper * cos_table + lower * sin_table], axis=-1)

def forward(params, inputs):
    w_qkv, w_out, w_gu, w_down, gains = params
    gain_vals = low(gains)
    seq_count, length = (inputs.shape[0], inputs.shape[1])
    q_width = HEADS * HD
    kv_width = KVH * HD
    normed_one = low(rms_scale(inputs, gain_vals[:D]))
    projected = low_back(matmul_high(normed_one, low(w_qkv)))
    queries = projected[..., :q_width].reshape(seq_count, length, HEADS, HD)
    keys_pre = projected[..., q_width:q_width + kv_width].reshape(seq_count, length, KVH, HD)
    values_pre = projected[..., q_width + kv_width:].reshape(seq_count, length, KVH, HD)
    cos_table, sin_table = rotary(jnp.arange(length, dtype=jnp.float32), HD // 2)
    factor = 1.0 / math.sqrt(HD)
    rot_q = low(rotate(rms_scale(queries, gain_vals[2 * D:2 * D + HD]), cos_table, sin_table) * factor)
    rot_k = low(rotate(rms_scale(keys_pre, gain_vals[2 * D + HD:]), cos_table, sin_table))
    low_v = low(values_pre)
    grouped = rot_q.reshape(seq_count, length, KVH, HEADS // KVH, HD)
    scores = low_back(jnp.einsum('bqkgd,bskd->bkgqs', grouped, rot_k, precision=HIGHEST))
    positions = jnp.arange(length, dtype=jnp.int32)
    causal = positions[None, :] <= positions[:, None]
    scores = jnp.where(causal, scores, NEG_FILL)
    attn_weights = jax.nn.softmax(scores, axis=-1)
    attended = jnp.einsum('bkgqs,bskd->bqkgd', low(attn_weights), low_v, precision=HIGHEST)
    attended = low_back(low(attended.reshape(seq_count, length, q_width)))
    state = inputs + low_back(matmul_high(attended, low(w_out)))
    normed_two = low(rms_scale(state, gain_vals[D:2 * D]))
    gate_up = low_back(matmul_high(normed_two, low(w_gu)))
    hidden = low(jax.nn.silu(gate_up[..., :FF]) * gate_up[..., FF:])
    return state + low_back(matmul_high(hidden, low(w_down)))

def adamw(weight, gradient, first_moment, second_moment, rate, decay_rate):
    first_moment = BETA_ONE * first_moment + (1.0 - BETA_ONE) * gradient
    second_moment = BETA_TWO * second_moment + (1.0 - BETA_TWO) * gradient * gradient
    first_hat = first_moment / (1.0 - BETA_ONE ** STEP)
    second_hat = second_moment / (1.0 - BETA_TWO ** STEP)
    weight = weight - rate * (first_hat / (jnp.sqrt(second_hat) + ADAM_EPS) + decay_rate * weight)
    return (weight, first_moment, second_moment)

def reference(tokens, cotangent, w_qkv, w_out, w_gu, w_down, gains, first_qkv, first_out, first_gu, first_down, first_gains, second_qkv, second_out, second_gu, second_down, second_gains):
    params = (w_qkv, w_out, w_gu, w_down, gains)
    seq_count, length = (tokens.shape[0], tokens.shape[1])
    per_step = math.gcd(seq_count, max(1, 2048 // length))
    inputs = tokens.astype(jnp.float32).reshape(seq_count // per_step, per_step, length, D)
    grads_in = cotangent.astype(jnp.float32).reshape(seq_count // per_step, per_step, length, D)

    def one_step(carried, pieces):
        value_out, pull_back = jax.vjp(forward, params, pieces[0])
        weight_grads, input_grad = pull_back(pieces[1])
        carried = jax.tree.map(lambda left, right: left + right, carried, weight_grads)
        return (carried, (value_out.astype(jnp.bfloat16), input_grad))
    start_grads = jax.tree.map(jnp.zeros_like, params)
    totals, (mixed, input_grad) = lax.scan(one_step, start_grads, (inputs, grads_in))
    mixed = mixed.reshape(seq_count, length, D)
    input_grad = input_grad.reshape(seq_count, length, D)
    firsts = (first_qkv, first_out, first_gu, first_down, first_gains)
    seconds = (second_qkv, second_out, second_gu, second_down, second_gains)
    updated = [adamw(params[member], totals[member], firsts[member], seconds[member], RATES[member], DECAYS[member]) for member in range(5)]
    return (mixed, input_grad, updated[0][0], updated[0][1], updated[0][2], updated[1][0], updated[1][1], updated[1][2], updated[2][0], updated[2][1], updated[2][2], updated[3][0], updated[3][1], updated[3][2], updated[4][0], updated[4][1], updated[4][2])
```

```python
import math

import jax
import jax.numpy as jnp
import numpy as np
from jax import lax
from jax.experimental import pallas as pl
from jax.experimental.pallas import tpu as pltpu
from jax.sharding import PartitionSpec as P

HEADS = 16
KVH = 8
HD = 128
FF = 3072
STEP = 10
EPS = 1e-06
THETA = 1000000.0
BETA_ONE = 0.9
BETA_TWO = 0.95
ADAM_EPS = 1e-08
RATES = (0.04, 0.2, 0.04, 0.03, 0.4)
DECAYS = (0.1, 0.1, 0.1, 0.1, 0.0)
NEG_FILL = -1e30

AXES = ("seq", "shard", "replica")
DEVICES = 128
BLOCK = 256
BF = jnp.bfloat16
F32 = jnp.float32
VMEM_LIMIT = 56 * 1024 * 1024


def place_of(device):
    replica, shard, x = device % 4, (device // 4) % 8, device // 32
    return x, shard % 4, (replica // 2) * 2 + shard // 4, replica % 2


def device_at(x, y, z, k):
    return (x * 8 + (z % 2) * 4 + y) * 4 + (z // 2) * 2 + k


def flip(dim, x, y, z, k):
    return {
        "a": (x ^ 1, y, z, k),
        "b": (3 - x, y, z, k),
        "c": (x, y ^ 1, z, k),
        "d": (x, 3 - y, z, k),
        "e": (x, y, z ^ 1, k),
        "f": (x, y, 3 - z, k),
        "h": (x, y, z ^ 2, k),
        "k": (x, y, z, k ^ 1),
    }[dim]


def quarter_of(x, k):
    return k if x < 2 else 3 - k


def partners(dims):
    pairs = []
    for device in range(DEVICES):
        place = place_of(device)
        pairs.append((device, device_at(*flip(dims[place[3]], *place))))
    return pairs


def swap(value, dims):
    return lax.ppermute(value, AXES, partners(dims))


def home_pairs():
    pairs = []
    for device in range(DEVICES):
        x, y, z, k = place_of(device)
        moved = {(0, 1): (1, 0), (1, 0): (0, 1), (2, 0): (3, 1), (3, 1): (2, 0)}.get((x, k), (x, k))
        pairs.append((device, device_at(moved[0], y, z, moved[1])))
    return pairs


def rehome(value):
    return lax.ppermute(value, AXES, home_pairs())


def spread(value, steps):
    for dims in steps:
        value = jnp.concatenate([value, swap(value, dims)], axis=0)
    return value


def shard_of(place):
    return (place[2] % 2) * 4 + place[1]


def slot_places(device, steps):
    places = [place_of(device)]
    for dims in steps:
        places = places + [flip(dims[p[3]], *p) for p in places]
    return places


def row_table(steps):
    table = np.zeros((DEVICES, 32), np.int32)
    for device in range(DEVICES):
        slots = slot_places(device, ("bb", "aa") + tuple(steps))
        table[device] = [p[0] * 8 + shard_of(p) for p in slots]
    return table


def shard_table(steps):
    table = np.zeros((DEVICES, 8), np.int32)
    for device in range(DEVICES):
        table[device] = [shard_of(p) for p in slot_places(device, steps)]
    return table


STEPS_Q = ("cd", "ef", "dc")
STEPS_KV = ("dc", "cd", "ef")
STEPS_ROWS = ("cd", "dc", "ef")
ROWS_Q = row_table(STEPS_Q)
ROWS_KV = row_table(STEPS_KV)
ROWS_SHARD = shard_table(STEPS_ROWS)


def natural_rows():
    table = np.zeros((DEVICES, 32), np.int32)
    for device in range(DEVICES):
        xs = [p[0] for p in slot_places(device, ("bb", "aa"))]
        table[device] = [x * 8 + shard for shard in range(8) for x in xs]
    return table


ROWS_GU = natural_rows()


def block_table():
    table = np.zeros((DEVICES, 4), np.int32)
    for device in range(DEVICES):
        x, _, _, k = place_of(device)
        own = quarter_of(x, k)
        table[device] = [own, own ^ 1, own ^ 3, own ^ 2]
    return table


BLOCKS = block_table()
X_SLOTS = np.array([[(0, 2, 3, 1)[own ^ x] for x in range(4)] for own in range(4)], np.int32)


def dot(left, right):
    return lax.dot_general(left, right, (((1,), (0,)), ((), ())), preferred_element_type=F32)


def dot_nt(left, right):
    return lax.dot_general(left, right, (((1,), (1,)), ((), ())), preferred_element_type=F32)


def dot_tn(left, right):
    return lax.dot_general(left, right, (((0,), (0,)), ((), ())), preferred_element_type=F32)


def at(index, size):
    return pl.ds(pl.multiple_of(index * size, size), size)


def causal_scores(queries, keys, block):
    scores = dot_nt(queries, keys)
    row = lax.broadcasted_iota(jnp.int32, scores.shape, 0) & (BLOCK - 1)
    col = lax.broadcasted_iota(jnp.int32, scores.shape, 1)
    return jnp.where(col <= row + block * BLOCK, scores, NEG_FILL)


def softmax_rows(scores):
    exponent = jnp.exp(scores - jnp.max(scores, axis=1, keepdims=True))
    return exponent * (1.0 / jnp.sum(exponent, axis=1, keepdims=True))


def attention_kernel(
    rows_q, rows_kv, blocks, n1, w_q, w_kv, cos, sin, gain_q, gain_k, w_all, pre, q_out, k_out, v_out, att
):
    factor = 1.0 / math.sqrt(HD)
    for slot in range(32):
        w_all[at(rows_q[slot], 32), 0:512] = w_q[slot]
        w_all[at(rows_kv[slot], 32), 512:1024] = w_kv[slot]
    for slot in range(4):
        block = blocks[slot]
        here = at(block, BLOCK)
        projected = dot(n1[slot * BLOCK : (slot + 1) * BLOCK, :], w_all[...])
        pre[here, :] = projected[:, :768]
        cos_part = cos[here, :]
        sin_part = sin[here, :]

        def turned(column, gain):
            head = projected[:, column : column + HD]
            normed = head * lax.rsqrt(jnp.mean(head * head, axis=1, keepdims=True) + EPS) * gain[...]
            return normed * cos_part + pltpu.roll(normed, HD // 2, 1) * sin_part

        for head in range(4):
            rotated = (turned(head * HD, gain_q) * factor).astype(BF)
            q_out[head // 2, block, (head % 2) * BLOCK : (head % 2 + 1) * BLOCK, :] = rotated
        for head in range(2):
            k_out[head, here, :] = turned(512 + head * HD, gain_k).astype(BF)
            v_out[head, here, :] = projected[:, 768 + head * HD : 768 + (head + 1) * HD].astype(BF)
    for group in range(2):
        for block in range(4):
            width = (block + 1) * BLOCK
            scores = causal_scores(q_out[group, block], k_out[group, :width, :], block)
            weights = softmax_rows(scores).astype(BF)
            attended = dot(weights, v_out[group, :width, :]).astype(BF)
            own = blocks[0] ^ block
            slot = own ^ (own >> 1)
            for head in range(2):
                column = (group * 2 + head) * HD
                att[at(slot, BLOCK), column : column + HD] = attended[head * BLOCK : (head + 1) * BLOCK]


def attention_back_kernel(
    blocks, grad_state, w_out, queries, keys, values, pre, cos, sin, gain_q, gain_k,
    grad_pre, grad_gain_q, grad_gain_k, grad_att,
):
    factor = 1.0 / math.sqrt(HD)
    for slot in range(4):
        part = dot_nt(grad_state[slot * BLOCK : (slot + 1) * BLOCK, :], w_out[...]).astype(BF)
        for head in range(4):
            grad_att[head // 2, blocks[slot], (head % 2) * BLOCK : (head % 2 + 1) * BLOCK, :] = part[
                :, head * HD : (head + 1) * HD
            ]

    def back_through(grad, head, cos_part, sin_part, gain):
        turned = grad * cos_part - pltpu.roll(grad, HD // 2, 1) * sin_part
        scale = lax.rsqrt(jnp.mean(head * head, axis=1, keepdims=True) + EPS)
        unit = head * scale
        scaled = turned * gain[...]
        grad_head = scale * (scaled - unit * jnp.mean(scaled * unit, axis=1, keepdims=True))
        return grad_head, jnp.sum(turned * unit, axis=0, keepdims=True)

    total_q = jnp.zeros((1, HD), F32)
    total_k = jnp.zeros((1, HD), F32)
    for group in range(2):
        grad_k = [jnp.zeros((BLOCK, HD), F32) for _ in range(4)]
        grad_v = [jnp.zeros((BLOCK, HD), F32) for _ in range(4)]
        for block in range(4):
            width = (block + 1) * BLOCK
            own = blocks[0] ^ block
            there = at(own ^ (own >> 1), BLOCK)
            query = queries[group, block]
            probs = softmax_rows(causal_scores(query, keys[group, :width, :], block))
            grad_o = grad_att[group, block]
            grad_probs = dot_nt(grad_o, values[group, :width, :])
            inner = jnp.sum(probs * grad_probs, axis=1, keepdims=True)
            grad_scores = (probs * (grad_probs - inner)).astype(BF)
            low_probs = probs.astype(BF)
            grad_q = dot(grad_scores, keys[group, :width, :]) * factor
            for head in range(2):
                column = (group * 2 + head) * HD
                grad_head, gain_part = back_through(
                    grad_q[head * BLOCK : (head + 1) * BLOCK],
                    pre[block * BLOCK : (block + 1) * BLOCK, column : column + HD],
                    cos[block * BLOCK : (block + 1) * BLOCK, :],
                    sin[block * BLOCK : (block + 1) * BLOCK, :],
                    gain_q,
                )
                total_q = total_q + gain_part
                grad_pre[there, column : column + HD] = grad_head.astype(BF)
            part_k = dot_tn(grad_scores, query)
            part_v = dot_tn(low_probs, grad_o)
            for key_block in range(block + 1):
                rows = slice(key_block * BLOCK, (key_block + 1) * BLOCK)
                grad_k[key_block] = grad_k[key_block] + part_k[rows]
                grad_v[key_block] = grad_v[key_block] + part_v[rows]
        for block in range(4):
            own = blocks[0] ^ block
            there = at(own ^ (own >> 1), BLOCK)
            column = 512 + group * HD
            grad_head, gain_part = back_through(
                grad_k[block],
                pre[block * BLOCK : (block + 1) * BLOCK, column : column + HD],
                cos[block * BLOCK : (block + 1) * BLOCK, :],
                sin[block * BLOCK : (block + 1) * BLOCK, :],
                gain_k,
            )
            total_k = total_k + gain_part
            grad_pre[there, column : column + HD] = grad_head.astype(BF)
            grad_pre[there, 768 + group * HD : 768 + (group + 1) * HD] = grad_v[block].astype(BF)
    grad_gain_q[...] = total_q
    grad_gain_k[...] = total_k


def out_kernel(rows, att, w_slots, w_out, keep, send):
    for slot in range(8):
        w_out[at(rows[slot], 64), :] = w_slots[slot]
    for slot in range(4):
        part = dot(att[slot * BLOCK : (slot + 1) * BLOCK, :], w_out[...])
        target = keep if slot % 2 == 0 else send
        target[slot // 2] = part.astype(target.dtype)


def mlp_kernel(
    rows_gu, rows_down, n2, grad_mix, w_gu_slots, w_down_slots,
    hidden, grad_gu, mix_keep, mix_send, grad_keep, grad_send, w_gu, w_down,
):
    for slot in range(32):
        w_gu[at(rows_gu[slot], 32), :] = w_gu_slots[slot]
    for slot in range(8):
        w_down[at(rows_down[slot], 96), :] = w_down_slots[slot]
    half = FF // 4
    for slot in range(2):
        here = slice(slot * BLOCK, (slot + 1) * BLOCK)
        gate_up = dot(n2[here, :], w_gu[...])
        grad_hidden = dot_nt(grad_mix[here, :], w_down[...])
        gate = gate_up[:, :half]
        up = gate_up[:, half:]
        sigmoid = 1.0 / (1.0 + jnp.exp(-gate))
        silu = gate * sigmoid
        low_hidden = (silu * up).astype(BF)
        hidden[here, :] = low_hidden
        grad_gate = grad_hidden * up * (sigmoid * (1.0 + gate * (1.0 - sigmoid)))
        low_grad = jnp.concatenate([grad_gate, grad_hidden * silu], axis=1).astype(BF)
        grad_gu[here, :] = low_grad
        mix = mix_keep if slot == 0 else mix_send
        back = grad_keep if slot == 0 else grad_send
        back[...] = dot_nt(low_grad, w_gu[...]).astype(back.dtype)
        mix[...] = dot(low_hidden, w_down[...]).astype(mix.dtype)


def mlp_weights_kernel(
    x_slots, n2_own, n2_far, hidden_own, hidden_far, mix_own, mix_far, gu_own, gu_far, grad_gu, grad_down
):
    for x in range(4):
        here = slice(x * BLOCK, (x + 1) * BLOCK)
        part = dot_tn(n2_own[:, here], gu_own[...]) + dot_tn(n2_far[:, here], gu_far[...])
        grad_gu[:, x_slots[x], :, :] = part.astype(BF).reshape(8, 32, 2 * FF // 4)
    for third in range(3):
        here = slice(third * BLOCK, (third + 1) * BLOCK)
        part = dot_tn(hidden_own[:, here], mix_own[...]) + dot_tn(hidden_far[:, here], mix_far[...])
        grad_down[here, :] = part.astype(BF)


def qkv_weights_kernel(rows_q, rows_kv, n1, grad_pre, grad_q, grad_kv, total):
    for x in range(4):
        here = slice(x * BLOCK, (x + 1) * BLOCK)
        total[here, :] = dot_tn(n1[:, here], grad_pre[...]).astype(BF)
    for slot in range(32):
        grad_q[slot] = total[at(rows_q[slot], 32), 0:512]
        grad_kv[slot] = total[at(rows_kv[slot], 32), 512:1024]


def input_kernel(grad_pre, w_all, keep, send):
    for slot in range(4):
        part = dot_nt(grad_pre[slot * BLOCK : (slot + 1) * BLOCK, :], w_all[...])
        target = keep if slot % 2 == 0 else send
        target[slot // 2] = part.astype(target.dtype)


def call(kernel, outs, args, scalars, scratch=(), flops=0):
    space = [pl.BlockSpec(memory_space=pltpu.SMEM)] * scalars
    space += [pl.BlockSpec(memory_space=pltpu.VMEM)] * (len(args) - scalars)
    size = sum(math.prod(a.shape) * a.dtype.itemsize for a in list(args) + list(outs))
    return pl.pallas_call(
        kernel,
        out_shape=outs,
        in_specs=space,
        out_specs=[pl.BlockSpec(memory_space=pltpu.VMEM)] * len(outs),
        scratch_shapes=list(scratch),
        compiler_params=pltpu.CompilerParams(vmem_limit_bytes=VMEM_LIMIT),
        cost_estimate=pl.CostEstimate(flops=flops, bytes_accessed=size, transcendentals=0),
    )(*args)


def struct(shape, dtype):
    return jax.ShapeDtypeStruct(shape, dtype)


def rms_scale(value, gain):
    return value * lax.rsqrt(jnp.mean(value * value, axis=-1, keepdims=True) + EPS) * gain


def rms_back(value, gain, grad):
    scale = lax.rsqrt(jnp.mean(value * value, axis=-1, keepdims=True) + EPS)
    scaled = grad * gain
    inner = jnp.mean(scaled * value, axis=-1, keepdims=True)
    grad_value = scale * scaled - value * (scale * scale * scale) * inner
    return grad_value, jnp.sum(grad * value * scale, axis=0)


def adamw(weight, gradient, first_moment, second_moment, rate, decay_rate):
    first_moment = BETA_ONE * first_moment + (1.0 - BETA_ONE) * gradient
    second_moment = BETA_TWO * second_moment + (1.0 - BETA_TWO) * gradient * gradient
    first_hat = first_moment / (1.0 - BETA_ONE**STEP)
    second_hat = second_moment / (1.0 - BETA_TWO**STEP)
    weight = weight - rate * (first_hat / (jnp.sqrt(second_hat) + ADAM_EPS) + decay_rate * weight)
    return (weight, first_moment, second_moment)


def fold(value, steps):
    for dims in reversed(steps):
        half = value.shape[0] // 2
        got = swap(value[half:].astype(BF), dims)
        value = value[:half].astype(F32) + got.astype(F32)
    return value


def rounded(value):
    return lax.reduce_precision(value.astype(F32), 8, 7)


def both(value, dims):
    low = rounded(value)
    return low + swap(low.astype(BF), dims).astype(F32)


def pick(stack, index):
    return lax.dynamic_index_in_dim(stack, index, 0, keepdims=False)


def on_device(
    tokens,
    cotangent,
    w_qkv,
    w_out,
    w_gu,
    w_down,
    gains,
    first_qkv,
    first_out,
    first_gu,
    first_down,
    first_gains,
    second_qkv,
    second_out,
    second_gu,
    second_down,
    second_gains,
):
    width = tokens.shape[-1]
    x_at = lax.axis_index("seq")
    shard_at = lax.axis_index("shard")
    replica_at = lax.axis_index("replica")
    device = (x_at * 8 + shard_at) * 4 + replica_at
    core = replica_at % 2
    quarter = jnp.where(x_at < 2, core, 3 - core)
    rows_q = pick(jnp.asarray(ROWS_Q), device)
    rows_kv = pick(jnp.asarray(ROWS_KV), device)
    rows_shard = pick(jnp.asarray(ROWS_SHARD), device)
    rows_gu = pick(jnp.asarray(ROWS_GU), device)
    blocks = pick(jnp.asarray(BLOCKS), device)
    x_slots = pick(jnp.asarray(X_SLOTS), x_at)

    low_qkv = w_qkv.astype(BF)
    stack_q = jnp.stack([low_qkv[:, 512 * n : 512 * (n + 1)] for n in range(4)])
    stack_kv = jnp.stack(
        [
            jnp.concatenate(
                [low_qkv[:, 2048 + 256 * n : 2304 + 256 * n], low_qkv[:, 3072 + 256 * n : 3328 + 256 * n]],
                axis=1,
            )
            for n in range(4)
        ]
    )
    stack_qkv = jnp.concatenate([stack_q, stack_kv], axis=2)
    mine = pick(stack_qkv, quarter)[None]
    mine = jnp.concatenate([mine, swap(pick(stack_qkv, 3 - quarter)[None], "bb")], axis=0)
    mine = jnp.concatenate([mine, swap(mine, "aa")], axis=0)
    slots_q = spread(mine[:, :, :512], STEPS_Q)
    slots_kv = spread(mine[:, :, 512:], STEPS_KV)

    own_tokens = rehome(tokens[0])
    far_tokens = swap(own_tokens, "bb")
    side_tokens = swap(jnp.stack([own_tokens, far_tokens]), "kk")
    all_tokens = jnp.concatenate([own_tokens, side_tokens[0], far_tokens, side_tokens[1]], axis=0)

    spot = (jnp.arange(32) == x_at * 8 + shard_at)[:, None]
    gain_vals = jnp.where(spot, rounded(gains)[None, :], 0.0)
    gain_vals = jnp.pad(gain_vals.reshape(-1), (0, 768)).reshape(24, 128)
    for dims in ("bb", "aa", "cd", "dc", "ef"):
        gain_vals = gain_vals + swap(gain_vals, dims)
    gain_vals = gain_vals.reshape(-1)[: 2 * width + 2 * HD]
    gain_one = gain_vals[:width]
    gain_two = gain_vals[width : 2 * width]
    gain_query = gain_vals[2 * width : 2 * width + HD].reshape(1, HD)
    gain_key = gain_vals[2 * width + HD :].reshape(1, HD)

    slots_out = spread(rehome(w_out.astype(BF))[None], STEPS_ROWS)
    slots_down = spread(rehome(w_down.astype(BF))[None], STEPS_ROWS)

    low_gu = w_gu.astype(BF)
    part = FF // 4
    stack_gu = jnp.stack(
        [
            jnp.concatenate(
                [low_gu[:, part * n : part * (n + 1)], low_gu[:, FF + part * n : FF + part * (n + 1)]], axis=1
            )
            for n in range(4)
        ]
    )
    mine_gu = pick(stack_gu, quarter)[None]
    mine_gu = jnp.concatenate([mine_gu, swap(pick(stack_gu, 3 - quarter)[None], "bb")], axis=0)
    mine_gu = jnp.concatenate([mine_gu, swap(mine_gu, "aa")], axis=0)
    slots_gu = lax.all_gather(mine_gu, "shard", axis=0, tiled=True)

    own_mix = rehome(cotangent[0])
    side_mix = swap(own_mix, "kk")
    near_mix = jnp.concatenate([own_mix, side_mix], axis=0)
    other_mix = swap(own_mix, "bb")
    far_mix = jnp.concatenate([other_mix, swap(other_mix, "kk")], axis=0)

    positions = jnp.arange(4 * BLOCK, dtype=F32)
    frequency = THETA ** (-jnp.arange(HD // 2, dtype=F32) / (HD // 2))
    angles = positions[:, None] * frequency[None, :]
    cos_half, sin_half = jnp.cos(angles), jnp.sin(angles)
    cos_table = jnp.concatenate([cos_half, cos_half], axis=1)
    sin_table = jnp.concatenate([-sin_half, sin_half], axis=1)

    n1 = rms_scale(all_tokens.astype(F32), gain_one).astype(BF)
    total = 4 * BLOCK
    w_all, pre, queries, keys, values, att = call(
        attention_kernel,
        [
            struct((width, 1024), BF),
            struct((total, 768), F32),
            struct((2, 4, 2 * BLOCK, HD), BF),
            struct((2, total, HD), BF),
            struct((2, total, HD), BF),
            struct((total, 512), BF),
        ],
        [rows_q, rows_kv, blocks, n1, slots_q, slots_kv, cos_table, sin_table, gain_query, gain_key],
        3,
        flops=3_600_000_000,
    )
    w_out_all, out_keep, out_send = call(
        out_kernel,
        [struct((512, width), BF), struct((2, BLOCK, width), F32), struct((2, BLOCK, width), BF)],
        [rows_shard, att, slots_out],
        1,
        flops=1_080_000_000,
    )
    out_half = out_keep + swap(out_send, "kk").astype(F32)
    out_full = out_half[0] + swap(out_half[1].astype(BF), "bb").astype(F32)
    inputs = own_tokens.astype(F32)
    state = inputs + out_full
    n2 = rms_scale(state, gain_two).astype(BF)
    near_n2 = jnp.concatenate([n2, swap(n2, "kk")], axis=0)
    other_n2 = swap(n2, "bb")
    far_n2 = jnp.concatenate([other_n2, swap(other_n2, "kk")], axis=0)

    def mlp(n2_part, mix_part):
        return call(
            mlp_kernel,
            [
                struct((2 * BLOCK, part), BF),
                struct((2 * BLOCK, 2 * part), BF),
                struct((BLOCK, width), F32),
                struct((BLOCK, width), BF),
                struct((BLOCK, width), F32),
                struct((BLOCK, width), BF),
            ],
            [rows_gu, rows_shard, n2_part, mix_part, slots_gu, slots_down],
            2,
            scratch=[pltpu.VMEM((width, 2 * part), BF), pltpu.VMEM((part, width), BF)],
            flops=4_840_000_000,
        )

    hidden_own, gu_own, mix_keep_own, mix_send_own, back_keep_own, back_send_own = mlp(near_n2, near_mix)
    hidden_far, gu_far, mix_keep_far, mix_send_far, back_keep_far, back_send_far = mlp(far_n2, far_mix)

    back_far = back_keep_far + swap(back_send_far, "kk").astype(F32)
    back_own = back_keep_own + swap(back_send_own, "kk").astype(F32)
    grad_n2 = back_own + swap(back_far.astype(BF), "bb").astype(F32)
    grad_state_norm, grad_gain_two = rms_back(state, gain_two, grad_n2)
    grad_state = own_mix.astype(F32) + grad_state_norm
    low_state = grad_state.astype(BF)
    far_state = swap(low_state, "bb")
    side_state = swap(jnp.stack([low_state, far_state]), "kk")
    all_state = jnp.concatenate([low_state, side_state[0], far_state, side_state[1]], axis=0)

    grad_gu, grad_down = call(
        mlp_weights_kernel,
        [struct((8, 4, 32, 2 * part), BF), struct((part, width), BF)],
        [x_slots, near_n2, far_n2, hidden_own, hidden_far, near_mix, far_mix, gu_own, gu_far],
        1,
        flops=4_840_000_000,
    )
    grad_down = lax.psum_scatter(grad_down, "shard", scatter_dimension=0, tiled=True)
    grad_gu = lax.psum_scatter(grad_gu, "shard", scatter_dimension=0, tiled=False)

    mix_far_sum = mix_keep_far + swap(mix_send_far, "kk").astype(F32)
    mix_own_sum = mix_keep_own + swap(mix_send_own, "kk").astype(F32)
    mixed = state + mix_own_sum + swap(mix_far_sum.astype(BF), "bb").astype(F32)
    mixed_out = rehome(mixed.astype(BF))[None]

    grad_out = dot_tn(att, all_state).astype(BF)
    grad_out = lax.psum_scatter(grad_out, "shard", scatter_dimension=0, tiled=True)
    grad_pre, grad_gain_query, grad_gain_key = call(
        attention_back_kernel,
        [struct((total, 1024), BF), struct((1, HD), F32), struct((1, HD), F32)],
        [
            blocks, all_state, w_out_all, queries, keys, values, pre, cos_table, sin_table, gain_query, gain_key,
        ],
        1,
        scratch=[pltpu.VMEM((2, 4, 2 * BLOCK, HD), BF)],
        flops=5_000_000_000,
    )
    grad_q_slots, grad_kv_slots = call(
        qkv_weights_kernel,
        [struct((32, 32, 512), BF), struct((32, 32, 512), BF)],
        [rows_q, rows_kv, n1, grad_pre],
        2,
        scratch=[pltpu.VMEM((width, 1024), BF)],
        flops=2_150_000_000,
    )
    in_keep, in_send = call(
        input_kernel,
        [struct((2, BLOCK, width), F32), struct((2, BLOCK, width), BF)],
        [grad_pre, w_all],
        0,
        flops=2_150_000_000,
    )
    in_half = in_keep + swap(in_send, "kk").astype(F32)
    grad_n1 = in_half[0] + swap(in_half[1].astype(BF), "bb").astype(F32)
    grad_input_norm, grad_gain_one = rms_back(inputs, gain_one, grad_n1)
    input_grad = rehome(grad_state + grad_input_norm)[None]

    def of_columns(value):
        value = both(value[:2].astype(F32) + swap(value[2:].astype(BF), "aa").astype(F32), "hh")
        value = rounded(value).astype(BF)
        value = jnp.stack([value[0], swap(value[1], "bb")])
        value = jnp.concatenate([value, swap(value, "kk")], axis=0)
        order = [pick(value, slot) for slot in quarter_slots]
        return [piece.astype(F32) for piece in order]

    quarter_slots = []
    for n in range(4):
        own = quarter ^ n
        quarter_slots.append(jnp.where(own == 0, 0, jnp.where(own == 3, 1, jnp.where(own == 1, 2, 3))))

    def of_rows(value):
        value = rounded(both(both(value, "aa"), "hh")).astype(BF)
        return jnp.where(quarter == x_at, value, swap(value, "kk")).astype(F32)

    own_down = of_rows(grad_down)
    own_out = of_rows(grad_out)
    pieces = of_columns(grad_gu)
    own_gu = jnp.concatenate([p[:, :part] for p in pieces] + [p[:, part:] for p in pieces], axis=1)
    shard_q = fold(grad_q_slots, STEPS_Q)
    shard_kv = fold(grad_kv_slots, STEPS_KV)
    pieces = of_columns(jnp.concatenate([shard_q, shard_kv], axis=2))
    own_qkv = jnp.concatenate(
        [p[:, :512] for p in pieces] + [p[:, 512:768] for p in pieces] + [p[:, 768:] for p in pieces], axis=1
    )
    grad_gains = jnp.concatenate([grad_gain_one, grad_gain_two, grad_gain_query[0], grad_gain_key[0]])
    grad_gains = jnp.pad(grad_gains, (0, 768)).reshape(24, 128)
    for dims in ("ab", "ba", "cd", "dc", "ef", "hh", "kk"):
        grad_gains = grad_gains + swap(grad_gains, dims)
    own_gains = pick(grad_gains.reshape(-1)[: 2 * width + 2 * HD].reshape(32, 72), x_at * 8 + shard_at)

    upd_qkv = adamw(w_qkv, own_qkv, first_qkv, second_qkv, RATES[0], DECAYS[0])
    upd_out = adamw(w_out, own_out, first_out, second_out, RATES[1], DECAYS[1])
    upd_gu = adamw(w_gu, own_gu, first_gu, second_gu, RATES[2], DECAYS[2])
    upd_down = adamw(w_down, own_down, first_down, second_down, RATES[3], DECAYS[3])
    upd_gains = adamw(gains, own_gains, first_gains, second_gains, RATES[4], DECAYS[4])
    return (mixed_out, input_grad, *upd_qkv, *upd_out, *upd_gu, *upd_down, *upd_gains)


def solution(mesh):
    rows = P(("seq", "shard"), None)
    flat = P(("seq", "shard"))
    whole = P(("shard", "replica"), "seq", None)
    per_weight = (rows, rows, rows, rows, flat)
    return jax.shard_map(
        on_device,
        mesh=mesh,
        in_specs=(whole, whole) + per_weight * 3,
        out_specs=(whole, whole) + (rows,) * 12 + (flat,) * 3,
        check_vma=False,
    )
```

```python
import math

import jax
import jax.numpy as jnp
import numpy as np
from jax import lax
from jax.experimental import pallas as pl
from jax.experimental.pallas import tpu as pltpu
from jax.sharding import PartitionSpec as P

HEADS = 16
KVH = 8
HD = 128
FF = 3072
STEP = 10
EPS = 1e-06
THETA = 1000000.0
BETA_ONE = 0.9
BETA_TWO = 0.95
ADAM_EPS = 1e-08
RATES = (0.04, 0.2, 0.04, 0.03, 0.4)
DECAYS = (0.1, 0.1, 0.1, 0.1, 0.0)
NEG_FILL = -1e30

AXES = ("seq", "shard", "replica")
DEVICES = 128
BLOCK = 256
BF = jnp.bfloat16
F32 = jnp.float32
VMEM_LIMIT = 56 * 1024 * 1024


def place_of(device):
    replica, shard, x = device % 4, (device // 4) % 8, device // 32
    return x, shard % 4, (replica // 2) * 2 + shard // 4, replica % 2


def device_at(x, y, z, k):
    return (x * 8 + (z % 2) * 4 + y) * 4 + (z // 2) * 2 + k


def flip(dim, x, y, z, k):
    return {
        "a": (x ^ 1, y, z, k),
        "b": (3 - x, y, z, k),
        "c": (x, y ^ 1, z, k),
        "d": (x, 3 - y, z, k),
        "e": (x, y, z ^ 1, k),
        "f": (x, y, 3 - z, k),
        "h": (x, y, z ^ 2, k),
        "k": (x, y, z, k ^ 1),
    }[dim]


def quarter_of(x, k):
    return k if x < 2 else 3 - k


def partners(dims):
    pairs = []
    for device in range(DEVICES):
        place = place_of(device)
        pairs.append((device, device_at(*flip(dims[place[3]], *place))))
    return pairs


def swap(value, dims):
    return lax.ppermute(value, AXES, partners(dims))


def home_pairs():
    pairs = []
    for device in range(DEVICES):
        x, y, z, k = place_of(device)
        moved = {(0, 1): (1, 0), (1, 0): (0, 1), (2, 0): (3, 1), (3, 1): (2, 0)}.get((x, k), (x, k))
        pairs.append((device, device_at(moved[0], y, z, moved[1])))
    return pairs


def rehome(value):
    return lax.ppermute(value, AXES, home_pairs())


def shard_of(place):
    return (place[2] % 2) * 4 + place[1]


def slot_places(device, steps):
    places = [place_of(device)]
    for dims in steps:
        places = places + [flip(dims[p[3]], *p) for p in places]
    return places


def row_table(steps):
    table = np.zeros((DEVICES, 32), np.int32)
    for device in range(DEVICES):
        slots = slot_places(device, ("bb", "aa") + tuple(steps))
        table[device] = [p[0] * 8 + shard_of(p) for p in slots]
    return table


def shard_table(steps):
    table = np.zeros((DEVICES, 8), np.int32)
    for device in range(DEVICES):
        table[device] = [shard_of(p) for p in slot_places(device, steps)]
    return table


STEPS_Q = ("cd", "dc", "ef")
STEPS_ROWS = ("cd", "dc", "ef")
STEPS_MAIN = ("cd", "dc", "ef")
STEPS_REST = ("dc", "ef", "cd")
STEPS_GRAD_OUT = ("ef", "dc", "cd")
STEPS_GRAD_Q = ("cd", "ef", "dc")
STEPS_GRAD_KV = ("dc", "cd", "ef")
def block_table():
    table = np.zeros((DEVICES, 4), np.int32)
    for device in range(DEVICES):
        x, _, _, k = place_of(device)
        own = quarter_of(x, k)
        table[device] = [own, own ^ 1, own ^ 3, own ^ 2]
    return table


def x_table():
    table = np.zeros((DEVICES, 4), np.int32)
    for device in range(DEVICES):
        own = place_of(device)[0]
        table[device] = [(0, 2, 3, 1)[own ^ x] for x in range(4)]
    return table


def home_table():
    table = np.zeros((DEVICES, 1), np.int32)
    for device in range(DEVICES):
        x, _, _, k = place_of(device)
        table[device] = quarter_of(x, k) == x
    return table


TABLES = [
    row_table(STEPS_Q), row_table(STEPS_GRAD_Q), row_table(STEPS_GRAD_KV), row_table(STEPS_MAIN),
    row_table(STEPS_REST), shard_table(STEPS_ROWS), shard_table(STEPS_REST), shard_table(STEPS_GRAD_OUT),
    block_table(), x_table(), home_table(),
]
AT_ALL, AT_Q, AT_KV, AT_MAIN, AT_REST, AT_OUT, AT_DOWN, AT_GRAD_OUT, AT_BLOCK, AT_X, AT_HOME = np.cumsum(
    [0] + [t.shape[1] for t in TABLES[:-1]]
).tolist()
PLACES = np.concatenate(TABLES, axis=1)


def dot(left, right):
    return lax.dot_general(left, right, (((1,), (0,)), ((), ())), preferred_element_type=F32)


def dot_nt(left, right):
    return lax.dot_general(left, right, (((1,), (1,)), ((), ())), preferred_element_type=F32)


def dot_tn(left, right):
    return lax.dot_general(left, right, (((0,), (0,)), ((), ())), preferred_element_type=F32)


def at(index, size):
    return pl.ds(pl.multiple_of(index * size, size), size)


def score_pieces(keys, queries, block):
    pieces = []
    if block > 0:
        rows = slice(0, block * BLOCK)
        pieces.append((rows, dot_nt(keys[rows, :], queries)))
    rows = slice(block * BLOCK, (block + 1) * BLOCK)
    scores = dot_nt(keys[rows, :], queries)
    key = lax.broadcasted_iota(jnp.int32, scores.shape, 0)
    query = lax.broadcasted_iota(jnp.int32, scores.shape, 1) & (BLOCK - 1)
    pieces.append((rows, jnp.where(key <= query, scores, NEG_FILL)))
    return pieces


def total_of(values):
    result = values[0]
    for value in values[1:]:
        result = result + value
    return result


def norm_kernel(own, side, far, last, gain, n1):
    for slot, ref in enumerate((own, side, far, last)):
        value = ref[...].astype(F32)
        scale = lax.rsqrt(jnp.mean(value * value, axis=1, keepdims=True) + EPS)
        n1[slot * BLOCK : (slot + 1) * BLOCK, :] = (value * scale * gain[...]).astype(BF)


def state_kernel(keep, got, far, tokens, gain, state, n2):
    value = tokens[...].astype(F32) + keep[0] + got[...].astype(F32) + far[...].astype(F32)
    state[...] = value
    scale = lax.rsqrt(jnp.mean(value * value, axis=1, keepdims=True) + EPS)
    n2[...] = (value * scale * gain[...]).astype(BF)


def far_kernel(keep, got, out):
    out[...] = (keep[...] + got[...].astype(F32)).astype(BF)


def state_back_kernel(keep, got, far, state, mix, gain, grad, low, grad_gain):
    grad_n2 = keep[...] + got[...].astype(F32) + far[...].astype(F32)
    value = state[...]
    scale = lax.rsqrt(jnp.mean(value * value, axis=1, keepdims=True) + EPS)
    unit = value * scale
    scaled = grad_n2 * gain[...]
    result = mix[...].astype(F32) + scale * (scaled - unit * jnp.mean(scaled * unit, axis=1, keepdims=True))
    grad[...] = result
    low[...] = result.astype(BF)
    grad_gain[...] = jnp.sum(grad_n2 * unit, axis=0, keepdims=True)


def input_back_kernel(keep, got, far, tokens, grad_state, gain, low):
    grad_n1 = keep[0] + got[...].astype(F32) + far[...].astype(F32)
    value = tokens[...].astype(F32)
    scale = lax.rsqrt(jnp.mean(value * value, axis=1, keepdims=True) + EPS)
    unit = value * scale
    scaled = grad_n1 * gain[...]
    result = grad_state[...] + scale * (scaled - unit * jnp.mean(scaled * unit, axis=1, keepdims=True))
    low[...] = result.astype(BF)


def columns(start, size):
    return pl.ds(pl.multiple_of(start, 128), size)


def update_refs(refs, gradient, outs, rate, decay_rate):
    results = adamw(refs[0][...], gradient, refs[1][...], refs[2][...], rate, decay_rate)
    for out, result in zip(outs, results):
        out[...] = result


def update_qkv_kernel(places, message, got, w_q, m_q, s_q, w_o, m_o, s_o, *outs):
    gradient = outs[6]
    for slot, (ref, row) in enumerate(((message, 0), (got, 0), (message, 64), (got, 64))):
        quarter = places[AT_BLOCK + slot]
        gradient[:, columns(quarter * 512, 512)] = ref[row : row + 32, :].astype(F32)
        gradient[:, columns(2048 + quarter * 256, 256)] = ref[row + 32 : row + 64, 0:256].astype(F32)
        gradient[:, columns(3072 + quarter * 256, 256)] = ref[row + 32 : row + 64, 256:512].astype(F32)
    update_refs((w_q, m_q, s_q), gradient[...], outs[0:3], RATES[0], DECAYS[0])
    home = places[AT_HOME] == 1
    for half in range(2):
        here = slice(half * 512, half * 512 + 512)
        rows = slice(128 + half * 64, 192 + half * 64)
        part = jnp.where(home, message[rows, :].astype(F32), got[rows, :].astype(F32))
        refs = (w_o.at[:, here], m_o.at[:, here], s_o.at[:, here])
        update_refs(refs, part, [out.at[:, here] for out in outs[3:6]], RATES[1], DECAYS[1])


def update_mlp_kernel(places, message, got, w_g, m_g, s_g, w_d, m_d, s_d, *outs):
    gradient = outs[6]
    part = FF // 4
    for slot, (ref, side) in enumerate(((message, 0), (got, 0), (message, 1), (got, 1))):
        quarter = places[AT_BLOCK + slot]
        main = ref[side * 32 : side * 32 + 32, :].astype(F32)
        gradient[:, columns(quarter * part, part)] = main[:, :part]
        gradient[:, columns(FF + quarter * part, 1024 - part)] = main[:, part:]
        gradient[:, columns(FF + quarter * part + 1024 - part, 512)] = ref[
            64:96, side * 512 : side * 512 + 512
        ].astype(F32)
    update_refs((w_g, m_g, s_g), gradient[...], outs[0:3], RATES[2], DECAYS[2])
    home = places[AT_HOME] == 1
    total = jnp.where(home, message[96:192, :].astype(F32), got[96:192, :].astype(F32))
    update_refs((w_d, m_d, s_d), total, outs[3:6], RATES[3], DECAYS[3])


def attention_kernel(
    places, n1, w_low, w_high, cos, sin, gain_q, gain_k, w_all, pre, q_out, k_out, v_out, att, log_total
):
    factor = 1.0 / math.sqrt(HD)
    for slot in range(32):
        w_all[at(places[AT_ALL + slot], 32), :] = w_low[slot] if slot < 16 else w_high[slot - 16]
    for slot in range(4):
        block = places[AT_BLOCK + slot]
        here = at(block, BLOCK)
        projected = dot(n1[slot * BLOCK : (slot + 1) * BLOCK, :], w_all[...])
        pre[here, :] = projected[:, :768]
        cos_part = cos[here, :]
        sin_part = sin[here, :]

        def turned(column, gain):
            head = projected[:, column : column + HD]
            normed = head * lax.rsqrt(jnp.mean(head * head, axis=1, keepdims=True) + EPS) * gain[...]
            return normed * cos_part + pltpu.roll(normed, HD // 2, 1) * sin_part

        for head in range(4):
            rotated = (turned(head * HD, gain_q) * factor).astype(BF)
            q_out[head // 2, block, (head % 2) * BLOCK : (head % 2 + 1) * BLOCK, :] = rotated
        for head in range(2):
            k_out[head, here, :] = turned(512 + head * HD, gain_k).astype(BF)
            v_out[head, here, :] = projected[:, 768 + head * HD : 768 + (head + 1) * HD].astype(BF)
    for group in range(2):
        for block in range(4):
            pieces = score_pieces(k_out.at[group], q_out[group, block], block)
            top = jnp.max(pieces[0][1], axis=0, keepdims=True)
            for _, scores in pieces[1:]:
                top = jnp.maximum(top, jnp.max(scores, axis=0, keepdims=True))
            exponents = [(rows_here, jnp.exp(scores - top)) for rows_here, scores in pieces]
            sums = total_of([jnp.sum(e, axis=0, keepdims=True) for _, e in exponents])
            inverse = 1.0 / sums
            attended = total_of(
                [dot_tn(v_out[group, rows_here, :], (e * inverse).astype(BF)) for rows_here, e in exponents]
            )
            attended = attended.T.astype(BF)
            log_total[group * 4 + block : group * 4 + block + 1, :] = top + jnp.log(sums)
            own = places[AT_BLOCK] ^ block
            slot = own ^ (own >> 1)
            for head in range(2):
                column = (group * 2 + head) * HD
                att[at(slot, BLOCK), column : column + HD] = attended[head * BLOCK : (head + 1) * BLOCK]


def attention_back_kernel(
    places, own, side, far, last, w_out, queries, keys, values, pre, log_total, cos, sin, gain_q, gain_k,
    grad_pre, grad_gain_q, grad_gain_k, grad_att, grad_k, grad_v,
):
    factor = 1.0 / math.sqrt(HD)
    for slot, ref in enumerate((own, side, far, last)):
        part = dot_nt(ref[...], w_out[...]).astype(BF)
        for head in range(4):
            grad_att[head // 2, places[AT_BLOCK + slot], (head % 2) * BLOCK : (head % 2 + 1) * BLOCK, :] = part[
                :, head * HD : (head + 1) * HD
            ]

    def back_through(grad, head, cos_part, sin_part, gain):
        turned = grad * cos_part - pltpu.roll(grad, HD // 2, 1) * sin_part
        scale = lax.rsqrt(jnp.mean(head * head, axis=1, keepdims=True) + EPS)
        unit = head * scale
        scaled = turned * gain[...]
        grad_head = scale * (scaled - unit * jnp.mean(scaled * unit, axis=1, keepdims=True))
        return grad_head, jnp.sum(turned * unit, axis=0, keepdims=True)

    total_q = jnp.zeros((1, HD), F32)
    total_k = jnp.zeros((1, HD), F32)
    for group in range(2):
        for block in range(3, -1, -1):
            own = places[AT_BLOCK] ^ block
            there = at(own ^ (own >> 1), BLOCK)
            query = queries[group, block]
            grad_o = grad_att[group, block]
            logs = log_total[group * 4 + block : group * 4 + block + 1, :]
            probs = [(r, jnp.exp(scores - logs)) for r, scores in score_pieces(keys.at[group], query, block)]
            grad_probs = [dot_nt(values[group, r, :], grad_o) for r, _ in probs]
            inner = total_of([jnp.sum(p * g, axis=0, keepdims=True) for (_, p), g in zip(probs, grad_probs)])
            grad_scores = [(r, (p * (g - inner)).astype(BF)) for (r, p), g in zip(probs, grad_probs)]
            grad_q = total_of([dot_tn(keys[group, r, :], d) for r, d in grad_scores]).T * factor
            for (r, p), (_, d) in zip(probs, grad_scores):
                part_k = dot(d, query)
                part_v = dot(p.astype(BF), grad_o)
                if block == 3:
                    grad_k[r, :] = part_k
                    grad_v[r, :] = part_v
                else:
                    grad_k[r, :] += part_k
                    grad_v[r, :] += part_v
            for head in range(2):
                column = (group * 2 + head) * HD
                grad_head, gain_part = back_through(
                    grad_q[head * BLOCK : (head + 1) * BLOCK],
                    pre[block * BLOCK : (block + 1) * BLOCK, column : column + HD],
                    cos[block * BLOCK : (block + 1) * BLOCK, :],
                    sin[block * BLOCK : (block + 1) * BLOCK, :],
                    gain_q,
                )
                total_q = total_q + gain_part
                grad_pre[there, column : column + HD] = grad_head.astype(BF)
        for block in range(4):
            own = places[AT_BLOCK] ^ block
            there = at(own ^ (own >> 1), BLOCK)
            column = 512 + group * HD
            grad_head, gain_part = back_through(
                grad_k[block * BLOCK : (block + 1) * BLOCK, :],
                pre[block * BLOCK : (block + 1) * BLOCK, column : column + HD],
                cos[block * BLOCK : (block + 1) * BLOCK, :],
                sin[block * BLOCK : (block + 1) * BLOCK, :],
                gain_k,
            )
            total_k = total_k + gain_part
            grad_pre[there, column : column + HD] = grad_head.astype(BF)
            grad_pre[there, 768 + group * HD : 768 + (group + 1) * HD] = grad_v[
                block * BLOCK : (block + 1) * BLOCK, :
            ].astype(BF)
    grad_gain_q[...] = total_q
    grad_gain_k[...] = total_k


def out_kernel(places, att, low_slots, high_slots, w_out, keep, send):
    for slot in range(8):
        slots = low_slots if slot < 4 else high_slots
        w_out[at(places[AT_OUT + slot], 64), :] = slots[slot % 4]
    for slot in range(4):
        part = dot(att[slot * BLOCK : (slot + 1) * BLOCK, :], w_out[...])
        target = keep if slot % 2 == 0 else send
        target[slot // 2] = part.astype(target.dtype)


def out_weights_kernel(places, att, own, side, far, last, low, high, scratch):
    total = jnp.zeros(scratch.shape, F32)
    for slot, ref in enumerate((own, side, far, last)):
        total = total + dot_tn(att[slot * BLOCK : (slot + 1) * BLOCK, :], ref[...])
    scratch[...] = total.astype(BF)
    for slot in range(8):
        target = low if slot < 4 else high
        for half in range(2):
            there = (slot % 4) * 128 + half * 64
            target[there : there + 64, :] = scratch[at(places[AT_GRAD_OUT + slot], 64), half * 512 : half * 512 + 512]


def mlp_kernel(
    places, n2_first, n2_second, mix_first, mix_second, main_low, main_high, rest_low, rest_high,
    hidden, grad_gu, mix_keep, grad_keep, send, w_gu, w_down,
):
    for slot in range(32):
        main = main_low if slot < 16 else main_high
        w_gu[at(places[AT_MAIN + slot], 32), 0:1024] = main[slot % 16]
        rest = rest_low if slot < 16 else rest_high
        x = slot % 4
        w_gu[at(places[AT_REST + slot], 32), 1024:1536] = rest[
            (slot % 16) // 4, (x // 2) * 32 : (x // 2) * 32 + 32, (x % 2) * 512 : (x % 2) * 512 + 512
        ]
    for slot in range(8):
        rest = rest_low if slot < 4 else rest_high
        w_down[at(places[AT_DOWN + slot], 96), :] = rest[slot % 4, 64:160, :]
    half = FF // 4
    for slot, (n2, grad_mix) in enumerate(((n2_first, mix_first), (n2_second, mix_second))):
        here = slice(slot * BLOCK, (slot + 1) * BLOCK)
        gate_up = dot(n2[...], w_gu[...])
        grad_hidden = dot_nt(grad_mix[...], w_down[...])
        gate = gate_up[:, :half]
        up = gate_up[:, half:]
        sigmoid = 1.0 / (1.0 + jnp.exp(-gate))
        silu = gate * sigmoid
        low_hidden = (silu * up).astype(BF)
        hidden[here, :] = low_hidden
        grad_gate = grad_hidden * up * (sigmoid * (1.0 + gate * (1.0 - sigmoid)))
        low_grad = jnp.concatenate([grad_gate, grad_hidden * silu], axis=1).astype(BF)
        grad_gu[here, :] = low_grad
        back = dot_nt(low_grad, w_gu[...])
        mixed = dot(low_hidden, w_down[...])
        if slot == 0:
            grad_keep[...] = back
            mix_keep[...] = mixed
        else:
            send[0] = back.astype(BF)
            send[1] = mixed.astype(BF)


def mlp_weights_kernel(
    places, n2_0, n2_1, n2_2, n2_3, mix_0, mix_1, mix_2, mix_3, hidden_own, hidden_far, gu_own, gu_far, out, total
):
    n2s, mixes = (n2_0, n2_1, n2_2, n2_3), (mix_0, mix_1, mix_2, mix_3)

    def tokens(near, far, slot):
        ref = near if slot < 2 else far
        return ref, slice((slot % 2) * BLOCK, (slot % 2 + 1) * BLOCK)

    for x in range(4):
        here = slice(x * BLOCK, (x + 1) * BLOCK)
        part = jnp.zeros((BLOCK, 2 * FF // 4), F32)
        for slot in range(4):
            ref, rows = tokens(gu_own, gu_far, slot)
            part = part + dot_tn(n2s[slot][:, here], ref[rows, :])
        total[places[AT_X + x]] = part.astype(BF).reshape(8, 32, 2 * FF // 4)
    for slot in range(4):
        start = (slot // 2) * 96
        side = slot % 2
        out[:, start + side * 32 : start + side * 32 + 32, :] = total[slot, :, :, 0:1024]
        out[:, start + 64 : start + 96, side * 512 : side * 512 + 512] = total[slot, :, :, 1024:1536]
    for third in range(3):
        here = slice(third * BLOCK, (third + 1) * BLOCK)
        part = jnp.zeros((BLOCK, out.shape[2]), F32)
        for slot in range(4):
            ref, rows = tokens(hidden_own, hidden_far, slot)
            part = part + dot_tn(ref[rows, here], mixes[slot][...])
        total_down = part.astype(BF)
        for piece in range(8):
            row = third * BLOCK + piece * 32
            out[row // 96, 192 + row % 96 : 192 + row % 96 + 32, :] = total_down[piece * 32 : piece * 32 + 32]


def qkv_weights_kernel(places, n1, grad_pre, q_low, q_high, kv_low, kv_high, total):
    for x in range(4):
        here = slice(x * BLOCK, (x + 1) * BLOCK)
        total[here, :] = dot_tn(n1[:, here], grad_pre[...]).astype(BF)
    for slot in range(32):
        there = slice((slot % 16) * 32, (slot % 16) * 32 + 32)
        (q_low if slot < 16 else q_high)[there, :] = total[at(places[AT_Q + slot], 32), 0:512]
        (kv_low if slot < 16 else kv_high)[there, :] = total[at(places[AT_KV + slot], 32), 512:1024]


def input_kernel(grad_pre, w_all, own, side, far, last, keep, send, grad_gain):
    total = jnp.zeros(grad_gain.shape, F32)
    for slot, ref in enumerate((own, side, far, last)):
        part = dot_nt(grad_pre[slot * BLOCK : (slot + 1) * BLOCK, :], w_all[...])
        value = ref[...].astype(F32)
        scale = lax.rsqrt(jnp.mean(value * value, axis=1, keepdims=True) + EPS)
        total = total + jnp.sum(part * (value * scale), axis=0, keepdims=True)
        target = keep if slot % 2 == 0 else send
        target[slot // 2] = part.astype(target.dtype)
    grad_gain[...] = total


def call(kernel, outs, args, scalars, scratch=(), flops=0):
    space = [pl.BlockSpec(memory_space=pltpu.SMEM)] * scalars
    space += [pl.BlockSpec(memory_space=pltpu.VMEM)] * (len(args) - scalars)
    size = sum(math.prod(a.shape) * a.dtype.itemsize for a in list(args) + list(outs))
    return pl.pallas_call(
        kernel,
        out_shape=outs,
        in_specs=space,
        out_specs=[pl.BlockSpec(memory_space=pltpu.VMEM)] * len(outs),
        scratch_shapes=list(scratch),
        compiler_params=pltpu.CompilerParams(vmem_limit_bytes=VMEM_LIMIT),
        cost_estimate=pl.CostEstimate(flops=flops, bytes_accessed=size, transcendentals=0),
    )(*args)


def struct(shape, dtype):
    return jax.ShapeDtypeStruct(shape, dtype)


def rms_scale(value, gain):
    return value * lax.rsqrt(jnp.mean(value * value, axis=-1, keepdims=True) + EPS) * gain


def rms_back(value, gain, grad):
    scale = lax.rsqrt(jnp.mean(value * value, axis=-1, keepdims=True) + EPS)
    scaled = grad * gain
    inner = jnp.mean(scaled * value, axis=-1, keepdims=True)
    grad_value = scale * scaled - value * (scale * scale * scale) * inner
    return grad_value, jnp.sum(grad * value * scale, axis=0)


def adamw(weight, gradient, first_moment, second_moment, rate, decay_rate):
    first_moment = BETA_ONE * first_moment + (1.0 - BETA_ONE) * gradient
    second_moment = BETA_TWO * second_moment + (1.0 - BETA_TWO) * gradient * gradient
    first_hat = first_moment / (1.0 - BETA_ONE**STEP)
    second_hat = second_moment / (1.0 - BETA_TWO**STEP)
    weight = weight - rate * (first_hat / (jnp.sqrt(second_hat) + ADAM_EPS) + decay_rate * weight)
    return (weight, first_moment, second_moment)


def halves(rider):
    high = rounded(rider)
    return jnp.concatenate([high, rounded(rider - high)], axis=0)


def joined(pair):
    half = pair.shape[0] // 2
    return pair[:half].astype(F32) + pair[half:].astype(F32)


def fold_step(low, high, dims, rider=None):
    rows = high.shape[0]
    if rider is None:
        got, rider_sum = swap(high.astype(BF), dims), None
    else:
        pair = halves(rider)
        got = swap(jnp.concatenate([high.astype(BF), pair.astype(BF)], axis=0), dims)
        rider_sum = joined(pair) + joined(got[rows:])
    value = low.astype(F32) + got[:rows].astype(F32)
    return value[: rows // 2], value[rows // 2 :], rider_sum


def rounded(value):
    return lax.reduce_precision(value.astype(F32), 8, 7)


def after(value, *others):
    return lax.optimization_barrier((value,) + others)[0]


def pick(stack, index):
    return lax.dynamic_index_in_dim(stack, index, 0, keepdims=False)


def on_device(
    tokens,
    cotangent,
    w_qkv,
    w_out,
    w_gu,
    w_down,
    gains,
    first_qkv,
    first_out,
    first_gu,
    first_down,
    first_gains,
    second_qkv,
    second_out,
    second_gu,
    second_down,
    second_gains,
):
    width = tokens.shape[-1]
    x_at = lax.axis_index("seq")
    shard_at = lax.axis_index("shard")
    replica_at = lax.axis_index("replica")
    device = (x_at * 8 + shard_at) * 4 + replica_at
    core = replica_at % 2
    quarter = jnp.where(x_at < 2, core, 3 - core)
    places = pick(jnp.asarray(PLACES), device)

    low_qkv = w_qkv.astype(BF)
    stack_qkv = jnp.stack(
        [
            jnp.concatenate(
                [
                    low_qkv[:, 512 * n : 512 * (n + 1)],
                    low_qkv[:, 2048 + 256 * n : 2304 + 256 * n],
                    low_qkv[:, 3072 + 256 * n : 3328 + 256 * n],
                ],
                axis=1,
            )
            for n in range(4)
        ]
    )
    spot = (jnp.arange(32) == x_at * 8 + shard_at)[:, None]
    gain_vals = jnp.where(spot, rounded(gains)[None, :], 0.0)
    gains_one = jnp.pad(gain_vals.reshape(-1), (0, 768)).reshape(24, 128)

    qkv_one = pick(stack_qkv, quarter)[None]
    qkv_two = jnp.concatenate([qkv_one, swap(pick(stack_qkv, 3 - quarter)[None], "bb")], axis=0)
    gains_two = gains_one + swap(gains_one, "bb")
    qkv_four = jnp.concatenate([qkv_two, swap(qkv_two, "aa")], axis=0)
    gains_four = gains_two + swap(after(gains_two, qkv_two), "aa")
    qkv_eight = jnp.concatenate([qkv_four, swap(after(qkv_four, gains_two), STEPS_Q[0])], axis=0)
    gains_eight = gains_four + swap(after(gains_four, qkv_four), STEPS_Q[2])
    qkv_low = jnp.concatenate([qkv_eight, swap(after(qkv_eight, gains_four), STEPS_Q[1])], axis=0)
    gains_low = gains_eight + swap(after(gains_eight, qkv_eight), STEPS_Q[0])
    qkv_high = swap(after(qkv_low, gains_eight), STEPS_Q[2])
    gain_vals = gains_low + swap(after(gains_low, qkv_low), STEPS_Q[1])
    gain_vals = gain_vals.reshape(1, -1)
    gain_one = gain_vals[:, :width]
    gain_two = gain_vals[:, width : 2 * width]
    gain_query = gain_vals[:, 2 * width : 2 * width + HD]
    gain_key = gain_vals[:, 2 * width + HD : 2 * width + 2 * HD]

    low_gu = after(w_gu, qkv_two).astype(BF)
    part = FF // 4
    stack_gu = jnp.stack(
        [
            jnp.concatenate(
                [low_gu[:, part * n : part * (n + 1)], low_gu[:, FF + part * n : FF + part * (n + 1)]], axis=1
            )
            for n in range(4)
        ]
    )
    gu_one = pick(stack_gu, quarter)[None]
    gu_two = jnp.concatenate([gu_one, swap(pick(stack_gu, 3 - quarter)[None], "bb")], axis=0)
    gu_four = jnp.concatenate([gu_two, swap(after(gu_two, qkv_eight, gains_four), "aa")], axis=0)

    own_tokens = rehome(after(tokens[0], qkv_four))
    side_tokens = swap(after(own_tokens, qkv_eight), "kk")
    far_tokens = swap(after(own_tokens, gu_two), "bb")
    last_tokens = swap(after(far_tokens, qkv_low), "kk")

    others = jnp.concatenate([w_out.astype(BF), w_down.astype(BF), cotangent[0]], axis=0)
    others = rehome(after(others, qkv_eight, gains_eight, own_tokens))
    own_mix = others[160:]
    far_mix = swap(after(own_mix, last_tokens, gain_vals), "bb")
    side_mix = swap(after(own_mix, gain_vals), "kk")
    out_one = others[None, :64]
    out_two = jnp.concatenate([out_one, swap(after(out_one, qkv_low), STEPS_ROWS[0])], axis=0)
    out_low = jnp.concatenate([out_two, swap(after(out_two, qkv_low, gains_low), STEPS_ROWS[1])], axis=0)
    out_high = swap(after(out_low, qkv_high, gain_vals), STEPS_ROWS[2])
    down_one = others[64:160]

    main_one = gu_four[:, :, :1024]
    last = gu_four[:, :, 1024:]
    rest_one = jnp.concatenate(
        [
            jnp.concatenate([last[0], last[1]], axis=1),
            jnp.concatenate([last[2], last[3]], axis=1),
            down_one,
        ],
        axis=0,
    )[None]
    main_two = jnp.concatenate([main_one, swap(after(main_one, qkv_low, out_two), STEPS_MAIN[0])], axis=0)
    rest_two = jnp.concatenate([rest_one, swap(after(rest_one, qkv_low, out_two), STEPS_REST[0])], axis=0)

    main_low = jnp.concatenate([main_two, swap(after(main_two, qkv_high, gain_vals), STEPS_MAIN[1])], axis=0)
    rest_low = jnp.concatenate([rest_two, swap(after(rest_two, qkv_high, gain_vals), STEPS_REST[1])], axis=0)

    positions = jnp.arange(4 * BLOCK, dtype=F32)
    frequency = THETA ** (-jnp.arange(HD // 2, dtype=F32) / (HD // 2))
    angles = positions[:, None] * frequency[None, :]
    cos_half, sin_half = jnp.cos(angles), jnp.sin(angles)
    cos_table = jnp.concatenate([cos_half, cos_half], axis=1)
    sin_table = jnp.concatenate([-sin_half, sin_half], axis=1)

    total = 4 * BLOCK
    (n1,) = call(norm_kernel, [struct((total, width), BF)], [own_tokens, side_tokens, far_tokens, last_tokens, gain_one], 0)
    w_all, pre, queries, keys, values, att, log_total = call(
        attention_kernel,
        [
            struct((width, 1024), BF),
            struct((total, 768), F32),
            struct((2, 4, 2 * BLOCK, HD), BF),
            struct((2, total, HD), BF),
            struct((2, total, HD), BF),
            struct((total, 512), BF),
            struct((8, 2 * BLOCK), F32),
        ],
        [
            places, n1, qkv_low.reshape(16, 32, 1024), qkv_high.reshape(16, 32, 1024),
            cos_table, sin_table, gain_query, gain_key,
        ],
        1,
        flops=3_600_000_000,
    )
    last_mix = swap(after(far_mix, att), "kk")
    main_high = swap(after(main_low, att), STEPS_MAIN[2])
    rest_high = swap(after(rest_low, att), STEPS_REST[2])
    w_out_all, out_keep, out_send = call(
        out_kernel,
        [struct((512, width), BF), struct((2, BLOCK, width), F32), struct((2, BLOCK, width), BF)],
        [places, after(att, main_low, rest_low, far_mix), out_low, out_high],
        1,
        flops=1_080_000_000,
    )
    got_out = swap(out_send, "kk")
    out_far = call(far_kernel, [struct((BLOCK, width), BF)], [out_keep[1], got_out[1]], 0)[0]
    state, n2 = call(
        state_kernel,
        [struct((BLOCK, width), F32), struct((BLOCK, width), BF)],
        [out_keep, got_out[0], swap(out_far, "bb"), own_tokens, gain_two],
        0,
    )
    far_n2 = swap(n2, "bb")
    side_n2 = swap(n2, "kk")


    def mlp(*parts):
        return call(
            mlp_kernel,
            [
                struct((2 * BLOCK, part), BF),
                struct((2 * BLOCK, 2 * part), BF),
                struct((BLOCK, width), F32),
                struct((BLOCK, width), F32),
                struct((2, BLOCK, width), BF),
            ],
            [
                places, *parts, main_low.reshape(16, 32, 1024), main_high.reshape(16, 32, 1024), rest_low, rest_high,
            ],
            1,
            scratch=[pltpu.VMEM((width, 2 * part), BF), pltpu.VMEM((part, width), BF)],
            flops=4_840_000_000,
        )

    hidden_own, gu_own, mix_keep_own, back_keep_own, send_own = mlp(n2, side_n2, own_mix, side_mix)
    far_n2 = after(far_n2, send_own)
    last_n2 = swap(far_n2, "kk")
    hidden_far, gu_far, mix_keep_far, back_keep_far, send_far = mlp(
        far_n2, last_n2, far_mix, last_mix
    )
    got_far = swap(send_far, "kk")
    got_own = swap(after(send_own, got_far), "kk")
    back_far = call(far_kernel, [struct((BLOCK, width), BF)], [back_keep_far, got_far[0]], 0)[0]
    back_arrived = swap(back_far, "bb")
    grad_mlp_parts = call(
        mlp_weights_kernel,
        [struct((8, 288, width), BF)],
        [
            places, after(n2, back_far), side_n2, far_n2, last_n2, own_mix, side_mix, far_mix, last_mix,
            hidden_own, hidden_far, gu_own, gu_far,
        ],
        1,
        scratch=[pltpu.VMEM((4, 8, 32, 2 * part), BF)],
        flops=4_840_000_000,
    )[0]
    grad_mlp = lax.psum_scatter(grad_mlp_parts, "shard", scatter_dimension=0, tiled=False)
    grad_mlp_done = grad_mlp

    grad_state, low_state, grad_gain_two = call(
        state_back_kernel,
        [struct((BLOCK, width), F32), struct((BLOCK, width), BF), struct((1, width), F32)],
        [back_keep_own, got_own[0], after(back_arrived, grad_mlp_parts), state, own_mix, gain_two],
        0,
    )
    far_state = swap(low_state, "bb")
    side_state = swap(low_state, "kk")
    last_state = swap(far_state, "kk")

    out_grads = call(
        out_weights_kernel,
        [struct((512, 512), BF)] * 2,
        [places, att, low_state, side_state, far_state, last_state],
        1,
        scratch=[pltpu.VMEM((512, width), BF)],
        flops=1_080_000_000,
    )
    grad_low, grad_high = out_grads
    got_grad = swap(grad_high, STEPS_GRAD_OUT[2])
    mix_far = (mix_keep_far + got_far[1].astype(F32)).astype(BF)
    mix_arrived = swap(after(mix_far, last_state), "bb")
    grad_pre, grad_gain_query, grad_gain_key = call(
        attention_back_kernel,
        [struct((total, 1024), BF), struct((1, HD), F32), struct((1, HD), F32)],
        [
            places, after(low_state, grad_low), side_state, far_state, last_state, w_out_all, queries, keys, values, pre,
            log_total, cos_table, sin_table, gain_query, gain_key,
        ],
        1,
        scratch=[
            pltpu.VMEM((2, 4, 2 * BLOCK, HD), BF), pltpu.VMEM((total, HD), F32), pltpu.VMEM((total, HD), F32)
        ],
        flops=8_000_000_000,
    )
    q_low, q_high, kv_low, kv_high = call(
        qkv_weights_kernel,
        [struct((512, 512), BF)] * 4,
        [places, after(n1, mix_arrived), grad_pre],
        1,
        scratch=[pltpu.VMEM((width, 1024), BF)],
        flops=2_150_000_000,
    )
    grad_total = grad_low.astype(F32) + after(got_grad, q_high).astype(F32)
    grad_low, grad_high = grad_total[:256], grad_total[256:]
    got_grad = swap(grad_high.astype(BF), STEPS_GRAD_OUT[1])
    in_keep, in_send, grad_gain_one = call(
        input_kernel,
        [struct((2, BLOCK, width), F32), struct((2, BLOCK, width), BF), struct((1, width), F32)],
        [after(grad_pre, q_high), w_all, own_tokens, side_tokens, far_tokens, last_tokens],
        0,
        flops=2_150_000_000,
    )

    rider = jnp.concatenate([grad_gain_one, grad_gain_two.reshape(1, -1), grad_gain_query, grad_gain_key], axis=1)
    rider = jnp.pad(rider, ((0, 0), (0, 1792))).reshape(8, 512)
    pair = halves(rider)
    rider = joined(pair) + joined(swap(pair.astype(BF), STEPS_GRAD_Q[2]))

    got_in = swap(in_send, "kk")
    in_far = call(far_kernel, [struct((BLOCK, width), BF)], [in_keep[1], got_in[1]], 0)[0]
    in_arrived = swap(in_far, "bb")

    q_low, q_high, _ = fold_step(q_low, q_high, STEPS_GRAD_Q[2])
    kv_low, kv_high, _ = fold_step(kv_low, kv_high, STEPS_GRAD_KV[2])
    grad_total = grad_low + after(got_grad, q_high, kv_high).astype(F32)
    grad_low, grad_high = grad_total[:128], grad_total[128:]
    got_grad = swap(grad_high.astype(BF), STEPS_GRAD_OUT[0])
    mixed = state + (mix_keep_own + got_own[1].astype(F32)) + after(mix_arrived, q_high).astype(F32)
    mixed_out = rehome(mixed.astype(BF))[None]

    grad_mlp = after(grad_mlp, q_high, kv_high).astype(F32)
    got = swap(grad_mlp[96:].astype(BF), "aa").astype(F32)
    grad_mlp = jnp.concatenate([grad_mlp[:96] + got[:96], rounded(grad_mlp[192:]) + got[96:]], axis=0)
    grad_mlp = rounded(grad_mlp)
    grad_mlp = rounded(grad_mlp + swap(grad_mlp.astype(BF), "hh").astype(F32)).astype(BF)
    got = swap(grad_mlp[32:96], "bb")
    message = jnp.concatenate(
        [
            grad_mlp[0:32],
            got[0:32],
            jnp.concatenate([grad_mlp[64:96, 0:512], got[32:64, 512:1024]], axis=1),
            grad_mlp[96:],
        ],
        axis=0,
    )
    got = swap(message, "kk")
    upd_mlp = call(
        update_mlp_kernel,
        [struct(w_gu.shape, F32)] * 3 + [struct(w_down.shape, F32)] * 3,
        [places, message, got, w_gu, first_gu, second_gu, w_down, first_down, second_down],
        1,
        scratch=[pltpu.VMEM(w_gu.shape, F32)],
    )

    q_low, q_high, rider = fold_step(q_low, after(q_high, grad_mlp_done), STEPS_GRAD_Q[1], rider)
    kv_low, kv_high, _ = fold_step(kv_low, kv_high, STEPS_GRAD_KV[1])
    q_low, q_high, rider = fold_step(q_low, q_high, STEPS_GRAD_Q[0], rider)
    kv_low, kv_high, _ = fold_step(kv_low, kv_high, STEPS_GRAD_KV[0])
    low_grad = call(
        input_back_kernel,
        [struct((BLOCK, width), BF)],
        [in_keep, got_in[0], in_arrived, own_tokens, grad_state, gain_one],
        0,
    )[0]
    grad_out = rounded(grad_low + got_grad.astype(F32))
    pair = halves(rider)
    message = jnp.concatenate([q_high, kv_high, grad_out, pair], axis=0)
    got = swap(after(message.astype(BF), low_grad), "aa").astype(F32)
    input_grad = rehome(after(low_grad, got))[None].astype(F32)
    summed = rounded(jnp.concatenate([q_low, kv_low, grad_out], axis=0) + got[:256])
    pair = halves(joined(pair) + joined(got[256:]))
    message = jnp.concatenate([summed, pair], axis=0)
    got = swap(message.astype(BF), "hh").astype(F32)
    summed = rounded(summed + got[:256])
    pair = halves(joined(pair) + joined(got[256:]))
    message = jnp.concatenate([summed[32:64], summed[96:128], pair], axis=0)
    got = swap(message.astype(BF), "bb").astype(F32)
    pair = halves(joined(pair) + joined(got[64:]))
    message = jnp.concatenate([summed[:32], summed[64:96], got[:64], summed[128:], pair], axis=0).astype(BF)
    got = swap(message, "kk")
    grad_gains = (joined(message[256:]) + joined(got[256:])).reshape(-1)[: 2 * width + 2 * HD]
    own_gains = pick(grad_gains.reshape(32, 72), x_at * 8 + shard_at)
    upd_qkv = call(
        update_qkv_kernel,
        [struct(w_qkv.shape, F32)] * 3 + [struct(w_out.shape, F32)] * 3,
        [places, message, got, w_qkv, first_qkv, second_qkv, w_out, first_out, second_out],
        1,
        scratch=[pltpu.VMEM(w_qkv.shape, F32)],
    )
    upd_gains = adamw(gains, own_gains, first_gains, second_gains, RATES[4], DECAYS[4])
    return (mixed_out, input_grad, *upd_qkv, *upd_mlp, *upd_gains)


def solution(mesh):
    rows = P(("seq", "shard"), None)
    flat = P(("seq", "shard"))
    whole = P(("shard", "replica"), "seq", None)
    per_weight = (rows, rows, rows, rows, flat)
    return jax.shard_map(
        on_device,
        mesh=mesh,
        in_specs=(whole, whole) + per_weight * 3,
        out_specs=(whole, whole) + (rows,) * 12 + (flat,) * 3,
        check_vma=False,
    )
```

```python
import functools
import math

import jax
import jax.numpy as jnp
import numpy as np
from jax import lax
from jax.experimental import pallas as pl
from jax.experimental.pallas import tpu as pltpu
from jax.sharding import PartitionSpec as P

HEADS = 16
KVH = 8
HD = 128
FF = 3072
STEP = 10
EPS = 1e-06
THETA = 1000000.0
BETA_ONE = 0.9
BETA_TWO = 0.95
ADAM_EPS = 1e-08
RATES = (0.04, 0.2, 0.04, 0.03, 0.4)
DECAYS = (0.1, 0.1, 0.1, 0.1, 0.0)
NEG_FILL = -1e30

AXES = ("seq", "shard", "replica")
DEVICES = 128
BLOCK = 256
BF = jnp.bfloat16
F32 = jnp.float32
VMEM_LIMIT = 52 * 1024 * 1024
SMALL_LIMIT = 12 * 1024 * 1024


def place_of(device):
    replica, shard, x = device % 4, (device // 4) % 8, device // 32
    return x, shard % 4, (replica // 2) * 2 + shard // 4, replica % 2


def device_at(x, y, z, k):
    return (x * 8 + (z % 2) * 4 + y) * 4 + (z // 2) * 2 + k


def flip(dim, x, y, z, k):
    return {
        "a": (x ^ 1, y, z, k),
        "b": (3 - x, y, z, k),
        "c": (x, y ^ 1, z, k),
        "d": (x, 3 - y, z, k),
        "e": (x, y, z ^ 1, k),
        "f": (x, y, 3 - z, k),
        "h": (x, y, z ^ 2, k),
        "k": (x, y, z, k ^ 1),
    }[dim]


def quarter_of(x, k):
    return k if x < 2 else 3 - k


def partners(dims):
    pairs = []
    for device in range(DEVICES):
        place = place_of(device)
        pairs.append((device, device_at(*flip(dims[place[3]], *place))))
    return pairs


def swap(value, dims):
    return lax.ppermute(value, AXES, partners(dims))


def home_pairs():
    pairs = []
    for device in range(DEVICES):
        x, y, z, k = place_of(device)
        moved = {(0, 1): (1, 0), (1, 0): (0, 1), (2, 0): (3, 1), (3, 1): (2, 0)}.get((x, k), (x, k))
        pairs.append((device, device_at(moved[0], y, z, moved[1])))
    return pairs


def rehome(value):
    return lax.ppermute(value, AXES, home_pairs())


def shard_of(place):
    return (place[2] % 2) * 4 + place[1]


def slot_places(device, steps):
    places = [place_of(device)]
    for dims in steps:
        places = places + [flip(dims[p[3]], *p) for p in places]
    return places


def row_table(steps):
    table = np.zeros((DEVICES, 32), np.int32)
    for device in range(DEVICES):
        slots = slot_places(device, ("bb", "aa") + tuple(steps))
        table[device] = [p[0] * 8 + shard_of(p) for p in slots]
    return table


def shard_table(steps):
    table = np.zeros((DEVICES, 8), np.int32)
    for device in range(DEVICES):
        table[device] = [shard_of(p) for p in slot_places(device, steps)]
    return table


STEPS_Q = ("cd", "dc", "ef")
STEPS_ROWS = ("cd", "dc", "ef")
STEPS_MLP = ("dc", "cd", "ef")
STEPS_GRAD_A = ("dc", "ef", "cd")
STEPS_GRAD_B = ("cd", "dc", "ef")
STEPS_GRAD_OUT = ("ef", "dc", "cd")
STEPS_GRAD_Q = ("cd", "ef", "dc")
STEPS_GRAD_KV = ("dc", "cd", "ef")
def block_table():
    table = np.zeros((DEVICES, 4), np.int32)
    for device in range(DEVICES):
        x, _, _, k = place_of(device)
        own = quarter_of(x, k)
        table[device] = [own, own ^ 1, own ^ 3, own ^ 2]
    return table


def x_table():
    table = np.zeros((DEVICES, 4), np.int32)
    for device in range(DEVICES):
        own = place_of(device)[0]
        table[device] = [(0, 2, 3, 1)[own ^ x] for x in range(4)]
    return table


def home_table():
    table = np.zeros((DEVICES, 1), np.int32)
    for device in range(DEVICES):
        x, _, _, k = place_of(device)
        table[device] = quarter_of(x, k) == x
    return table


TABLES = [
    row_table(STEPS_Q), row_table(STEPS_GRAD_Q), row_table(STEPS_GRAD_KV), row_table(STEPS_MLP),
    shard_table(STEPS_ROWS), shard_table(STEPS_MLP), shard_table(STEPS_GRAD_OUT),
    block_table(), x_table(), home_table(), shard_table(STEPS_GRAD_A), shard_table(STEPS_GRAD_B),
]
AT_ALL, AT_Q, AT_KV, AT_MAIN, AT_OUT, AT_DOWN, AT_GRAD_OUT, AT_BLOCK, AT_X, AT_HOME, AT_A, AT_B = np.cumsum(
    [0] + [t.shape[1] for t in TABLES[:-1]]
).tolist()
PLACES = np.concatenate(TABLES, axis=1)


def dot(left, right):
    return lax.dot_general(left, right, (((1,), (0,)), ((), ())), preferred_element_type=F32)


def dot_nt(left, right):
    return lax.dot_general(left, right, (((1,), (1,)), ((), ())), preferred_element_type=F32)


def dot_tn(left, right):
    return lax.dot_general(left, right, (((0,), (0,)), ((), ())), preferred_element_type=F32)


def at(index, size):
    return pl.ds(pl.multiple_of(index * size, size), size)


def score_pieces(keys, queries, block):
    pieces = []
    if block > 0:
        rows = slice(0, block * BLOCK)
        pieces.append((rows, dot_nt(keys[rows, :], queries)))
    rows = slice(block * BLOCK, (block + 1) * BLOCK)
    scores = dot_nt(keys[rows, :], queries)
    key = lax.broadcasted_iota(jnp.int32, scores.shape, 0)
    query = lax.broadcasted_iota(jnp.int32, scores.shape, 1) & (BLOCK - 1)
    pieces.append((rows, jnp.where(key <= query, scores, NEG_FILL)))
    return pieces


def total_of(values):
    result = values[0]
    for value in values[1:]:
        result = result + value
    return result


def norm_kernel(own, side, far, last, gain, n1):
    for slot, ref in enumerate((own, side, far, last)):
        value = ref[...].astype(F32)
        scale = lax.rsqrt(jnp.mean(value * value, axis=1, keepdims=True) + EPS)
        n1[slot * BLOCK : (slot + 1) * BLOCK, :] = (value * scale * gain[...]).astype(BF)


def halves(rider):
    high = rider.astype(BF).astype(F32)
    return jnp.concatenate([high, rider - high], axis=0).astype(BF)


def joined(message):
    pair = message[message.shape[0] - 16 :, :].astype(F32)
    return pair[:8] + pair[8:]


def fold_kernel(q_low, q_sent, q_got, kv_low, kv_got, q_keep, q_send, kv_keep, kv_send):
    rows = kv_got.shape[0]
    half = rows // 2
    value = q_low[...].astype(F32) + q_got[:rows, :].astype(F32)
    q_keep[...] = value[:half]
    q_send[:half, :] = value[half:].astype(BF)
    q_send[half:, :] = halves(joined(q_sent) + joined(q_got))
    value = kv_low[...].astype(F32) + kv_got[...].astype(F32)
    kv_keep[...] = value[:half]
    kv_send[...] = value[half:].astype(BF)


def fold_last_kernel(q_low, q_sent, q_got, kv_low, kv_got, out_low, out_got, keep, send):
    value = q_low[...] + q_got[:128, :].astype(F32)
    keep[0:64, :] = value[:64]
    send[0:64, :] = value[64:].astype(BF)
    value = kv_low[...] + kv_got[...].astype(F32)
    keep[64:128, :] = value[:64]
    send[64:128, :] = value[64:].astype(BF)
    value = (out_low[...] + out_got[...].astype(F32)).astype(BF)
    keep[128:256, :] = value.astype(F32)
    send[128:256, :] = value
    send[256:272, :] = halves(joined(q_sent) + joined(q_got))


def sum_kernel(keep, sent, got, send):
    send[0:256, :] = (keep[0:256, :].astype(F32) + got[0:256, :].astype(F32)).astype(BF)
    send[256:272, :] = halves(joined(sent) + joined(got))


def side_kernel(sent, got, whole, send):
    value = (sent[0:256, :].astype(F32) + got[0:256, :].astype(F32)).astype(BF)
    pair = halves(joined(sent) + joined(got))
    whole[0:256, :] = value
    whole[256:272, :] = pair
    send[0:32, :] = value[32:64]
    send[32:64, :] = value[96:128]
    send[64:80, :] = pair


def gather_kernel(whole, sent, got, message):
    message[0:32, :] = whole[0:32, :]
    message[32:64, :] = whole[64:96, :]
    message[64:128, :] = got[0:64, :]
    message[128:256, :] = whole[128:256, :]
    message[256:272, :] = halves(joined(sent) + joined(got))


def fold_pair_kernel(a_low, a_got, b_low, b_got, a_keep, a_send, b_keep, b_send):
    for low, got, keep, send in ((a_low, a_got, a_keep, a_send), (b_low, b_got, b_keep, b_send)):
        half = low.shape[0] // 2
        for slot in range(2 * half):
            value = (low[slot].astype(F32) + got[slot].astype(F32)).astype(BF)
            if slot < half:
                keep[slot] = value
            else:
                send[slot - half] = value


def fold_pair_last_kernel(a_low, a_got, b_low, b_got, keep, send):
    value = (a_low[0].astype(F32) + a_got[0].astype(F32)).astype(BF)
    keep[...] = value[0:96]
    send[0:48, :] = value[96:144]
    send[48:192, :] = (b_low[0].astype(F32) + b_got[0].astype(F32)).astype(BF)


def mlp_sum_kernel(keep, send, got, out):
    out[0:96, :] = (keep[...].astype(F32) + got[0:96, :].astype(F32)).astype(BF)
    out[96:192, :] = (send[96:192, :].astype(F32) + got[96:192, :].astype(F32)).astype(BF)


def mlp_side_kernel(low, got, whole, send):
    value = (low[...].astype(F32) + got[...].astype(F32)).astype(BF)
    whole[...] = value
    send[...] = value[32:96]


def mlp_gather_kernel(whole, got, message):
    message[0:32, :] = whole[0:32, :]
    message[32:64, :] = got[0:32, :]
    message[64:96, 0:512] = whole[64:96, 0:512]
    message[64:96, 512:1024] = got[32:64, 512:1024]
    message[96:192, :] = whole[96:192, :]


def state_kernel(keep, got, far, tokens, gain, state, n2):
    value = tokens[...].astype(F32) + keep[...] + got[0].astype(F32) + far[...].astype(F32)
    state[...] = value
    scale = lax.rsqrt(jnp.mean(value * value, axis=1, keepdims=True) + EPS)
    n2[...] = (value * scale * gain[...]).astype(BF)


def far_kernel(part, keep, got, out):
    out[...] = (keep[...] + got[part].astype(F32)).astype(BF)


def state_back_kernel(keep, got, far, state, mix, gain, grad, low, grad_gain):
    grad_n2 = keep[...] + got[0].astype(F32) + far[...].astype(F32)
    value = state[...]
    scale = lax.rsqrt(jnp.mean(value * value, axis=1, keepdims=True) + EPS)
    unit = value * scale
    scaled = grad_n2 * gain[...]
    result = mix[...].astype(F32) + scale * (scaled - unit * jnp.mean(scaled * unit, axis=1, keepdims=True))
    grad[...] = result
    low[...] = result.astype(BF)
    grad_gain[...] = jnp.sum(grad_n2 * unit, axis=0, keepdims=True)


def input_back_kernel(keep, got, far, tokens, grad_state, gain, low):
    grad_n1 = keep[...] + got[0].astype(F32) + far[...].astype(F32)
    value = tokens[...].astype(F32)
    scale = lax.rsqrt(jnp.mean(value * value, axis=1, keepdims=True) + EPS)
    unit = value * scale
    scaled = grad_n1 * gain[...]
    result = grad_state[...] + scale * (scaled - unit * jnp.mean(scaled * unit, axis=1, keepdims=True))
    low[...] = result.astype(BF)


def columns(start, size):
    return pl.ds(pl.multiple_of(start, 128), size)


def update_refs(refs, gradient, outs, rate, decay_rate):
    results = adamw(refs[0][...], gradient, refs[1][...], refs[2][...], rate, decay_rate)
    for out, result in zip(outs, results):
        out[...] = result


def update_qkv_kernel(places, message, got, w_q, m_q, s_q, w_o, m_o, s_o, *outs):
    gradient = outs[6]
    for slot, (ref, row) in enumerate(((message, 0), (got, 0), (message, 64), (got, 64))):
        quarter = places[AT_BLOCK + slot]
        gradient[:, columns(quarter * 512, 512)] = ref[row : row + 32, :].astype(F32)
        gradient[:, columns(2048 + quarter * 256, 256)] = ref[row + 32 : row + 64, 0:256].astype(F32)
        gradient[:, columns(3072 + quarter * 256, 256)] = ref[row + 32 : row + 64, 256:512].astype(F32)
    update_refs((w_q, m_q, s_q), gradient[...], outs[0:3], RATES[0], DECAYS[0])
    home = places[AT_HOME] == 1
    for half in range(2):
        here = slice(half * 512, half * 512 + 512)
        rows = slice(128 + half * 64, 192 + half * 64)
        part = jnp.where(home, message[rows, :].astype(F32), got[rows, :].astype(F32))
        refs = (w_o.at[:, here], m_o.at[:, here], s_o.at[:, here])
        update_refs(refs, part, [out.at[:, here] for out in outs[3:6]], RATES[1], DECAYS[1])


def update_mlp_kernel(places, message, got, w_g, m_g, s_g, w_d, m_d, s_d, *outs):
    gradient = outs[6]
    part = FF // 4
    for slot, (ref, side) in enumerate(((message, 0), (got, 0), (message, 1), (got, 1))):
        quarter = places[AT_BLOCK + slot]
        main = ref[side * 32 : side * 32 + 32, :].astype(F32)
        gradient[:, columns(quarter * part, part)] = main[:, :part]
        gradient[:, columns(FF + quarter * part, 1024 - part)] = main[:, part:]
        gradient[:, columns(FF + quarter * part + 1024 - part, 512)] = ref[
            64:96, side * 512 : side * 512 + 512
        ].astype(F32)
    update_refs((w_g, m_g, s_g), gradient[...], outs[0:3], RATES[2], DECAYS[2])
    home = places[AT_HOME] == 1
    total = jnp.where(home, message[96:192, :].astype(F32), got[96:192, :].astype(F32))
    update_refs((w_d, m_d, s_d), total, outs[3:6], RATES[3], DECAYS[3])


def attention_kernel(
    places, n1, w_low, w_high, cos, sin, gain_q, gain_k, w_all, pre, q_out, k_out, v_out, att, log_total
):
    factor = 1.0 / math.sqrt(HD)
    for slot in range(32):
        w_all[at(places[AT_ALL + slot], 32), :] = w_low[slot] if slot < 16 else w_high[slot - 16]
    for slot in range(4):
        block = places[AT_BLOCK + slot]
        here = at(block, BLOCK)
        projected = dot(n1[slot * BLOCK : (slot + 1) * BLOCK, :], w_all[...])
        pre[here, :] = projected[:, :768]
        cos_part = cos[here, :]
        sin_part = sin[here, :]

        def turned(column, gain):
            head = projected[:, column : column + HD]
            normed = head * lax.rsqrt(jnp.mean(head * head, axis=1, keepdims=True) + EPS) * gain[...]
            return normed * cos_part + pltpu.roll(normed, HD // 2, 1) * sin_part

        for head in range(4):
            rotated = (turned(head * HD, gain_q) * factor).astype(BF)
            q_out[head // 2, block, (head % 2) * BLOCK : (head % 2 + 1) * BLOCK, :] = rotated
        for head in range(2):
            k_out[head, here, :] = turned(512 + head * HD, gain_k).astype(BF)
            v_out[head, here, :] = projected[:, 768 + head * HD : 768 + (head + 1) * HD].astype(BF)
    for group in range(2):
        for block in range(4):
            pieces = score_pieces(k_out.at[group], q_out[group, block], block)
            top = jnp.max(pieces[0][1], axis=0, keepdims=True)
            for _, scores in pieces[1:]:
                top = jnp.maximum(top, jnp.max(scores, axis=0, keepdims=True))
            exponents = [(rows_here, jnp.exp(scores - top)) for rows_here, scores in pieces]
            sums = total_of([jnp.sum(e, axis=0, keepdims=True) for _, e in exponents])
            inverse = 1.0 / sums
            attended = total_of(
                [dot_tn(v_out[group, rows_here, :], (e * inverse).astype(BF)) for rows_here, e in exponents]
            )
            attended = attended.T.astype(BF)
            log_total[group * 4 + block : group * 4 + block + 1, :] = top + jnp.log(sums)
            own = places[AT_BLOCK] ^ block
            slot = own ^ (own >> 1)
            for head in range(2):
                column = (group * 2 + head) * HD
                att[at(slot, BLOCK), column : column + HD] = attended[head * BLOCK : (head + 1) * BLOCK]


def attention_back_kernel(
    places, own, side, far, last, w_out, queries, keys, values, pre, log_total, cos, sin, gain_q, gain_k,
    grad_pre, grad_gain_q, grad_gain_k, grad_att, grad_k, grad_v,
):
    factor = 1.0 / math.sqrt(HD)
    for slot, ref in enumerate((own, side, far, last)):
        part = dot_nt(ref[...], w_out[...]).astype(BF)
        for head in range(4):
            grad_att[head // 2, places[AT_BLOCK + slot], (head % 2) * BLOCK : (head % 2 + 1) * BLOCK, :] = part[
                :, head * HD : (head + 1) * HD
            ]

    def back_through(grad, head, cos_part, sin_part, gain):
        turned = grad * cos_part - pltpu.roll(grad, HD // 2, 1) * sin_part
        scale = lax.rsqrt(jnp.mean(head * head, axis=1, keepdims=True) + EPS)
        unit = head * scale
        scaled = turned * gain[...]
        grad_head = scale * (scaled - unit * jnp.mean(scaled * unit, axis=1, keepdims=True))
        return grad_head, jnp.sum(turned * unit, axis=0, keepdims=True)

    total_q = jnp.zeros((1, HD), F32)
    total_k = jnp.zeros((1, HD), F32)
    for group in range(2):
        for block in range(3, -1, -1):
            own = places[AT_BLOCK] ^ block
            there = at(own ^ (own >> 1), BLOCK)
            query = queries[group, block]
            grad_o = grad_att[group, block]
            logs = log_total[group * 4 + block : group * 4 + block + 1, :]
            probs = [(r, jnp.exp(scores - logs)) for r, scores in score_pieces(keys.at[group], query, block)]
            grad_probs = [dot_nt(values[group, r, :], grad_o) for r, _ in probs]
            inner = total_of([jnp.sum(p * g, axis=0, keepdims=True) for (_, p), g in zip(probs, grad_probs)])
            grad_scores = [(r, (p * (g - inner)).astype(BF)) for (r, p), g in zip(probs, grad_probs)]
            grad_q = total_of([dot_tn(keys[group, r, :], d) for r, d in grad_scores]).T * factor
            for (r, p), (_, d) in zip(probs, grad_scores):
                part_k = dot(d, query)
                part_v = dot(p.astype(BF), grad_o)
                if block == 3:
                    grad_k[r, :] = part_k
                    grad_v[r, :] = part_v
                else:
                    grad_k[r, :] += part_k
                    grad_v[r, :] += part_v
            for head in range(2):
                column = (group * 2 + head) * HD
                grad_head, gain_part = back_through(
                    grad_q[head * BLOCK : (head + 1) * BLOCK],
                    pre[block * BLOCK : (block + 1) * BLOCK, column : column + HD],
                    cos[block * BLOCK : (block + 1) * BLOCK, :],
                    sin[block * BLOCK : (block + 1) * BLOCK, :],
                    gain_q,
                )
                total_q = total_q + gain_part
                grad_pre[there, column : column + HD] = grad_head.astype(BF)
        for block in range(4):
            own = places[AT_BLOCK] ^ block
            there = at(own ^ (own >> 1), BLOCK)
            column = 512 + group * HD
            grad_head, gain_part = back_through(
                grad_k[block * BLOCK : (block + 1) * BLOCK, :],
                pre[block * BLOCK : (block + 1) * BLOCK, column : column + HD],
                cos[block * BLOCK : (block + 1) * BLOCK, :],
                sin[block * BLOCK : (block + 1) * BLOCK, :],
                gain_k,
            )
            total_k = total_k + gain_part
            grad_pre[there, column : column + HD] = grad_head.astype(BF)
            grad_pre[there, 768 + group * HD : 768 + (group + 1) * HD] = grad_v[
                block * BLOCK : (block + 1) * BLOCK, :
            ].astype(BF)
    grad_gain_q[...] = total_q
    grad_gain_k[...] = total_k


def out_kernel(places, att, low_slots, high_slots, w_out, keep_own, keep_far, send):
    for slot in range(8):
        slots = low_slots if slot < 4 else high_slots
        w_out[at(places[AT_OUT + slot], 64), :] = slots[slot % 4]
    for slot in range(4):
        part = dot(att[slot * BLOCK : (slot + 1) * BLOCK, :], w_out[...])
        if slot % 2 == 1:
            send[slot // 2] = part.astype(BF)
        else:
            (keep_own if slot == 0 else keep_far)[...] = part


def out_weights_kernel(places, att, own, side, far, last, low, high, scratch):
    total = jnp.zeros(scratch.shape, F32)
    for slot, ref in enumerate((own, side, far, last)):
        total = total + dot_tn(att[slot * BLOCK : (slot + 1) * BLOCK, :], ref[...])
    scratch[...] = total.astype(BF)
    for slot in range(8):
        target = low if slot < 4 else high
        for half in range(2):
            there = (slot % 4) * 128 + half * 64
            target[there : there + 64, :] = scratch[at(places[AT_GRAD_OUT + slot], 64), half * 512 : half * 512 + 512]


def mlp_kernel(
    places, n2_first, n2_second, mix_first, mix_second, low_slots, high_slots,
    hidden, grad_gu, mix_keep, grad_keep, send, w_gu, w_down,
):
    for slot in range(8):
        ref = low_slots if slot < 4 else high_slots
        for x in range(4):
            start, side = (x // 2) * 96, x % 2
            here = at(places[AT_MAIN + slot * 4 + x], 32)
            w_gu[here, 0:1024] = ref[slot % 4, start + side * 32 : start + side * 32 + 32, :]
            w_gu[here, 1024:1536] = ref[slot % 4, start + 64 : start + 96, side * 512 : side * 512 + 512]
        w_down[at(places[AT_DOWN + slot], 96), :] = ref[slot % 4, 192:288, :]
    half = FF // 4
    for slot, (n2, grad_mix) in enumerate(((n2_first, mix_first), (n2_second, mix_second))):
        here = slice(slot * BLOCK, (slot + 1) * BLOCK)
        gate_up = dot(n2[...], w_gu[...])
        grad_hidden = dot_nt(grad_mix[...], w_down[...])
        gate = gate_up[:, :half]
        up = gate_up[:, half:]
        sigmoid = 1.0 / (1.0 + jnp.exp(-gate))
        silu = gate * sigmoid
        low_hidden = (silu * up).astype(BF)
        hidden[here, :] = low_hidden
        grad_gate = grad_hidden * up * (sigmoid * (1.0 + gate * (1.0 - sigmoid)))
        low_grad = jnp.concatenate([grad_gate, grad_hidden * silu], axis=1).astype(BF)
        grad_gu[here, :] = low_grad
        back = dot_nt(low_grad, w_gu[...])
        mixed = dot(low_hidden, w_down[...])
        if slot == 0:
            grad_keep[...] = back
            mix_keep[...] = mixed
        else:
            send[0] = back.astype(BF)
            send[1] = mixed.astype(BF)


def mlp_weights_kernel(
    places, n2_0, n2_1, n2_2, n2_3, mix_0, mix_1, mix_2, mix_3, hidden_own, hidden_far, gu_own, gu_far,
    a_low, a_high, b_low, b_high, out, total,
):
    n2s, mixes = (n2_0, n2_1, n2_2, n2_3), (mix_0, mix_1, mix_2, mix_3)

    def tokens(near, far, slot):
        ref = near if slot < 2 else far
        return ref, slice((slot % 2) * BLOCK, (slot % 2 + 1) * BLOCK)

    for x in range(4):
        here = slice(x * BLOCK, (x + 1) * BLOCK)
        part = jnp.zeros((BLOCK, 2 * FF // 4), F32)
        for slot in range(4):
            ref, rows = tokens(gu_own, gu_far, slot)
            part = part + dot_tn(n2s[slot][:, here], ref[rows, :])
        total[places[AT_X + x]] = part.astype(BF).reshape(8, 32, 2 * FF // 4)
    for slot in range(4):
        start = (slot // 2) * 96
        side = slot % 2
        out[:, start + side * 32 : start + side * 32 + 32, :] = total[slot, :, :, 0:1024]
        out[:, start + 64 : start + 96, side * 512 : side * 512 + 512] = total[slot, :, :, 1024:1536]
    for third in range(3):
        here = slice(third * BLOCK, (third + 1) * BLOCK)
        part = jnp.zeros((BLOCK, out.shape[2]), F32)
        for slot in range(4):
            ref, rows = tokens(hidden_own, hidden_far, slot)
            part = part + dot_tn(ref[rows, here], mixes[slot][...])
        total_down = part.astype(BF)
        for piece in range(8):
            row = third * BLOCK + piece * 32
            out[row // 96, 192 + row % 96 : 192 + row % 96 + 32, :] = total_down[piece * 32 : piece * 32 + 32]
    for slot in range(8):
        (a_low if slot < 4 else a_high)[slot % 4] = out[places[AT_A + slot], 0:144, :]
        (b_low if slot < 4 else b_high)[slot % 4] = out[places[AT_B + slot], 144:288, :]


def qkv_back_kernel(
    places, n1, grad_pre, w_all, own, side, far, last, gain_two, gain_q, gain_k,
    q_low, q_high, kv_low, kv_high, keep_own, keep_far, send, total,
):
    for x in range(4):
        here = slice(x * BLOCK, (x + 1) * BLOCK)
        total[here, :] = dot_tn(n1[:, here], grad_pre[...]).astype(BF)
    for slot in range(32):
        there = slice((slot % 16) * 32, (slot % 16) * 32 + 32)
        (q_low if slot < 16 else q_high)[there, :] = total[at(places[AT_Q + slot], 32), 0:512]
        (kv_low if slot < 16 else kv_high)[there, :] = total[at(places[AT_KV + slot], 32), 512:1024]
    gain_sum = jnp.zeros((1, n1.shape[1]), F32)
    for slot, ref in enumerate((own, side, far, last)):
        part = dot_nt(grad_pre[slot * BLOCK : (slot + 1) * BLOCK, :], w_all[...])
        value = ref[...].astype(F32)
        scale = lax.rsqrt(jnp.mean(value * value, axis=1, keepdims=True) + EPS)
        gain_sum = gain_sum + jnp.sum(part * (value * scale), axis=0, keepdims=True)
        if slot % 2 == 1:
            send[slot // 2] = part.astype(BF)
        else:
            (keep_own if slot == 0 else keep_far)[...] = part
    rows = [gain_sum[:, :512], gain_sum[:, 512:], gain_two[:, :512], gain_two[:, 512:]]
    rows += [jnp.concatenate([gain_q[...], gain_k[...], jnp.zeros((1, 256), F32)], axis=1), jnp.zeros((3, 512), F32)]
    q_high[512:528, :] = halves(jnp.concatenate(rows, axis=0))


def far_sum(part, keep, got):
    kernel = functools.partial(far_kernel, part)
    return call(kernel, [struct(keep.shape, BF)], [keep, got], 0, small=True)[0]


def call(kernel, outs, args, scalars, scratch=(), flops=0, small=False):
    space = [pl.BlockSpec(memory_space=pltpu.SMEM)] * scalars
    space += [pl.BlockSpec(memory_space=pltpu.VMEM)] * (len(args) - scalars)
    size = sum(math.prod(a.shape) * a.dtype.itemsize for a in list(args) + list(outs))
    return pl.pallas_call(
        kernel,
        out_shape=outs,
        in_specs=space,
        out_specs=[pl.BlockSpec(memory_space=pltpu.VMEM)] * len(outs),
        scratch_shapes=list(scratch),
        compiler_params=pltpu.CompilerParams(vmem_limit_bytes=SMALL_LIMIT if small else VMEM_LIMIT),
        cost_estimate=pl.CostEstimate(flops=flops, bytes_accessed=size, transcendentals=0),
    )(*args)


def struct(shape, dtype):
    return jax.ShapeDtypeStruct(shape, dtype)


def rms_scale(value, gain):
    return value * lax.rsqrt(jnp.mean(value * value, axis=-1, keepdims=True) + EPS) * gain


def rms_back(value, gain, grad):
    scale = lax.rsqrt(jnp.mean(value * value, axis=-1, keepdims=True) + EPS)
    scaled = grad * gain
    inner = jnp.mean(scaled * value, axis=-1, keepdims=True)
    grad_value = scale * scaled - value * (scale * scale * scale) * inner
    return grad_value, jnp.sum(grad * value * scale, axis=0)


def adamw(weight, gradient, first_moment, second_moment, rate, decay_rate):
    first_moment = BETA_ONE * first_moment + (1.0 - BETA_ONE) * gradient
    second_moment = BETA_TWO * second_moment + (1.0 - BETA_TWO) * gradient * gradient
    first_hat = first_moment / (1.0 - BETA_ONE**STEP)
    second_hat = second_moment / (1.0 - BETA_TWO**STEP)
    weight = weight - rate * (first_hat / (jnp.sqrt(second_hat) + ADAM_EPS) + decay_rate * weight)
    return (weight, first_moment, second_moment)


def rounded(value):
    return lax.reduce_precision(value.astype(F32), 8, 7)


def after(value, *others):
    return lax.optimization_barrier((value,) + others)[0]


def pick(stack, index):
    return lax.dynamic_index_in_dim(stack, index, 0, keepdims=False)


def on_device(
    tokens,
    cotangent,
    w_qkv,
    w_out,
    w_gu,
    w_down,
    gains,
    first_qkv,
    first_out,
    first_gu,
    first_down,
    first_gains,
    second_qkv,
    second_out,
    second_gu,
    second_down,
    second_gains,
):
    width = tokens.shape[-1]
    x_at = lax.axis_index("seq")
    shard_at = lax.axis_index("shard")
    replica_at = lax.axis_index("replica")
    device = (x_at * 8 + shard_at) * 4 + replica_at
    core = replica_at % 2
    quarter = jnp.where(x_at < 2, core, 3 - core)
    places = pick(jnp.asarray(PLACES), device)

    low_qkv = w_qkv.astype(BF)
    stack_qkv = jnp.stack(
        [
            jnp.concatenate(
                [
                    low_qkv[:, 512 * n : 512 * (n + 1)],
                    low_qkv[:, 2048 + 256 * n : 2304 + 256 * n],
                    low_qkv[:, 3072 + 256 * n : 3328 + 256 * n],
                ],
                axis=1,
            )
            for n in range(4)
        ]
    )
    spot = (jnp.arange(32) == x_at * 8 + shard_at)[:, None]
    gain_vals = jnp.where(spot, rounded(gains)[None, :], 0.0)
    gains_one = jnp.pad(gain_vals.reshape(-1), (0, 768)).reshape(24, 128)

    qkv_one = pick(stack_qkv, quarter)[None]
    qkv_two = jnp.concatenate([qkv_one, swap(pick(stack_qkv, 3 - quarter)[None], "bb")], axis=0)
    gains_two = gains_one + swap(gains_one, "bb")
    qkv_four = jnp.concatenate([qkv_two, swap(qkv_two, "aa")], axis=0)
    gains_four = gains_two + swap(after(gains_two, qkv_two), "aa")
    qkv_eight = jnp.concatenate([qkv_four, swap(after(qkv_four, gains_four), STEPS_Q[0])], axis=0)
    gains_eight = gains_four + swap(after(gains_four, qkv_four), STEPS_Q[2])
    low_gu = after(w_gu, qkv_four).astype(BF)
    part = FF // 4
    stack_gu = jnp.stack(
        [
            jnp.concatenate(
                [low_gu[:, part * n : part * (n + 1)], low_gu[:, FF + part * n : FF + part * (n + 1)]], axis=1
            )
            for n in range(4)
        ]
    )
    gu_one = pick(stack_gu, quarter)[None]
    gu_two = jnp.concatenate([gu_one, swap(pick(stack_gu, 3 - quarter)[None], "bb")], axis=0)

    first = rehome(jnp.concatenate([tokens[0], w_out.astype(BF), w_down.astype(BF)], axis=0))
    own_tokens = first[:BLOCK]
    out_one = first[None, BLOCK : BLOCK + 64]
    down_one = first[BLOCK + 64 :]
    far_tokens = swap(after(own_tokens, gu_two), "bb")
    side_tokens = swap(after(own_tokens, qkv_eight), "kk")

    qkv_low = jnp.concatenate([qkv_eight, swap(after(qkv_eight, gains_eight, gu_two), STEPS_Q[1])], axis=0)
    gains_low = gains_eight + swap(after(gains_eight, qkv_eight), STEPS_Q[0])
    gu_four = jnp.concatenate([gu_two, swap(after(gu_two, qkv_eight), "aa")], axis=0)
    qkv_high = swap(after(qkv_low, gains_low, gu_four), STEPS_Q[2])
    gain_vals = gains_low + swap(after(gains_low, qkv_low), STEPS_Q[1])
    last_tokens = swap(after(far_tokens, gain_vals), "kk")
    own_mix = rehome(after(cotangent[0], gu_four))
    far_mix = swap(after(own_mix, far_tokens), "bb")
    side_mix = swap(after(own_mix, gain_vals), "kk")
    out_two = jnp.concatenate([out_one, swap(after(out_one, qkv_low), STEPS_ROWS[0])], axis=0)
    out_low = jnp.concatenate([out_two, swap(out_two, STEPS_ROWS[1])], axis=0)
    out_high = swap(after(out_low, qkv_high), STEPS_ROWS[2])
    gain_vals = gain_vals.reshape(1, -1)
    gain_one = gain_vals[:, :width]
    gain_two = gain_vals[:, width : 2 * width]
    gain_query = gain_vals[:, 2 * width : 2 * width + HD]
    gain_key = gain_vals[:, 2 * width + HD : 2 * width + 2 * HD]

    last = gu_four[:, :, 1024:]
    mlp_one = jnp.concatenate(
        [
            gu_four[0, :, :1024], gu_four[1, :, :1024], jnp.concatenate([last[0], last[1]], axis=1),
            gu_four[2, :, :1024], gu_four[3, :, :1024], jnp.concatenate([last[2], last[3]], axis=1),
            down_one,
        ],
        axis=0,
    )[None]
    mlp_two = jnp.concatenate([mlp_one, swap(after(mlp_one, out_two), STEPS_MLP[0])], axis=0)

    positions = jnp.arange(4 * BLOCK, dtype=F32)
    frequency = THETA ** (-jnp.arange(HD // 2, dtype=F32) / (HD // 2))
    angles = positions[:, None] * frequency[None, :]
    cos_half, sin_half = jnp.cos(angles), jnp.sin(angles)
    cos_table = jnp.concatenate([cos_half, cos_half], axis=1)
    sin_table = jnp.concatenate([-sin_half, sin_half], axis=1)

    total = 4 * BLOCK
    (n1,) = call(norm_kernel, [struct((total, width), BF)], [own_tokens, side_tokens, far_tokens, last_tokens, gain_one], 0, small=True)
    w_all, pre, queries, keys, values, att, log_total = call(
        attention_kernel,
        [
            struct((width, 1024), BF),
            struct((total, 768), F32),
            struct((2, 4, 2 * BLOCK, HD), BF),
            struct((2, total, HD), BF),
            struct((2, total, HD), BF),
            struct((total, 512), BF),
            struct((8, 2 * BLOCK), F32),
        ],
        [
            places, n1, qkv_low.reshape(16, 32, 1024), qkv_high.reshape(16, 32, 1024),
            cos_table, sin_table, gain_query, gain_key,
        ],
        1,
        flops=3_600_000_000,
    )
    last_mix = swap(after(far_mix, att), "kk")
    mlp_low = jnp.concatenate([mlp_two, swap(after(mlp_two, out_low, gain_vals), STEPS_MLP[1])], axis=0)
    mlp_high = swap(after(mlp_low, att), STEPS_MLP[2])
    w_out_all, out_own, out_keep, out_send = call(
        out_kernel,
        [struct((512, width), BF)] + [struct((BLOCK, width), F32)] * 2 + [struct((2, BLOCK, width), BF)],
        [places, after(att, mlp_low, far_mix), out_low, out_high],
        1,
        flops=1_080_000_000,
    )
    got_out = swap(out_send, "kk")
    out_far = far_sum(1, out_keep, got_out)
    state, n2 = call(
        state_kernel,
        [struct((BLOCK, width), F32), struct((BLOCK, width), BF)],
        [out_own, got_out, swap(out_far, "bb"), own_tokens, gain_two],
        0,
        small=True,
    )
    far_n2 = swap(n2, "bb")
    side_n2 = swap(n2, "kk")


    def mlp(*parts):
        return call(
            mlp_kernel,
            [
                struct((2 * BLOCK, part), BF),
                struct((2 * BLOCK, 2 * part), BF),
                struct((BLOCK, width), F32),
                struct((BLOCK, width), F32),
                struct((2, BLOCK, width), BF),
            ],
            [places, *parts, mlp_low, mlp_high],
            1,
            scratch=[pltpu.VMEM((width, 2 * part), BF), pltpu.VMEM((part, width), BF)],
            flops=4_840_000_000,
        )

    hidden_own, gu_own, mix_keep_own, back_keep_own, send_own = mlp(n2, side_n2, own_mix, side_mix)
    far_n2 = after(far_n2, send_own)
    last_n2 = swap(far_n2, "kk")
    hidden_far, gu_far, mix_keep_far, back_keep_far, send_far = mlp(
        far_n2, last_n2, far_mix, last_mix
    )
    got_far = swap(send_far, "kk")
    got_own = swap(after(send_own, got_far), "kk")
    back_far = far_sum(0, back_keep_far, got_far)
    back_arrived = swap(back_far, "bb")
    grad_mlp_parts = call(
        mlp_weights_kernel,
        [struct((4, 144, width), BF)] * 4,
        [
            places, after(n2, back_far), side_n2, far_n2, last_n2, own_mix, side_mix, far_mix, last_mix,
            hidden_own, hidden_far, gu_own, gu_far,
        ],
        1,
        scratch=[pltpu.VMEM((8, 288, width), BF), pltpu.VMEM((4, 8, 32, 2 * part), BF)],
        flops=4_840_000_000,
    )
    grad_state, low_state, grad_gain_two = call(
        state_back_kernel,
        [struct((BLOCK, width), F32), struct((BLOCK, width), BF), struct((1, width), F32)],
        [back_keep_own, got_own, after(back_arrived, grad_mlp_parts[1]), state, own_mix, gain_two],
        0,
        small=True,
    )
    far_state = swap(low_state, "bb")
    side_state = swap(low_state, "kk")
    last_state = swap(far_state, "kk")

    def fold_mlp(a_low, a_high, b_low, b_high, index, tie):
        slots = a_low.shape[0] // 2
        outs = [struct((slots, 144, width), BF)] * 4
        args = [
            a_low, after(swap(after(a_high, tie), STEPS_GRAD_A[index]), b_high),
            b_low, swap(after(b_high, tie), STEPS_GRAD_B[index]),
        ]
        if slots == 0:
            kernel, outs = fold_pair_last_kernel, [struct((96, width), BF), struct((192, width), BF)]
        else:
            kernel = fold_pair_kernel
        return call(kernel, outs, args, 0, small=True)

    mlp_grads = fold_mlp(*grad_mlp_parts, 2, low_state)

    out_grads = call(
        out_weights_kernel,
        [struct((512, 512), BF)] * 2,
        [places, att, low_state, side_state, far_state, last_state],
        1,
        scratch=[pltpu.VMEM((512, width), BF)],
        flops=1_080_000_000,
    )
    grad_low, grad_high = out_grads
    got_grad = swap(grad_high, STEPS_GRAD_OUT[2])
    mix_far = (mix_keep_far + got_far[1].astype(F32)).astype(BF)
    mix_arrived = swap(after(mix_far, last_state), "bb")
    grad_pre, grad_gain_query, grad_gain_key = call(
        attention_back_kernel,
        [struct((total, 1024), BF), struct((1, HD), F32), struct((1, HD), F32)],
        [
            places, after(low_state, grad_low, mlp_grads[0]), side_state, far_state, last_state, w_out_all, queries, keys, values, pre,
            log_total, cos_table, sin_table, gain_query, gain_key,
        ],
        1,
        scratch=[
            pltpu.VMEM((2, 4, 2 * BLOCK, HD), BF), pltpu.VMEM((total, HD), F32), pltpu.VMEM((total, HD), F32)
        ],
        flops=8_000_000_000,
    )
    grad_total = grad_low.astype(F32) + after(got_grad, grad_pre).astype(F32)
    grad_low, grad_high = grad_total[:256], grad_total[256:].astype(BF)
    got_grad = swap(grad_high, STEPS_GRAD_OUT[1])
    mlp_grads = fold_mlp(*mlp_grads, 1, mlp_grads[1])
    q_low, q_high, kv_low, kv_high, in_own, in_keep, in_send = call(
        qkv_back_kernel,
        [struct((512, 512), BF), struct((528, 512), BF), struct((512, 512), BF), struct((512, 512), BF)]
        + [struct((BLOCK, width), F32)] * 2
        + [struct((2, BLOCK, width), BF)],
        [
            places, after(n1, mix_arrived, grad_high, mlp_grads[0]), grad_pre, w_all, own_tokens, side_tokens, far_tokens, last_tokens,
            grad_gain_two, grad_gain_query, grad_gain_key,
        ],
        1,
        scratch=[pltpu.VMEM((width, 1024), BF)],
        flops=4_300_000_000,
    )
    def step(kernel, outs, *args):
        return call(kernel, [struct(*out) for out in outs], args, 0, small=True)

    def fold(rows, q, kv, index, *ties):
        q_got = swap(after(q[1], *ties) if ties else q[1], STEPS_GRAD_Q[index])
        kv_got = swap(kv[1], STEPS_GRAD_KV[index])
        half = rows // 2
        outs = [((half, 512), F32), ((half + 16, 512), BF), ((half, 512), F32), ((half, 512), BF)]
        result = step(fold_kernel, outs, q[0], q[1], q_got, kv[0], kv_got)
        return result[0:2], result[2:4]

    mlp_keep, mlp_send = fold_mlp(*mlp_grads, 0, mlp_grads[1])
    in_send = after(in_send, mlp_send, got_grad)
    kv_high = after(kv_high, mlp_send, got_grad)
    got_in = swap(in_send, "kk")
    in_far = far_sum(1, in_keep, got_in)
    in_arrived = swap(in_far, "bb")

    q, kv = fold(512, (q_low, q_high), (kv_low, kv_high), 2, got_grad, mlp_send)
    grad_total = grad_low + got_grad.astype(F32)
    grad_low, grad_high = grad_total[:128], grad_total[128:]
    got_grad = swap(grad_high.astype(BF), STEPS_GRAD_OUT[0])
    mixed = state + (mix_keep_own + got_own[1].astype(F32)) + after(mix_arrived, q[1]).astype(F32)

    mlp_got = swap(mlp_send, "aa")
    (mlp_rows,) = step(mlp_sum_kernel, [((192, width), BF)], mlp_keep, mlp_send, mlp_got)

    q, kv = fold(256, q, kv, 1, in_arrived, got_grad)
    q_got = swap(after(q[1], mlp_got), STEPS_GRAD_Q[0])
    kv_got = swap(kv[1], STEPS_GRAD_KV[0])
    keep, send = step(
        fold_last_kernel,
        [((256, 512), F32), ((272, 512), BF)],
        q[0], q[1], q_got, kv[0], kv_got, grad_low, got_grad,
    )
    mlp_got = swap(mlp_rows, "hh")
    mlp_whole, mlp_send = step(mlp_side_kernel, [((192, width), BF), ((64, width), BF)], mlp_rows, mlp_got)

    got = swap(send, "aa")
    (send_next,) = step(sum_kernel, [((272, 512), BF)], keep, send, got)
    (low_grad,) = step(
        input_back_kernel,
        [((BLOCK, width), BF)],
        in_own, got_in, in_arrived, own_tokens, grad_state, gain_one,
    )
    returned = rehome(after(jnp.concatenate([mixed.astype(BF), low_grad], axis=0), got))
    mixed_out = returned[None, :BLOCK]
    input_grad = returned[None, BLOCK:].astype(F32)
    got = swap(after(send_next, mlp_send), "hh")
    whole, send = step(side_kernel, [((272, 512), BF), ((80, 512), BF)], send_next, got)

    mlp_got = swap(mlp_send, "bb")
    (mlp_message,) = step(mlp_gather_kernel, [((192, width), BF)], mlp_whole, mlp_got)
    mlp_got = swap(mlp_message, "kk")
    upd_mlp = call(
        update_mlp_kernel,
        [struct(w_gu.shape, F32)] * 3 + [struct(w_down.shape, F32)] * 3,
        [places, mlp_message, mlp_got, w_gu, first_gu, second_gu, w_down, first_down, second_down],
        1,
        scratch=[pltpu.VMEM(w_gu.shape, F32)],
    )

    got = swap(after(send, low_grad, mlp_message), "bb")
    (message,) = step(gather_kernel, [((272, 512), BF)], whole, send, got)
    got = swap(after(message, upd_mlp[5]), "kk")
    own_gains = pick((joined(message) + joined(got)).reshape(-1)[: 2 * width + 2 * HD].reshape(32, 72), x_at * 8 + shard_at)
    upd_qkv = call(
        update_qkv_kernel,
        [struct(w_qkv.shape, F32)] * 3 + [struct(w_out.shape, F32)] * 3,
        [places, message, got, w_qkv, first_qkv, second_qkv, w_out, first_out, second_out],
        1,
        scratch=[pltpu.VMEM(w_qkv.shape, F32)],
    )
    upd_gains = adamw(gains, own_gains, first_gains, second_gains, RATES[4], DECAYS[4])
    return (mixed_out, input_grad, *upd_qkv, *upd_mlp, *upd_gains)


def solution(mesh):
    rows = P(("seq", "shard"), None)
    flat = P(("seq", "shard"))
    whole = P(("shard", "replica"), "seq", None)
    per_weight = (rows, rows, rows, rows, flat)
    return jax.shard_map(
        on_device,
        mesh=mesh,
        in_specs=(whole, whole) + per_weight * 3,
        out_specs=(whole, whole) + (rows,) * 12 + (flat,) * 3,
        check_vma=False,
    )
```

```python
import functools
import math

import jax
import jax.numpy as jnp
import numpy as np
from jax import lax
from jax.experimental import pallas as pl
from jax.experimental.pallas import tpu as pltpu
from jax.sharding import PartitionSpec as P

HEADS = 16
KVH = 8
HD = 128
FF = 3072
STEP = 10
EPS = 1e-06
THETA = 1000000.0
BETA_ONE = 0.9
BETA_TWO = 0.95
ADAM_EPS = 1e-08
RATES = (0.04, 0.2, 0.04, 0.03, 0.4)
DECAYS = (0.1, 0.1, 0.1, 0.1, 0.0)
NEG_FILL = -1e30

AXES = ("seq", "shard", "replica")
DEVICES = 128
BLOCK = 256
BF = jnp.bfloat16
F32 = jnp.float32
VMEM_LIMIT = 52 * 1024 * 1024
SMALL_LIMIT = 12 * 1024 * 1024


def place_of(device):
    replica, shard, x = device % 4, (device // 4) % 8, device // 32
    return x, shard % 4, (replica // 2) * 2 + shard // 4, replica % 2


def device_at(x, y, z, k):
    return (x * 8 + (z % 2) * 4 + y) * 4 + (z // 2) * 2 + k


def flip(dim, x, y, z, k):
    return {
        "a": (x ^ 1, y, z, k),
        "b": (3 - x, y, z, k),
        "c": (x, y ^ 1, z, k),
        "d": (x, 3 - y, z, k),
        "e": (x, y, z ^ 1, k),
        "f": (x, y, 3 - z, k),
        "h": (x, y, z ^ 2, k),
        "k": (x, y, z, k ^ 1),
    }[dim]


def quarter_of(x, k):
    return k if x < 2 else 3 - k


def partners(dims):
    pairs = []
    for device in range(DEVICES):
        place = place_of(device)
        pairs.append((device, device_at(*flip(dims[place[3]], *place))))
    return pairs


def swap(value, dims):
    return lax.ppermute(value, AXES, partners(dims))


def home_pairs():
    pairs = []
    for device in range(DEVICES):
        x, y, z, k = place_of(device)
        moved = {(0, 1): (1, 0), (1, 0): (0, 1), (2, 0): (3, 1), (3, 1): (2, 0)}.get((x, k), (x, k))
        pairs.append((device, device_at(moved[0], y, z, moved[1])))
    return pairs


def rehome(value):
    return lax.ppermute(value, AXES, home_pairs())


def shard_of(place):
    return (place[2] % 2) * 4 + place[1]


def slot_places(device, steps):
    places = [place_of(device)]
    for dims in steps:
        places = places + [flip(dims[p[3]], *p) for p in places]
    return places


def row_table(steps):
    table = np.zeros((DEVICES, 32), np.int32)
    for device in range(DEVICES):
        slots = slot_places(device, ("bb", "aa") + tuple(steps))
        table[device] = [p[0] * 8 + shard_of(p) for p in slots]
    return table


def shard_table(steps):
    table = np.zeros((DEVICES, 8), np.int32)
    for device in range(DEVICES):
        table[device] = [shard_of(p) for p in slot_places(device, steps)]
    return table


STEPS_Q = ("cd", "dc", "ef")
STEPS_ROWS = ("cd", "dc", "ef")
STEPS_MLP = ("dc", "cd", "ef")
STEPS_GRAD_A = ("dc", "ef", "cd")
STEPS_GRAD_B = ("cd", "dc", "ef")
STEPS_GRAD_OUT = ("ef", "dc", "cd")
STEPS_GRAD_Q = ("cd", "ef", "dc")
STEPS_GRAD_KV = ("dc", "cd", "ef")
def block_table():
    table = np.zeros((DEVICES, 4), np.int32)
    for device in range(DEVICES):
        x, _, _, k = place_of(device)
        own = quarter_of(x, k)
        table[device] = [own, own ^ 1, own ^ 3, own ^ 2]
    return table


def x_table():
    table = np.zeros((DEVICES, 4), np.int32)
    for device in range(DEVICES):
        own = place_of(device)[0]
        table[device] = [(0, 2, 3, 1)[own ^ x] for x in range(4)]
    return table


def home_table():
    table = np.zeros((DEVICES, 1), np.int32)
    for device in range(DEVICES):
        x, _, _, k = place_of(device)
        table[device] = quarter_of(x, k) == x
    return table


TABLES = [
    row_table(STEPS_Q), row_table(STEPS_GRAD_Q), row_table(STEPS_GRAD_KV), row_table(STEPS_MLP),
    shard_table(STEPS_ROWS), shard_table(STEPS_MLP), shard_table(STEPS_GRAD_OUT),
    block_table(), x_table(), home_table(), shard_table(STEPS_GRAD_A), shard_table(STEPS_GRAD_B),
]
AT_ALL, AT_Q, AT_KV, AT_MAIN, AT_OUT, AT_DOWN, AT_GRAD_OUT, AT_BLOCK, AT_X, AT_HOME, AT_A, AT_B = np.cumsum(
    [0] + [t.shape[1] for t in TABLES[:-1]]
).tolist()
PLACES = np.concatenate(TABLES, axis=1)


def dot(left, right):
    return lax.dot_general(left, right, (((1,), (0,)), ((), ())), preferred_element_type=F32)


def dot_nt(left, right):
    return lax.dot_general(left, right, (((1,), (1,)), ((), ())), preferred_element_type=F32)


def dot_tn(left, right):
    return lax.dot_general(left, right, (((0,), (0,)), ((), ())), preferred_element_type=F32)


def at(index, size):
    return pl.ds(pl.multiple_of(index * size, size), size)


def score_pieces(keys, queries, block):
    pieces = []
    if block > 0:
        rows = slice(0, block * BLOCK)
        pieces.append((rows, dot_nt(keys[rows, :], queries)))
    rows = slice(block * BLOCK, (block + 1) * BLOCK)
    scores = dot_nt(keys[rows, :], queries)
    key = lax.broadcasted_iota(jnp.int32, scores.shape, 0)
    query = lax.broadcasted_iota(jnp.int32, scores.shape, 1) & (BLOCK - 1)
    pieces.append((rows, jnp.where(key <= query, scores, NEG_FILL)))
    return pieces


def total_of(values):
    result = values[0]
    for value in values[1:]:
        result = result + value
    return result


def double_kernel(held, got, out):
    rows = held.shape[0]
    out[0:16, :] = held[0:16, :] + got[0:16, :]
    out[16:rows, :] = held[16:rows, :]
    out[rows : 2 * rows - 16, :] = got[16:rows, :]


def norm_kernel(own, side, far, last, rows_0, rows_1, rows_2, rows_3, n1, gain_one, gain_two, gain_q, gain_k):
    rows = total_of([r[...].astype(F32) for r in (rows_0, rows_1, rows_2, rows_3)])
    gain = rows[0:1, :]
    gain_one[...] = gain
    gain_two[...] = rows[1:2, :]
    gain_q[...] = rows[2:3, 0:HD]
    gain_k[...] = rows[2:3, HD : 2 * HD]
    for slot, ref in enumerate((own, side, far, last)):
        value = ref[...].astype(F32)
        scale = lax.rsqrt(jnp.mean(value * value, axis=1, keepdims=True) + EPS)
        n1[slot * BLOCK : (slot + 1) * BLOCK, :] = (value * scale * gain).astype(BF)


def halves(rider):
    high = rider.astype(BF).astype(F32)
    return jnp.concatenate([high, rider - high], axis=0).astype(BF)


def joined(message):
    pair = message[message.shape[0] - 16 :, :].astype(F32)
    return pair[:8] + pair[8:]


def fold_kernel(q_low, q_sent, q_got, kv_low, kv_got, q_keep, q_send, kv_keep, kv_send):
    rows = kv_got.shape[0]
    half = rows // 2
    value = q_low[...].astype(F32) + q_got[:rows, :].astype(F32)
    q_keep[...] = value[:half]
    q_send[:half, :] = value[half:].astype(BF)
    q_send[half:, :] = halves(joined(q_sent) + joined(q_got))
    value = kv_low[...].astype(F32) + kv_got[...].astype(F32)
    kv_keep[...] = value[:half]
    kv_send[...] = value[half:].astype(BF)


def fold_last_kernel(q_low, q_sent, q_got, kv_low, kv_got, out_low, out_got, keep, send):
    value = q_low[...] + q_got[:128, :].astype(F32)
    keep[0:64, :] = value[:64]
    send[0:64, :] = value[64:].astype(BF)
    value = kv_low[...] + kv_got[...].astype(F32)
    keep[64:128, :] = value[:64]
    send[64:128, :] = value[64:].astype(BF)
    value = (out_low[...] + out_got[...].astype(F32)).astype(BF)
    keep[128:256, :] = value.astype(F32)
    send[128:256, :] = value
    send[256:272, :] = halves(joined(q_sent) + joined(q_got))


def sum_kernel(keep, sent, got, send):
    send[0:256, :] = (keep[0:256, :].astype(F32) + got[0:256, :].astype(F32)).astype(BF)
    send[256:272, :] = halves(joined(sent) + joined(got))


def side_kernel(sent, got, whole, send):
    value = (sent[0:256, :].astype(F32) + got[0:256, :].astype(F32)).astype(BF)
    pair = halves(joined(sent) + joined(got))
    whole[0:256, :] = value
    whole[256:272, :] = pair
    send[0:32, :] = value[32:64]
    send[32:64, :] = value[96:128]
    send[64:80, :] = pair


def gather_kernel(whole, sent, got, message):
    message[0:32, :] = whole[0:32, :]
    message[32:64, :] = whole[64:96, :]
    message[64:128, :] = got[0:64, :]
    message[128:256, :] = whole[128:256, :]
    message[256:272, :] = halves(joined(sent) + joined(got))


def fold_pair_kernel(a_low, a_got, b_low, b_got, a_keep, a_send, b_keep, b_send):
    for low, got, keep, send in ((a_low, a_got, a_keep, a_send), (b_low, b_got, b_keep, b_send)):
        half = low.shape[0] // 2
        for slot in range(2 * half):
            value = (low[slot].astype(F32) + got[slot].astype(F32)).astype(BF)
            if slot < half:
                keep[slot] = value
            else:
                send[slot - half] = value


def fold_pair_last_kernel(a_low, a_got, b_low, b_got, keep, send):
    value = (a_low[0].astype(F32) + a_got[0].astype(F32)).astype(BF)
    keep[...] = value[0:96]
    send[0:48, :] = value[96:144]
    send[48:192, :] = (b_low[0].astype(F32) + b_got[0].astype(F32)).astype(BF)


def mlp_sum_kernel(keep, send, got, out):
    out[0:96, :] = (keep[...].astype(F32) + got[0:96, :].astype(F32)).astype(BF)
    out[96:192, :] = (send[96:192, :].astype(F32) + got[96:192, :].astype(F32)).astype(BF)


def mlp_side_kernel(low, got, whole, send):
    value = (low[...].astype(F32) + got[...].astype(F32)).astype(BF)
    whole[...] = value
    send[...] = value[32:96]


def mlp_gather_kernel(whole, got, message):
    message[0:32, :] = whole[0:32, :]
    message[32:64, :] = got[0:32, :]
    message[64:96, 0:512] = whole[64:96, 0:512]
    message[64:96, 512:1024] = got[32:64, 512:1024]
    message[96:192, :] = whole[96:192, :]


def state_kernel(keep, got, far, tokens, gain, state, n2):
    value = tokens[...].astype(F32) + keep[...] + got[0].astype(F32) + far[...].astype(F32)
    state[...] = value
    scale = lax.rsqrt(jnp.mean(value * value, axis=1, keepdims=True) + EPS)
    n2[...] = (value * scale * gain[...]).astype(BF)


def far_kernel(part, keep, got, out):
    out[...] = (keep[...] + got[part].astype(F32)).astype(BF)


def state_back_kernel(keep, got, far, state, mix, gain, grad, low, grad_gain):
    grad_n2 = keep[...] + got[0].astype(F32) + far[...].astype(F32)
    value = state[...]
    scale = lax.rsqrt(jnp.mean(value * value, axis=1, keepdims=True) + EPS)
    unit = value * scale
    scaled = grad_n2 * gain[...]
    result = mix[...].astype(F32) + scale * (scaled - unit * jnp.mean(scaled * unit, axis=1, keepdims=True))
    grad[...] = result
    low[...] = result.astype(BF)
    grad_gain[...] = jnp.sum(grad_n2 * unit, axis=0, keepdims=True)


def input_back_kernel(keep, got, far, tokens, grad_state, gain, low):
    grad_n1 = keep[...] + got[0].astype(F32) + far[...].astype(F32)
    value = tokens[...].astype(F32)
    scale = lax.rsqrt(jnp.mean(value * value, axis=1, keepdims=True) + EPS)
    unit = value * scale
    scaled = grad_n1 * gain[...]
    result = grad_state[...] + scale * (scaled - unit * jnp.mean(scaled * unit, axis=1, keepdims=True))
    low[...] = result.astype(BF)


def columns(start, size):
    return pl.ds(pl.multiple_of(start, 128), size)


def update_refs(refs, gradient, outs, rate, decay_rate):
    results = adamw(refs[0][...], gradient, refs[1][...], refs[2][...], rate, decay_rate)
    for out, result in zip(outs, results):
        out[...] = result


def update_qkv_kernel(places, message, got, w_q, m_q, s_q, w_o, m_o, s_o, *outs):
    gradient = outs[6]
    for slot, (ref, row) in enumerate(((message, 0), (got, 0), (message, 64), (got, 64))):
        quarter = places[AT_BLOCK + slot]
        gradient[:, columns(quarter * 512, 512)] = ref[row : row + 32, :].astype(F32)
        gradient[:, columns(2048 + quarter * 256, 256)] = ref[row + 32 : row + 64, 0:256].astype(F32)
        gradient[:, columns(3072 + quarter * 256, 256)] = ref[row + 32 : row + 64, 256:512].astype(F32)
    update_refs((w_q, m_q, s_q), gradient[...], outs[0:3], RATES[0], DECAYS[0])
    home = places[AT_HOME] == 1
    for half in range(2):
        here = slice(half * 512, half * 512 + 512)
        rows = slice(128 + half * 64, 192 + half * 64)
        part = jnp.where(home, message[rows, :].astype(F32), got[rows, :].astype(F32))
        refs = (w_o.at[:, here], m_o.at[:, here], s_o.at[:, here])
        update_refs(refs, part, [out.at[:, here] for out in outs[3:6]], RATES[1], DECAYS[1])


def update_mlp_kernel(places, message, got, w_g, m_g, s_g, w_d, m_d, s_d, *outs):
    gradient = outs[6]
    part = FF // 4
    for slot, (ref, side) in enumerate(((message, 0), (got, 0), (message, 1), (got, 1))):
        quarter = places[AT_BLOCK + slot]
        main = ref[side * 32 : side * 32 + 32, :].astype(F32)
        gradient[:, columns(quarter * part, part)] = main[:, :part]
        gradient[:, columns(FF + quarter * part, 1024 - part)] = main[:, part:]
        gradient[:, columns(FF + quarter * part + 1024 - part, 512)] = ref[
            64:96, side * 512 : side * 512 + 512
        ].astype(F32)
    update_refs((w_g, m_g, s_g), gradient[...], outs[0:3], RATES[2], DECAYS[2])
    home = places[AT_HOME] == 1
    total = jnp.where(home, message[96:192, :].astype(F32), got[96:192, :].astype(F32))
    update_refs((w_d, m_d, s_d), total, outs[3:6], RATES[3], DECAYS[3])


def attention_kernel(
    places, n1, w_0, w_1, w_2, w_3, cos, sin, gain_q, gain_k, w_all, pre, q_out, k_out, v_out, att, log_total
):
    factor = 1.0 / math.sqrt(HD)
    for slot in range(32):
        row = 16 + (slot % 8) * 32
        w_all[at(places[AT_ALL + slot], 32), :] = (w_0, w_1, w_2, w_3)[slot // 8][row : row + 32, :]
    for slot in range(4):
        block = places[AT_BLOCK + slot]
        here = at(block, BLOCK)
        projected = dot(n1[slot * BLOCK : (slot + 1) * BLOCK, :], w_all[...])
        pre[here, :] = projected[:, :768]
        cos_part = cos[here, :]
        sin_part = sin[here, :]

        def turned(column, gain):
            head = projected[:, column : column + HD]
            normed = head * lax.rsqrt(jnp.mean(head * head, axis=1, keepdims=True) + EPS) * gain[...]
            return normed * cos_part + pltpu.roll(normed, HD // 2, 1) * sin_part

        for head in range(4):
            rotated = (turned(head * HD, gain_q) * factor).astype(BF)
            q_out[head // 2, block, (head % 2) * BLOCK : (head % 2 + 1) * BLOCK, :] = rotated
        for head in range(2):
            k_out[head, here, :] = turned(512 + head * HD, gain_k).astype(BF)
            v_out[head, here, :] = projected[:, 768 + head * HD : 768 + (head + 1) * HD].astype(BF)
    for group in range(2):
        for block in range(4):
            pieces = score_pieces(k_out.at[group], q_out[group, block], block)
            top = jnp.max(pieces[0][1], axis=0, keepdims=True)
            for _, scores in pieces[1:]:
                top = jnp.maximum(top, jnp.max(scores, axis=0, keepdims=True))
            exponents = [(rows_here, jnp.exp(scores - top)) for rows_here, scores in pieces]
            sums = total_of([jnp.sum(e, axis=0, keepdims=True) for _, e in exponents])
            inverse = 1.0 / sums
            attended = total_of(
                [dot_tn(v_out[group, rows_here, :], (e * inverse).astype(BF)) for rows_here, e in exponents]
            )
            attended = attended.T.astype(BF)
            log_total[group * 4 + block : group * 4 + block + 1, :] = top + jnp.log(sums)
            own = places[AT_BLOCK] ^ block
            slot = own ^ (own >> 1)
            for head in range(2):
                column = (group * 2 + head) * HD
                att[at(slot, BLOCK), column : column + HD] = attended[head * BLOCK : (head + 1) * BLOCK]


def attention_back_kernel(
    places, own, side, far, last, w_out, queries, keys, values, pre, log_total, cos, sin, gain_q, gain_k,
    grad_pre, grad_gain_q, grad_gain_k, grad_att, grad_k, grad_v,
):
    factor = 1.0 / math.sqrt(HD)
    for slot, ref in enumerate((own, side, far, last)):
        part = dot_nt(ref[...], w_out[...]).astype(BF)
        for head in range(4):
            grad_att[head // 2, places[AT_BLOCK + slot], (head % 2) * BLOCK : (head % 2 + 1) * BLOCK, :] = part[
                :, head * HD : (head + 1) * HD
            ]

    def back_through(grad, head, cos_part, sin_part, gain):
        turned = grad * cos_part - pltpu.roll(grad, HD // 2, 1) * sin_part
        scale = lax.rsqrt(jnp.mean(head * head, axis=1, keepdims=True) + EPS)
        unit = head * scale
        scaled = turned * gain[...]
        grad_head = scale * (scaled - unit * jnp.mean(scaled * unit, axis=1, keepdims=True))
        return grad_head, jnp.sum(turned * unit, axis=0, keepdims=True)

    total_q = jnp.zeros((1, HD), F32)
    total_k = jnp.zeros((1, HD), F32)
    for group in range(2):
        for block in range(3, -1, -1):
            own = places[AT_BLOCK] ^ block
            there = at(own ^ (own >> 1), BLOCK)
            query = queries[group, block]
            grad_o = grad_att[group, block]
            logs = log_total[group * 4 + block : group * 4 + block + 1, :]
            probs = [(r, jnp.exp(scores - logs)) for r, scores in score_pieces(keys.at[group], query, block)]
            grad_probs = [dot_nt(values[group, r, :], grad_o) for r, _ in probs]
            inner = total_of([jnp.sum(p * g, axis=0, keepdims=True) for (_, p), g in zip(probs, grad_probs)])
            grad_scores = [(r, (p * (g - inner)).astype(BF)) for (r, p), g in zip(probs, grad_probs)]
            grad_q = total_of([dot_tn(keys[group, r, :], d) for r, d in grad_scores]).T * factor
            for (r, p), (_, d) in zip(probs, grad_scores):
                part_k = dot(d, query)
                part_v = dot(p.astype(BF), grad_o)
                if block == 3:
                    grad_k[r, :] = part_k
                    grad_v[r, :] = part_v
                else:
                    grad_k[r, :] += part_k
                    grad_v[r, :] += part_v
            for head in range(2):
                column = (group * 2 + head) * HD
                grad_head, gain_part = back_through(
                    grad_q[head * BLOCK : (head + 1) * BLOCK],
                    pre[block * BLOCK : (block + 1) * BLOCK, column : column + HD],
                    cos[block * BLOCK : (block + 1) * BLOCK, :],
                    sin[block * BLOCK : (block + 1) * BLOCK, :],
                    gain_q,
                )
                total_q = total_q + gain_part
                grad_pre[there, column : column + HD] = grad_head.astype(BF)
        for block in range(4):
            own = places[AT_BLOCK] ^ block
            there = at(own ^ (own >> 1), BLOCK)
            column = 512 + group * HD
            grad_head, gain_part = back_through(
                grad_k[block * BLOCK : (block + 1) * BLOCK, :],
                pre[block * BLOCK : (block + 1) * BLOCK, column : column + HD],
                cos[block * BLOCK : (block + 1) * BLOCK, :],
                sin[block * BLOCK : (block + 1) * BLOCK, :],
                gain_k,
            )
            total_k = total_k + gain_part
            grad_pre[there, column : column + HD] = grad_head.astype(BF)
            grad_pre[there, 768 + group * HD : 768 + (group + 1) * HD] = grad_v[
                block * BLOCK : (block + 1) * BLOCK, :
            ].astype(BF)
    grad_gain_q[...] = total_q
    grad_gain_k[...] = total_k


def out_kernel(places, att, low_slots, high_slots, w_out, keep_own, keep_far, send):
    for slot in range(8):
        slots = low_slots if slot < 4 else high_slots
        w_out[at(places[AT_OUT + slot], 64), :] = slots[slot % 4]
    for slot in range(4):
        part = dot(att[slot * BLOCK : (slot + 1) * BLOCK, :], w_out[...])
        if slot % 2 == 1:
            send[slot // 2] = part.astype(BF)
        else:
            (keep_own if slot == 0 else keep_far)[...] = part


def out_weights_kernel(places, att, own, side, far, last, low, high, scratch):
    total = jnp.zeros(scratch.shape, F32)
    for slot, ref in enumerate((own, side, far, last)):
        total = total + dot_tn(att[slot * BLOCK : (slot + 1) * BLOCK, :], ref[...])
    scratch[...] = total.astype(BF)
    for slot in range(8):
        target = low if slot < 4 else high
        for half in range(2):
            there = (slot % 4) * 128 + half * 64
            target[there : there + 64, :] = scratch[at(places[AT_GRAD_OUT + slot], 64), half * 512 : half * 512 + 512]


def mlp_kernel(
    places, n2_first, n2_second, mix_first, mix_second, low_slots, high_slots,
    hidden, grad_gu, mix_keep, grad_keep, send, w_gu, w_down,
):
    for slot in range(8):
        ref = low_slots if slot < 4 else high_slots
        for x in range(4):
            start, side = (x // 2) * 96, x % 2
            here = at(places[AT_MAIN + slot * 4 + x], 32)
            w_gu[here, 0:1024] = ref[slot % 4, start + side * 32 : start + side * 32 + 32, :]
            w_gu[here, 1024:1536] = ref[slot % 4, start + 64 : start + 96, side * 512 : side * 512 + 512]
        w_down[at(places[AT_DOWN + slot], 96), :] = ref[slot % 4, 192:288, :]
    half = FF // 4
    for slot, (n2, grad_mix) in enumerate(((n2_first, mix_first), (n2_second, mix_second))):
        here = slice(slot * BLOCK, (slot + 1) * BLOCK)
        gate_up = dot(n2[...], w_gu[...])
        grad_hidden = dot_nt(grad_mix[...], w_down[...])
        gate = gate_up[:, :half]
        up = gate_up[:, half:]
        sigmoid = 1.0 / (1.0 + jnp.exp(-gate))
        silu = gate * sigmoid
        low_hidden = (silu * up).astype(BF)
        hidden[here, :] = low_hidden
        grad_gate = grad_hidden * up * (sigmoid * (1.0 + gate * (1.0 - sigmoid)))
        low_grad = jnp.concatenate([grad_gate, grad_hidden * silu], axis=1).astype(BF)
        grad_gu[here, :] = low_grad
        back = dot_nt(low_grad, w_gu[...])
        mixed = dot(low_hidden, w_down[...])
        if slot == 0:
            grad_keep[...] = back
            mix_keep[...] = mixed
        else:
            send[0] = back.astype(BF)
            send[1] = mixed.astype(BF)


def mlp_weights_kernel(
    places, n2_0, n2_1, n2_2, n2_3, mix_0, mix_1, mix_2, mix_3, hidden_own, hidden_far, gu_own, gu_far,
    a_low, a_high, b_low, b_high, out, total,
):
    n2s, mixes = (n2_0, n2_1, n2_2, n2_3), (mix_0, mix_1, mix_2, mix_3)

    def tokens(near, far, slot):
        ref = near if slot < 2 else far
        return ref, slice((slot % 2) * BLOCK, (slot % 2 + 1) * BLOCK)

    for x in range(4):
        here = slice(x * BLOCK, (x + 1) * BLOCK)
        part = jnp.zeros((BLOCK, 2 * FF // 4), F32)
        for slot in range(4):
            ref, rows = tokens(gu_own, gu_far, slot)
            part = part + dot_tn(n2s[slot][:, here], ref[rows, :])
        total[places[AT_X + x]] = part.astype(BF).reshape(8, 32, 2 * FF // 4)
    for slot in range(4):
        start = (slot // 2) * 96
        side = slot % 2
        out[:, start + side * 32 : start + side * 32 + 32, :] = total[slot, :, :, 0:1024]
        out[:, start + 64 : start + 96, side * 512 : side * 512 + 512] = total[slot, :, :, 1024:1536]
    for third in range(3):
        here = slice(third * BLOCK, (third + 1) * BLOCK)
        part = jnp.zeros((BLOCK, out.shape[2]), F32)
        for slot in range(4):
            ref, rows = tokens(hidden_own, hidden_far, slot)
            part = part + dot_tn(ref[rows, here], mixes[slot][...])
        total_down = part.astype(BF)
        for piece in range(8):
            row = third * BLOCK + piece * 32
            out[row // 96, 192 + row % 96 : 192 + row % 96 + 32, :] = total_down[piece * 32 : piece * 32 + 32]
    for slot in range(8):
        (a_low if slot < 4 else a_high)[slot % 4] = out[places[AT_A + slot], 0:144, :]
        (b_low if slot < 4 else b_high)[slot % 4] = out[places[AT_B + slot], 144:288, :]


def qkv_back_kernel(
    places, n1, grad_pre, w_all, own, side, far, last, gain_two, gain_q, gain_k,
    q_low, q_high, kv_low, kv_high, keep_own, keep_far, send, total,
):
    for x in range(4):
        here = slice(x * BLOCK, (x + 1) * BLOCK)
        total[here, :] = dot_tn(n1[:, here], grad_pre[...]).astype(BF)
    for slot in range(32):
        there = slice((slot % 16) * 32, (slot % 16) * 32 + 32)
        (q_low if slot < 16 else q_high)[there, :] = total[at(places[AT_Q + slot], 32), 0:512]
        (kv_low if slot < 16 else kv_high)[there, :] = total[at(places[AT_KV + slot], 32), 512:1024]
    gain_sum = jnp.zeros((1, n1.shape[1]), F32)
    for slot, ref in enumerate((own, side, far, last)):
        part = dot_nt(grad_pre[slot * BLOCK : (slot + 1) * BLOCK, :], w_all[...])
        value = ref[...].astype(F32)
        scale = lax.rsqrt(jnp.mean(value * value, axis=1, keepdims=True) + EPS)
        gain_sum = gain_sum + jnp.sum(part * (value * scale), axis=0, keepdims=True)
        if slot % 2 == 1:
            send[slot // 2] = part.astype(BF)
        else:
            (keep_own if slot == 0 else keep_far)[...] = part
    rows = [gain_sum[:, :512], gain_sum[:, 512:], gain_two[:, :512], gain_two[:, 512:]]
    rows += [jnp.concatenate([gain_q[...], gain_k[...], jnp.zeros((1, 256), F32)], axis=1), jnp.zeros((3, 512), F32)]
    q_high[512:528, :] = halves(jnp.concatenate(rows, axis=0))


def far_sum(part, keep, got):
    kernel = functools.partial(far_kernel, part)
    return call(kernel, [struct(keep.shape, BF)], [keep, got], 0, small=True)[0]


def call(kernel, outs, args, scalars, scratch=(), flops=0, small=False):
    space = [pl.BlockSpec(memory_space=pltpu.SMEM)] * scalars
    space += [pl.BlockSpec(memory_space=pltpu.VMEM)] * (len(args) - scalars)
    size = sum(math.prod(a.shape) * a.dtype.itemsize for a in list(args) + list(outs))
    return pl.pallas_call(
        kernel,
        out_shape=outs,
        in_specs=space,
        out_specs=[pl.BlockSpec(memory_space=pltpu.VMEM)] * len(outs),
        scratch_shapes=list(scratch),
        compiler_params=pltpu.CompilerParams(vmem_limit_bytes=SMALL_LIMIT if small else VMEM_LIMIT),
        cost_estimate=pl.CostEstimate(flops=flops, bytes_accessed=size, transcendentals=0),
    )(*args)


def struct(shape, dtype):
    return jax.ShapeDtypeStruct(shape, dtype)


def rms_scale(value, gain):
    return value * lax.rsqrt(jnp.mean(value * value, axis=-1, keepdims=True) + EPS) * gain


def rms_back(value, gain, grad):
    scale = lax.rsqrt(jnp.mean(value * value, axis=-1, keepdims=True) + EPS)
    scaled = grad * gain
    inner = jnp.mean(scaled * value, axis=-1, keepdims=True)
    grad_value = scale * scaled - value * (scale * scale * scale) * inner
    return grad_value, jnp.sum(grad * value * scale, axis=0)


def adamw(weight, gradient, first_moment, second_moment, rate, decay_rate):
    first_moment = BETA_ONE * first_moment + (1.0 - BETA_ONE) * gradient
    second_moment = BETA_TWO * second_moment + (1.0 - BETA_TWO) * gradient * gradient
    first_hat = first_moment / (1.0 - BETA_ONE**STEP)
    second_hat = second_moment / (1.0 - BETA_TWO**STEP)
    weight = weight - rate * (first_hat / (jnp.sqrt(second_hat) + ADAM_EPS) + decay_rate * weight)
    return (weight, first_moment, second_moment)


def rounded(value):
    return lax.reduce_precision(value.astype(F32), 8, 7)


def after(value, *others):
    return lax.optimization_barrier((value,) + others)[0]


def pick(stack, index):
    return lax.dynamic_index_in_dim(stack, index, 0, keepdims=False)


def on_device(
    tokens,
    cotangent,
    w_qkv,
    w_out,
    w_gu,
    w_down,
    gains,
    first_qkv,
    first_out,
    first_gu,
    first_down,
    first_gains,
    second_qkv,
    second_out,
    second_gu,
    second_down,
    second_gains,
):
    width = tokens.shape[-1]
    x_at = lax.axis_index("seq")
    shard_at = lax.axis_index("shard")
    replica_at = lax.axis_index("replica")
    device = (x_at * 8 + shard_at) * 4 + replica_at
    core = replica_at % 2
    quarter = jnp.where(x_at < 2, core, 3 - core)
    places = pick(jnp.asarray(PLACES), device)

    positions = jnp.arange(4 * BLOCK, dtype=F32)
    frequency = THETA ** (-jnp.arange(HD // 2, dtype=F32) / (HD // 2))
    angles = positions[:, None] * frequency[None, :]
    cos_half, sin_half = jnp.cos(angles), jnp.sin(angles)
    cos_table = jnp.concatenate([cos_half, cos_half], axis=1)
    sin_table = jnp.concatenate([-sin_half, sin_half], axis=1)

    low_qkv = w_qkv.astype(BF)
    stack_qkv = jnp.stack(
        [
            jnp.concatenate(
                [
                    low_qkv[:, 512 * n : 512 * (n + 1)],
                    low_qkv[:, 2048 + 256 * n : 2304 + 256 * n],
                    low_qkv[:, 3072 + 256 * n : 3328 + 256 * n],
                ],
                axis=1,
            )
            for n in range(4)
        ]
    )
    spot = (jnp.arange(32) == x_at * 8 + shard_at)[:, None]
    gain_vals = jnp.where(spot, gains[None, :], 0.0).reshape(1, -1)
    gain_vals = jnp.pad(gain_vals, ((0, 0), (0, 3 * 1024 - 32 * 72))).reshape(3, 1024)
    gain_rows = jnp.pad(gain_vals, ((0, 13), (0, 0))).astype(BF)

    def doubled(held, got):
        return call(double_kernel, [struct((2 * held.shape[0] - 16, 1024), BF)], [held, got], 0, small=True)[0]

    qkv_one = jnp.concatenate([gain_rows, pick(stack_qkv, quarter)], axis=0)
    sent = jnp.concatenate([gain_rows, pick(stack_qkv, 3 - quarter)], axis=0)
    qkv_two = doubled(qkv_one, swap(sent, "bb"))
    qkv_four = doubled(qkv_two, swap(qkv_two, "aa"))
    qkv_eight = doubled(qkv_four, swap(qkv_four, STEPS_Q[0]))

    low_gu = after(w_gu, qkv_four).astype(BF)
    part = FF // 4
    stack_gu = jnp.stack(
        [
            jnp.concatenate(
                [low_gu[:, part * n : part * (n + 1)], low_gu[:, FF + part * n : FF + part * (n + 1)]], axis=1
            )
            for n in range(4)
        ]
    )
    gu_one = pick(stack_gu, quarter)[None]
    gu_two = jnp.concatenate([gu_one, swap(pick(stack_gu, 3 - quarter)[None], "bb")], axis=0)

    first = rehome(jnp.concatenate([tokens[0], w_out.astype(BF), w_down.astype(BF)], axis=0))
    own_tokens = first[:BLOCK]
    out_one = first[None, BLOCK : BLOCK + 64]
    down_one = first[BLOCK + 64 :]
    far_tokens = swap(after(own_tokens, gu_two), "bb")
    side_tokens = swap(after(own_tokens, qkv_eight), "kk")

    qkv_next = swap(qkv_eight, STEPS_Q[1])
    qkv_parts = [qkv_eight, qkv_next, swap(qkv_eight, STEPS_Q[2]), swap(qkv_next, STEPS_Q[2])]
    gu_four = jnp.concatenate([gu_two, swap(after(gu_two, qkv_eight, cos_table, sin_table, places), "aa")], axis=0)
    last_tokens = swap(far_tokens, "kk")
    own_mix = rehome(after(cotangent[0], gu_four))
    far_mix = swap(after(own_mix, far_tokens), "bb")
    side_mix = swap(after(own_mix, qkv_next), "kk")
    out_two = jnp.concatenate([out_one, swap(after(out_one, qkv_eight), STEPS_ROWS[0])], axis=0)
    out_low = jnp.concatenate([out_two, swap(out_two, STEPS_ROWS[1])], axis=0)
    out_high = swap(out_low, STEPS_ROWS[2])

    last = gu_four[:, :, 1024:]
    mlp_one = jnp.concatenate(
        [
            gu_four[0, :, :1024], gu_four[1, :, :1024], jnp.concatenate([last[0], last[1]], axis=1),
            gu_four[2, :, :1024], gu_four[3, :, :1024], jnp.concatenate([last[2], last[3]], axis=1),
            down_one,
        ],
        axis=0,
    )[None]
    mlp_two = jnp.concatenate([mlp_one, swap(after(mlp_one, out_low, qkv_next), STEPS_MLP[0])], axis=0)

    total = 4 * BLOCK
    n1, gain_one, gain_two, gain_query, gain_key = call(
        norm_kernel,
        [struct((total, width), BF)] + [struct((1, width), F32)] * 2 + [struct((1, HD), F32)] * 2,
        [own_tokens, side_tokens, far_tokens, last_tokens] + [piece[:16] for piece in qkv_parts],
        0,
        small=True,
    )
    w_all, pre, queries, keys, values, att, log_total = call(
        attention_kernel,
        [
            struct((width, 1024), BF),
            struct((total, 768), F32),
            struct((2, 4, 2 * BLOCK, HD), BF),
            struct((2, total, HD), BF),
            struct((2, total, HD), BF),
            struct((total, 512), BF),
            struct((8, 2 * BLOCK), F32),
        ],
        [
            places, n1, *qkv_parts,
            cos_table, sin_table, gain_query, gain_key,
        ],
        1,
        flops=14_000_000_000,
    )
    last_mix = swap(after(far_mix, att), "kk")
    mlp_low = jnp.concatenate([mlp_two, swap(after(mlp_two, out_low), STEPS_MLP[1])], axis=0)
    mlp_high = swap(after(mlp_low, att), STEPS_MLP[2])
    w_out_all, out_own, out_keep, out_send = call(
        out_kernel,
        [struct((512, width), BF)] + [struct((BLOCK, width), F32)] * 2 + [struct((2, BLOCK, width), BF)],
        [places, after(att, mlp_low, far_mix), out_low, out_high],
        1,
        flops=4_500_000_000,
    )
    got_out = swap(out_send, "kk")
    out_far = far_sum(1, out_keep, got_out)
    state, n2 = call(
        state_kernel,
        [struct((BLOCK, width), F32), struct((BLOCK, width), BF)],
        [out_own, got_out, swap(out_far, "bb"), own_tokens, gain_two],
        0,
        small=True,
    )
    far_n2 = swap(n2, "bb")
    side_n2 = swap(n2, "kk")


    def mlp(*parts):
        return call(
            mlp_kernel,
            [
                struct((2 * BLOCK, part), BF),
                struct((2 * BLOCK, 2 * part), BF),
                struct((BLOCK, width), F32),
                struct((BLOCK, width), F32),
                struct((2, BLOCK, width), BF),
            ],
            [places, *parts, mlp_low, mlp_high],
            1,
            scratch=[pltpu.VMEM((width, 2 * part), BF), pltpu.VMEM((part, width), BF)],
            flops=10_400_000_000,
        )

    hidden_own, gu_own, mix_keep_own, back_keep_own, send_own = mlp(n2, side_n2, own_mix, side_mix)
    far_n2 = after(far_n2, send_own)
    last_n2 = swap(far_n2, "kk")
    hidden_far, gu_far, mix_keep_far, back_keep_far, send_far = mlp(
        far_n2, last_n2, far_mix, last_mix
    )
    got_far = swap(send_far, "kk")
    got_own = swap(after(send_own, got_far), "kk")
    back_far = far_sum(0, back_keep_far, got_far)
    back_arrived = swap(back_far, "bb")
    grad_mlp_parts = call(
        mlp_weights_kernel,
        [struct((4, 144, width), BF)] * 4,
        [
            places, after(n2, back_far), side_n2, far_n2, last_n2, own_mix, side_mix, far_mix, last_mix,
            hidden_own, hidden_far, gu_own, gu_far,
        ],
        1,
        scratch=[pltpu.VMEM((8, 288, width), BF), pltpu.VMEM((4, 8, 32, 2 * part), BF)],
        flops=12_200_000_000,
    )
    grad_state, low_state, grad_gain_two = call(
        state_back_kernel,
        [struct((BLOCK, width), F32), struct((BLOCK, width), BF), struct((1, width), F32)],
        [back_keep_own, got_own, after(back_arrived, grad_mlp_parts[1]), state, own_mix, gain_two],
        0,
        small=True,
    )
    far_state = swap(low_state, "bb")
    side_state = swap(low_state, "kk")
    last_state = swap(far_state, "kk")

    def fold_mlp(a_low, a_high, b_low, b_high, index, tie):
        slots = a_low.shape[0] // 2
        outs = [struct((slots, 144, width), BF)] * 4
        args = [
            a_low, after(swap(after(a_high, tie), STEPS_GRAD_A[index]), b_high),
            b_low, swap(after(b_high, tie), STEPS_GRAD_B[index]),
        ]
        if slots == 0:
            kernel, outs = fold_pair_last_kernel, [struct((96, width), BF), struct((192, width), BF)]
        else:
            kernel = fold_pair_kernel
        return call(kernel, outs, args, 0, small=True)

    mlp_grads = fold_mlp(*grad_mlp_parts, 2, low_state)

    out_grads = call(
        out_weights_kernel,
        [struct((512, 512), BF)] * 2,
        [places, att, low_state, side_state, far_state, last_state],
        1,
        scratch=[pltpu.VMEM((512, width), BF)],
        flops=3_500_000_000,
    )
    grad_low, grad_high = out_grads
    got_grad = swap(grad_high, STEPS_GRAD_OUT[2])
    mix_far = (mix_keep_far + got_far[1].astype(F32)).astype(BF)
    mix_arrived = swap(after(mix_far, last_state), "bb")
    grad_pre, grad_gain_query, grad_gain_key = call(
        attention_back_kernel,
        [struct((total, 1024), BF), struct((1, HD), F32), struct((1, HD), F32)],
        [
            places, after(low_state, grad_low, mlp_grads[0]), side_state, far_state, last_state, w_out_all, queries, keys, values, pre,
            log_total, cos_table, sin_table, gain_query, gain_key,
        ],
        1,
        scratch=[
            pltpu.VMEM((2, 4, 2 * BLOCK, HD), BF), pltpu.VMEM((total, HD), F32), pltpu.VMEM((total, HD), F32)
        ],
        flops=18_000_000_000,
    )
    grad_total = grad_low.astype(F32) + after(got_grad, grad_pre).astype(F32)
    grad_low, grad_high = grad_total[:256], grad_total[256:].astype(BF)
    got_grad = swap(grad_high, STEPS_GRAD_OUT[1])
    mlp_grads = fold_mlp(*mlp_grads, 1, mlp_grads[1])
    q_low, q_high, kv_low, kv_high, in_own, in_keep, in_send = call(
        qkv_back_kernel,
        [struct((512, 512), BF), struct((528, 512), BF), struct((512, 512), BF), struct((512, 512), BF)]
        + [struct((BLOCK, width), F32)] * 2
        + [struct((2, BLOCK, width), BF)],
        [
            places, after(n1, mix_arrived, grad_high, mlp_grads[0]), grad_pre, w_all, own_tokens, side_tokens, far_tokens, last_tokens,
            grad_gain_two, grad_gain_query, grad_gain_key,
        ],
        1,
        scratch=[pltpu.VMEM((width, 1024), BF)],
        flops=11_000_000_000,
    )
    def step(kernel, outs, *args):
        return call(kernel, [struct(*out) for out in outs], args, 0, small=True)

    def fold(rows, q, kv, index, *ties):
        q_got = swap(after(q[1], *ties) if ties else q[1], STEPS_GRAD_Q[index])
        kv_got = swap(kv[1], STEPS_GRAD_KV[index])
        half = rows // 2
        outs = [((half, 512), F32), ((half + 16, 512), BF), ((half, 512), F32), ((half, 512), BF)]
        result = step(fold_kernel, outs, q[0], q[1], q_got, kv[0], kv_got)
        return result[0:2], result[2:4]

    mlp_keep, mlp_send = fold_mlp(*mlp_grads, 0, mlp_grads[1])
    in_send = after(in_send, mlp_send, got_grad)
    kv_high = after(kv_high, mlp_send, got_grad)
    got_in = swap(in_send, "kk")
    in_far = far_sum(1, in_keep, got_in)
    in_arrived = swap(in_far, "bb")

    q, kv = fold(512, (q_low, q_high), (kv_low, kv_high), 2, got_grad, mlp_send)
    grad_total = grad_low + got_grad.astype(F32)
    grad_low, grad_high = grad_total[:128], grad_total[128:]
    got_grad = swap(grad_high.astype(BF), STEPS_GRAD_OUT[0])
    mixed = state + (mix_keep_own + got_own[1].astype(F32)) + after(mix_arrived, q[1]).astype(F32)

    mlp_send = after(mlp_send, q[1])
    mlp_got = swap(mlp_send, "aa")
    (mlp_rows,) = step(mlp_sum_kernel, [((192, width), BF)], mlp_keep, mlp_send, mlp_got)

    q, kv = fold(256, q, kv, 1, in_arrived, got_grad)
    q_got = swap(after(q[1], mlp_got), STEPS_GRAD_Q[0])
    kv_got = swap(kv[1], STEPS_GRAD_KV[0])
    keep, send = step(
        fold_last_kernel,
        [((256, 512), F32), ((272, 512), BF)],
        q[0], q[1], q_got, kv[0], kv_got, grad_low, got_grad,
    )
    mlp_got = swap(mlp_rows, "hh")
    mlp_whole, mlp_send = step(mlp_side_kernel, [((192, width), BF), ((64, width), BF)], mlp_rows, mlp_got)

    got = swap(send, "aa")
    (send_next,) = step(sum_kernel, [((272, 512), BF)], keep, send, got)
    (low_grad,) = step(
        input_back_kernel,
        [((BLOCK, width), BF)],
        in_own, got_in, in_arrived, own_tokens, grad_state, gain_one,
    )
    returned = rehome(after(jnp.concatenate([mixed.astype(BF), low_grad], axis=0), got))
    mixed_out = returned[None, :BLOCK]
    input_grad = returned[None, BLOCK:].astype(F32)
    got = swap(after(send_next, mlp_send), "hh")
    whole, send = step(side_kernel, [((272, 512), BF), ((80, 512), BF)], send_next, got)

    mlp_got = swap(mlp_send, "bb")
    (mlp_message,) = step(mlp_gather_kernel, [((192, width), BF)], mlp_whole, mlp_got)
    mlp_got = swap(mlp_message, "kk")
    upd_mlp = call(
        update_mlp_kernel,
        [struct(w_gu.shape, F32)] * 3 + [struct(w_down.shape, F32)] * 3,
        [places, mlp_message, mlp_got, w_gu, first_gu, second_gu, w_down, first_down, second_down],
        1,
        scratch=[pltpu.VMEM(w_gu.shape, F32)],
    )

    got = swap(after(send, low_grad, mlp_message), "bb")
    (message,) = step(gather_kernel, [((272, 512), BF)], whole, send, got)
    got = swap(after(message, upd_mlp[5]), "kk")
    own_gains = pick((joined(message) + joined(got)).reshape(-1)[: 2 * width + 2 * HD].reshape(32, 72), x_at * 8 + shard_at)
    upd_qkv = call(
        update_qkv_kernel,
        [struct(w_qkv.shape, F32)] * 3 + [struct(w_out.shape, F32)] * 3,
        [places, message, got, w_qkv, first_qkv, second_qkv, w_out, first_out, second_out],
        1,
        scratch=[pltpu.VMEM(w_qkv.shape, F32)],
    )
    upd_gains = adamw(gains, own_gains, first_gains, second_gains, RATES[4], DECAYS[4])
    return (mixed_out, input_grad, *upd_qkv, *upd_mlp, *upd_gains)


def solution(mesh):
    rows = P(("seq", "shard"), None)
    flat = P(("seq", "shard"))
    whole = P(("shard", "replica"), "seq", None)
    per_weight = (rows, rows, rows, rows, flat)
    return jax.shard_map(
        on_device,
        mesh=mesh,
        in_specs=(whole, whole) + per_weight * 3,
        out_specs=(whole, whole) + (rows,) * 12 + (flat,) * 3,
        check_vma=False,
    )
```

```python
import functools
import math

import jax
import jax.numpy as jnp
import numpy as np
from jax import lax
from jax.experimental import pallas as pl
from jax.experimental.pallas import tpu as pltpu
from jax.sharding import PartitionSpec as P

HEADS = 16
KVH = 8
HD = 128
FF = 3072
STEP = 10
EPS = 1e-06
THETA = 1000000.0
BETA_ONE = 0.9
BETA_TWO = 0.95
ADAM_EPS = 1e-08
RATES = (0.04, 0.2, 0.04, 0.03, 0.4)
DECAYS = (0.1, 0.1, 0.1, 0.1, 0.0)
NEG_FILL = -1e30

AXES = ("seq", "shard", "replica")
DEVICES = 128
BLOCK = 256
BF = jnp.bfloat16
F32 = jnp.float32
VMEM_LIMIT = 44 * 1024 * 1024
UPDATE_LIMIT = 56 * 1024 * 1024
SMALL_LIMIT = 12 * 1024 * 1024


def place_of(device):
    replica, shard, x = device % 4, (device // 4) % 8, device // 32
    return x, shard % 4, (replica // 2) * 2 + shard // 4, replica % 2


def device_at(x, y, z, k):
    return (x * 8 + (z % 2) * 4 + y) * 4 + (z // 2) * 2 + k


def flip(dim, x, y, z, k):
    return {
        "a": (x ^ 1, y, z, k),
        "b": (3 - x, y, z, k),
        "c": (x, y ^ 1, z, k),
        "d": (x, 3 - y, z, k),
        "e": (x, y, z ^ 1, k),
        "f": (x, y, 3 - z, k),
        "h": (x, y, z ^ 2, k),
        "k": (x, y, z, k ^ 1),
    }[dim]


def quarter_of(x, k):
    return k if x < 2 else 3 - k


def partners(dims):
    pairs = []
    for device in range(DEVICES):
        place = place_of(device)
        pairs.append((device, device_at(*flip(dims[place[3]], *place))))
    return pairs


def swap(value, dims):
    return lax.ppermute(value, AXES, partners(dims))


def home_pairs():
    pairs = []
    for device in range(DEVICES):
        x, y, z, k = place_of(device)
        moved = {(0, 1): (1, 0), (1, 0): (0, 1), (2, 0): (3, 1), (3, 1): (2, 0)}.get((x, k), (x, k))
        pairs.append((device, device_at(moved[0], y, z, moved[1])))
    return pairs


def rehome(value):
    return lax.ppermute(value, AXES, home_pairs())


def shard_of(place):
    return (place[2] % 2) * 4 + place[1]


def slot_places(device, steps):
    places = [place_of(device)]
    for dims in steps:
        places = places + [flip(dims[p[3]], *p) for p in places]
    return places


def row_table(steps):
    table = np.zeros((DEVICES, 32), np.int32)
    for device in range(DEVICES):
        slots = slot_places(device, ("bb", "aa") + tuple(steps))
        table[device] = [p[0] * 8 + shard_of(p) for p in slots]
    return table


def shard_table(steps):
    table = np.zeros((DEVICES, 8), np.int32)
    for device in range(DEVICES):
        table[device] = [shard_of(p) for p in slot_places(device, steps)]
    return table


STEPS_Q = ("cd", "dc", "ef")
STEPS_ROWS = ("cd", "dc", "ef")
STEPS_MLP = ("dc", "cd", "ef")
STEPS_GRAD_A = ("dc", "ef", "cd")
STEPS_GRAD_B = ("cd", "dc", "ef")
STEPS_GRAD_OUT = ("ef", "dc", "cd")
STEPS_GRAD_Q = ("cd", "ef", "dc")
STEPS_GRAD_KV = ("dc", "cd", "ef")
def block_table():
    table = np.zeros((DEVICES, 4), np.int32)
    for device in range(DEVICES):
        x, _, _, k = place_of(device)
        own = quarter_of(x, k)
        table[device] = [own, own ^ 1, own ^ 3, own ^ 2]
    return table


def x_table():
    table = np.zeros((DEVICES, 4), np.int32)
    for device in range(DEVICES):
        own = place_of(device)[0]
        table[device] = [(0, 2, 3, 1)[own ^ x] for x in range(4)]
    return table


def home_table():
    table = np.zeros((DEVICES, 1), np.int32)
    for device in range(DEVICES):
        x, _, _, k = place_of(device)
        table[device] = quarter_of(x, k) == x
    return table


TABLES = [
    row_table(STEPS_Q), row_table(STEPS_GRAD_Q), row_table(STEPS_GRAD_KV), row_table(STEPS_MLP),
    shard_table(STEPS_ROWS), shard_table(STEPS_MLP), shard_table(STEPS_GRAD_OUT),
    block_table(), x_table(), home_table(), shard_table(STEPS_GRAD_A), shard_table(STEPS_GRAD_B),
]
AT_ALL, AT_Q, AT_KV, AT_MAIN, AT_OUT, AT_DOWN, AT_GRAD_OUT, AT_BLOCK, AT_X, AT_HOME, AT_A, AT_B = np.cumsum(
    [0] + [t.shape[1] for t in TABLES[:-1]]
).tolist()
PLACES = np.concatenate(TABLES, axis=1)


def dot(left, right):
    return lax.dot_general(left, right, (((1,), (0,)), ((), ())), preferred_element_type=F32)


def dot_nt(left, right):
    return lax.dot_general(left, right, (((1,), (1,)), ((), ())), preferred_element_type=F32)


def dot_tn(left, right):
    return lax.dot_general(left, right, (((0,), (0,)), ((), ())), preferred_element_type=F32)


def at(index, size):
    return pl.ds(pl.multiple_of(index * size, size), size)


def score_pieces(keys, queries, block):
    pieces = []
    if block > 0:
        rows = slice(0, block * BLOCK)
        pieces.append((rows, dot_nt(keys[rows, :], queries)))
    rows = slice(block * BLOCK, (block + 1) * BLOCK)
    scores = dot_nt(keys[rows, :], queries)
    key = lax.broadcasted_iota(jnp.int32, scores.shape, 0)
    query = lax.broadcasted_iota(jnp.int32, scores.shape, 1) & (BLOCK - 1)
    pieces.append((rows, jnp.where(key <= query, scores, NEG_FILL)))
    return pieces


def total_of(values):
    result = values[0]
    for value in values[1:]:
        result = result + value
    return result


def double_kernel(held, got, out):
    rows = held.shape[0]
    out[0:16, :] = held[0:16, :] + got[0:16, :]
    out[16:rows, :] = held[16:rows, :]
    out[rows : 2 * rows - 16, :] = got[16:rows, :]


def norm_kernel(own, side, far, last, rows_0, rows_1, rows_2, rows_3, n1, gain_one, gain_two, gain_q, gain_k):
    rows = total_of([r[...].astype(F32) for r in (rows_0, rows_1, rows_2, rows_3)])
    gain = rows[0:1, :]
    gain_one[...] = gain
    gain_two[...] = rows[1:2, :]
    gain_q[...] = rows[2:3, 0:HD]
    gain_k[...] = rows[2:3, HD : 2 * HD]
    for slot, ref in enumerate((own, side, far, last)):
        value = ref[...].astype(F32)
        scale = lax.rsqrt(jnp.mean(value * value, axis=1, keepdims=True) + EPS)
        n1[slot * BLOCK : (slot + 1) * BLOCK, :] = (value * scale * gain).astype(BF)


def halves(rider):
    high = rider.astype(BF).astype(F32)
    return jnp.concatenate([high, rider - high], axis=0).astype(BF)


def joined(message):
    pair = message[message.shape[0] - 16 :, :].astype(F32)
    return pair[:8] + pair[8:]


def fold_kernel(q_low, q_sent, q_got, kv_low, kv_got, q_keep, q_send, kv_keep, kv_send):
    rows = kv_got.shape[0]
    half = rows // 2
    value = q_low[...].astype(F32) + q_got[:rows, :].astype(F32)
    q_keep[...] = value[:half]
    q_send[:half, :] = value[half:].astype(BF)
    q_send[half:, :] = halves(joined(q_sent) + joined(q_got))
    value = kv_low[...].astype(F32) + kv_got[...].astype(F32)
    kv_keep[...] = value[:half]
    kv_send[...] = value[half:].astype(BF)


def fold_last_kernel(q_low, q_sent, q_got, kv_low, kv_got, out_low, out_got, keep, send):
    value = q_low[...] + q_got[:128, :].astype(F32)
    keep[0:64, :] = value[:64]
    send[0:64, :] = value[64:].astype(BF)
    value = kv_low[...] + kv_got[...].astype(F32)
    keep[64:128, :] = value[:64]
    send[64:128, :] = value[64:].astype(BF)
    value = (out_low[...] + out_got[...].astype(F32)).astype(BF)
    keep[128:256, :] = value.astype(F32)
    send[128:256, :] = value
    send[256:272, :] = halves(joined(q_sent) + joined(q_got))


def sum_kernel(keep, sent, got, send):
    send[0:256, :] = (keep[0:256, :].astype(F32) + got[0:256, :].astype(F32)).astype(BF)
    send[256:272, :] = halves(joined(sent) + joined(got))


def side_kernel(sent, got, whole, send):
    value = (sent[0:256, :].astype(F32) + got[0:256, :].astype(F32)).astype(BF)
    pair = halves(joined(sent) + joined(got))
    whole[0:256, :] = value
    whole[256:272, :] = pair
    send[0:32, :] = value[32:64]
    send[32:64, :] = value[96:128]
    send[64:80, :] = pair


def gather_kernel(whole, sent, got, message):
    message[0:32, :] = whole[0:32, :]
    message[32:64, :] = whole[64:96, :]
    message[64:128, :] = got[0:64, :]
    message[128:256, :] = whole[128:256, :]
    message[256:272, :] = halves(joined(sent) + joined(got))


def fold_pair_kernel(a_low, a_got, b_low, b_got, a_keep, a_send, b_keep, b_send):
    for low, got, keep, send in ((a_low, a_got, a_keep, a_send), (b_low, b_got, b_keep, b_send)):
        half = low.shape[0] // 2
        for slot in range(2 * half):
            value = (low[slot].astype(F32) + got[slot].astype(F32)).astype(BF)
            if slot < half:
                keep[slot] = value
            else:
                send[slot - half] = value


def fold_pair_last_kernel(a_low, a_got, b_low, b_got, keep, send):
    value = (a_low[0].astype(F32) + a_got[0].astype(F32)).astype(BF)
    keep[...] = value[0:96]
    send[0:48, :] = value[96:144]
    send[48:192, :] = (b_low[0].astype(F32) + b_got[0].astype(F32)).astype(BF)


def mlp_sum_kernel(keep, send, got, out):
    out[0:96, :] = (keep[...].astype(F32) + got[0:96, :].astype(F32)).astype(BF)
    out[96:192, :] = (send[96:192, :].astype(F32) + got[96:192, :].astype(F32)).astype(BF)


def mlp_side_kernel(low, got, whole, send):
    value = (low[...].astype(F32) + got[...].astype(F32)).astype(BF)
    whole[...] = value
    send[...] = value[32:96]


def mlp_gather_kernel(whole, got, message):
    message[0:32, :] = whole[0:32, :]
    message[32:64, :] = got[0:32, :]
    message[64:96, 0:512] = whole[64:96, 0:512]
    message[64:96, 512:1024] = got[32:64, 512:1024]
    message[96:192, :] = whole[96:192, :]


def state_kernel(keep, got, far, tokens, gain, state, n2):
    value = tokens[...].astype(F32) + keep[...] + got[0].astype(F32) + far[...].astype(F32)
    state[...] = value
    scale = lax.rsqrt(jnp.mean(value * value, axis=1, keepdims=True) + EPS)
    n2[...] = (value * scale * gain[...]).astype(BF)


def far_kernel(part, keep, got, out):
    out[...] = (keep[...] + got[part].astype(F32)).astype(BF)


def state_back_kernel(keep, got, far, state, mix, gain, grad, low, grad_gain):
    grad_n2 = keep[...] + got[0].astype(F32) + far[...].astype(F32)
    value = state[...]
    scale = lax.rsqrt(jnp.mean(value * value, axis=1, keepdims=True) + EPS)
    unit = value * scale
    scaled = grad_n2 * gain[...]
    result = mix[...].astype(F32) + scale * (scaled - unit * jnp.mean(scaled * unit, axis=1, keepdims=True))
    grad[...] = result
    low[...] = result.astype(BF)
    grad_gain[...] = jnp.sum(grad_n2 * unit, axis=0, keepdims=True)


def input_back_kernel(keep, got, far, tokens, grad_state, gain, low):
    grad_n1 = keep[...] + got[0].astype(F32) + far[...].astype(F32)
    value = tokens[...].astype(F32)
    scale = lax.rsqrt(jnp.mean(value * value, axis=1, keepdims=True) + EPS)
    unit = value * scale
    scaled = grad_n1 * gain[...]
    result = grad_state[...] + scale * (scaled - unit * jnp.mean(scaled * unit, axis=1, keepdims=True))
    low[...] = result.astype(BF)


def columns(start, size):
    return pl.ds(pl.multiple_of(start, 128), size)


def update_refs(refs, gradient, outs, rate, decay_rate):
    results = adamw(refs[0][...], gradient, refs[1][...], refs[2][...], rate, decay_rate)
    for out, result in zip(outs, results):
        out[...] = result


def update_qkv_kernel(places, message, got, w_q, m_q, s_q, w_o, m_o, s_o, *outs):
    gradient = outs[6]
    for slot, (ref, row) in enumerate(((message, 0), (got, 0), (message, 64), (got, 64))):
        quarter = places[AT_BLOCK + slot]
        gradient[:, columns(quarter * 512, 512)] = ref[row : row + 32, :].astype(F32)
        gradient[:, columns(2048 + quarter * 256, 256)] = ref[row + 32 : row + 64, 0:256].astype(F32)
        gradient[:, columns(3072 + quarter * 256, 256)] = ref[row + 32 : row + 64, 256:512].astype(F32)
    update_refs((w_q, m_q, s_q), gradient[...], outs[0:3], RATES[0], DECAYS[0])
    home = places[AT_HOME] == 1
    for half in range(2):
        here = slice(half * 512, half * 512 + 512)
        rows = slice(128 + half * 64, 192 + half * 64)
        part = jnp.where(home, message[rows, :].astype(F32), got[rows, :].astype(F32))
        refs = (w_o.at[:, here], m_o.at[:, here], s_o.at[:, here])
        update_refs(refs, part, [out.at[:, here] for out in outs[3:6]], RATES[1], DECAYS[1])


def update_mlp_kernel(places, message, got, w_g, m_g, s_g, w_d, m_d, s_d, *outs):
    gradient = outs[6]
    part = FF // 4
    for slot, (ref, side) in enumerate(((message, 0), (got, 0), (message, 1), (got, 1))):
        quarter = places[AT_BLOCK + slot]
        main = ref[side * 32 : side * 32 + 32, :].astype(F32)
        gradient[:, columns(quarter * part, part)] = main[:, :part]
        gradient[:, columns(FF + quarter * part, 1024 - part)] = main[:, part:]
        gradient[:, columns(FF + quarter * part + 1024 - part, 512)] = ref[
            64:96, side * 512 : side * 512 + 512
        ].astype(F32)
    update_refs((w_g, m_g, s_g), gradient[...], outs[0:3], RATES[2], DECAYS[2])
    home = places[AT_HOME] == 1
    total = jnp.where(home, message[96:192, :].astype(F32), got[96:192, :].astype(F32))
    update_refs((w_d, m_d, s_d), total, outs[3:6], RATES[3], DECAYS[3])


def attention_kernel(
    places, n1, w_0, w_1, w_2, w_3, cos, sin, gain_q, gain_k, w_all, pre, q_out, k_out, v_out, att, log_total
):
    factor = 1.0 / math.sqrt(HD)
    for slot in range(32):
        row = 16 + (slot % 8) * 32
        w_all[at(places[AT_ALL + slot], 32), :] = (w_0, w_1, w_2, w_3)[slot // 8][row : row + 32, :]
    for slot in range(4):
        block = places[AT_BLOCK + slot]
        here = at(block, BLOCK)
        projected = dot(n1[slot * BLOCK : (slot + 1) * BLOCK, :], w_all[...])
        pre[here, :] = projected[:, :768]
        cos_part = cos[here, :]
        sin_part = sin[here, :]

        def turned(column, gain):
            head = projected[:, column : column + HD]
            normed = head * lax.rsqrt(jnp.mean(head * head, axis=1, keepdims=True) + EPS) * gain[...]
            return normed * cos_part + pltpu.roll(normed, HD // 2, 1) * sin_part

        for head in range(4):
            rotated = (turned(head * HD, gain_q) * factor).astype(BF)
            q_out[head // 2, block, (head % 2) * BLOCK : (head % 2 + 1) * BLOCK, :] = rotated
        for head in range(2):
            k_out[head, here, :] = turned(512 + head * HD, gain_k).astype(BF)
            v_out[head, here, :] = projected[:, 768 + head * HD : 768 + (head + 1) * HD].astype(BF)
    for group in range(2):
        for block in range(4):
            pieces = score_pieces(k_out.at[group], q_out[group, block], block)
            top = jnp.max(pieces[0][1], axis=0, keepdims=True)
            for _, scores in pieces[1:]:
                top = jnp.maximum(top, jnp.max(scores, axis=0, keepdims=True))
            exponents = [(rows_here, jnp.exp(scores - top)) for rows_here, scores in pieces]
            sums = total_of([jnp.sum(e, axis=0, keepdims=True) for _, e in exponents])
            inverse = 1.0 / sums
            attended = total_of(
                [dot_tn(v_out[group, rows_here, :], (e * inverse).astype(BF)) for rows_here, e in exponents]
            )
            attended = attended.T.astype(BF)
            log_total[group * 4 + block : group * 4 + block + 1, :] = top + jnp.log(sums)
            own = places[AT_BLOCK] ^ block
            slot = own ^ (own >> 1)
            for head in range(2):
                column = (group * 2 + head) * HD
                att[at(slot, BLOCK), column : column + HD] = attended[head * BLOCK : (head + 1) * BLOCK]


def attention_back_kernel(
    places, own, side, far, last, w_out, queries, keys, values, pre, log_total, cos, sin, gain_q, gain_k,
    grad_pre, grad_gain_q, grad_gain_k, grad_att, grad_k, grad_v,
):
    factor = 1.0 / math.sqrt(HD)
    for slot, ref in enumerate((own, side, far, last)):
        part = dot_nt(ref[...], w_out[...]).astype(BF)
        for head in range(4):
            grad_att[head // 2, places[AT_BLOCK + slot], (head % 2) * BLOCK : (head % 2 + 1) * BLOCK, :] = part[
                :, head * HD : (head + 1) * HD
            ]

    def back_through(grad, head, cos_part, sin_part, gain):
        turned = grad * cos_part - pltpu.roll(grad, HD // 2, 1) * sin_part
        scale = lax.rsqrt(jnp.mean(head * head, axis=1, keepdims=True) + EPS)
        unit = head * scale
        scaled = turned * gain[...]
        grad_head = scale * (scaled - unit * jnp.mean(scaled * unit, axis=1, keepdims=True))
        return grad_head, jnp.sum(turned * unit, axis=0, keepdims=True)

    total_q = jnp.zeros((1, HD), F32)
    total_k = jnp.zeros((1, HD), F32)
    for group in range(2):
        for block in range(3, -1, -1):
            own = places[AT_BLOCK] ^ block
            there = at(own ^ (own >> 1), BLOCK)
            query = queries[group, block]
            grad_o = grad_att[group, block]
            logs = log_total[group * 4 + block : group * 4 + block + 1, :]
            probs = [(r, jnp.exp(scores - logs)) for r, scores in score_pieces(keys.at[group], query, block)]
            grad_probs = [dot_nt(values[group, r, :], grad_o) for r, _ in probs]
            inner = total_of([jnp.sum(p * g, axis=0, keepdims=True) for (_, p), g in zip(probs, grad_probs)])
            grad_scores = [(r, (p * (g - inner)).astype(BF)) for (r, p), g in zip(probs, grad_probs)]
            grad_q = total_of([dot_tn(keys[group, r, :], d) for r, d in grad_scores]).T * factor
            for (r, p), (_, d) in zip(probs, grad_scores):
                part_k = dot(d, query)
                part_v = dot(p.astype(BF), grad_o)
                if block == 3:
                    grad_k[r, :] = part_k
                    grad_v[r, :] = part_v
                else:
                    grad_k[r, :] += part_k
                    grad_v[r, :] += part_v
            for head in range(2):
                column = (group * 2 + head) * HD
                grad_head, gain_part = back_through(
                    grad_q[head * BLOCK : (head + 1) * BLOCK],
                    pre[block * BLOCK : (block + 1) * BLOCK, column : column + HD],
                    cos[block * BLOCK : (block + 1) * BLOCK, :],
                    sin[block * BLOCK : (block + 1) * BLOCK, :],
                    gain_q,
                )
                total_q = total_q + gain_part
                grad_pre[there, column : column + HD] = grad_head.astype(BF)
        for block in range(4):
            own = places[AT_BLOCK] ^ block
            there = at(own ^ (own >> 1), BLOCK)
            column = 512 + group * HD
            grad_head, gain_part = back_through(
                grad_k[block * BLOCK : (block + 1) * BLOCK, :],
                pre[block * BLOCK : (block + 1) * BLOCK, column : column + HD],
                cos[block * BLOCK : (block + 1) * BLOCK, :],
                sin[block * BLOCK : (block + 1) * BLOCK, :],
                gain_k,
            )
            total_k = total_k + gain_part
            grad_pre[there, column : column + HD] = grad_head.astype(BF)
            grad_pre[there, 768 + group * HD : 768 + (group + 1) * HD] = grad_v[
                block * BLOCK : (block + 1) * BLOCK, :
            ].astype(BF)
    grad_gain_q[...] = total_q
    grad_gain_k[...] = total_k


def out_kernel(places, att, low_slots, high_slots, w_out, keep_own, keep_far, send):
    for slot in range(8):
        slots = low_slots if slot < 4 else high_slots
        w_out[at(places[AT_OUT + slot], 64), :] = slots[slot % 4]
    for slot in range(4):
        part = dot(att[slot * BLOCK : (slot + 1) * BLOCK, :], w_out[...])
        if slot % 2 == 1:
            send[slot // 2] = part.astype(BF)
        else:
            (keep_own if slot == 0 else keep_far)[...] = part


def out_weights_kernel(places, att, own, side, far, last, low, high, scratch):
    total = jnp.zeros(scratch.shape, F32)
    for slot, ref in enumerate((own, side, far, last)):
        total = total + dot_tn(att[slot * BLOCK : (slot + 1) * BLOCK, :], ref[...])
    scratch[...] = total.astype(BF)
    for slot in range(8):
        target = low if slot < 4 else high
        for half in range(2):
            there = (slot % 4) * 128 + half * 64
            target[there : there + 64, :] = scratch[at(places[AT_GRAD_OUT + slot], 64), half * 512 : half * 512 + 512]


def mlp_kernel(
    places, n2_first, n2_second, mix_first, mix_second, low_slots, high_slots,
    hidden, grad_gu, mix_keep, grad_keep, send, w_gu, w_down,
):
    for slot in range(8):
        ref = low_slots if slot < 4 else high_slots
        for x in range(4):
            start, side = (x // 2) * 96, x % 2
            here = at(places[AT_MAIN + slot * 4 + x], 32)
            w_gu[here, 0:1024] = ref[slot % 4, start + side * 32 : start + side * 32 + 32, :]
            w_gu[here, 1024:1536] = ref[slot % 4, start + 64 : start + 96, side * 512 : side * 512 + 512]
        w_down[at(places[AT_DOWN + slot], 96), :] = ref[slot % 4, 192:288, :]
    half = FF // 4
    for slot, (n2, grad_mix) in enumerate(((n2_first, mix_first), (n2_second, mix_second))):
        here = slice(slot * BLOCK, (slot + 1) * BLOCK)
        gate_up = dot(n2[...], w_gu[...])
        grad_hidden = dot_nt(grad_mix[...], w_down[...])
        gate = gate_up[:, :half]
        up = gate_up[:, half:]
        sigmoid = 1.0 / (1.0 + jnp.exp(-gate))
        silu = gate * sigmoid
        low_hidden = (silu * up).astype(BF)
        hidden[here, :] = low_hidden
        grad_gate = grad_hidden * up * (sigmoid * (1.0 + gate * (1.0 - sigmoid)))
        low_grad = jnp.concatenate([grad_gate, grad_hidden * silu], axis=1).astype(BF)
        grad_gu[here, :] = low_grad
        back = dot_nt(low_grad, w_gu[...])
        mixed = dot(low_hidden, w_down[...])
        if slot == 0:
            grad_keep[...] = back
            mix_keep[...] = mixed
        else:
            send[0] = back.astype(BF)
            send[1] = mixed.astype(BF)


def mlp_weights_kernel(
    places, n2_0, n2_1, n2_2, n2_3, mix_0, mix_1, mix_2, mix_3, hidden_own, hidden_far, gu_own, gu_far,
    a_low, a_high, b_low, b_high, out, total,
):
    n2s, mixes = (n2_0, n2_1, n2_2, n2_3), (mix_0, mix_1, mix_2, mix_3)

    def tokens(near, far, slot):
        ref = near if slot < 2 else far
        return ref, slice((slot % 2) * BLOCK, (slot % 2 + 1) * BLOCK)

    for x in range(4):
        here = slice(x * BLOCK, (x + 1) * BLOCK)
        part = jnp.zeros((BLOCK, 2 * FF // 4), F32)
        for slot in range(4):
            ref, rows = tokens(gu_own, gu_far, slot)
            part = part + dot_tn(n2s[slot][:, here], ref[rows, :])
        total[places[AT_X + x]] = part.astype(BF).reshape(8, 32, 2 * FF // 4)
    for slot in range(4):
        start = (slot // 2) * 96
        side = slot % 2
        out[:, start + side * 32 : start + side * 32 + 32, :] = total[slot, :, :, 0:1024]
        out[:, start + 64 : start + 96, side * 512 : side * 512 + 512] = total[slot, :, :, 1024:1536]
    for third in range(3):
        here = slice(third * BLOCK, (third + 1) * BLOCK)
        part = jnp.zeros((BLOCK, out.shape[2]), F32)
        for slot in range(4):
            ref, rows = tokens(hidden_own, hidden_far, slot)
            part = part + dot_tn(ref[rows, here], mixes[slot][...])
        total_down = part.astype(BF)
        for piece in range(8):
            row = third * BLOCK + piece * 32
            out[row // 96, 192 + row % 96 : 192 + row % 96 + 32, :] = total_down[piece * 32 : piece * 32 + 32]
    for slot in range(8):
        (a_low if slot < 4 else a_high)[slot % 4] = out[places[AT_A + slot], 0:144, :]
        (b_low if slot < 4 else b_high)[slot % 4] = out[places[AT_B + slot], 144:288, :]


def qkv_back_kernel(
    places, n1, grad_pre, w_all, own, side, far, last, gain_two, gain_q, gain_k,
    q_low, q_high, kv_low, kv_high, keep_own, keep_far, send, total,
):
    for x in range(4):
        here = slice(x * BLOCK, (x + 1) * BLOCK)
        total[here, :] = dot_tn(n1[:, here], grad_pre[...]).astype(BF)
    for slot in range(32):
        there = slice((slot % 16) * 32, (slot % 16) * 32 + 32)
        (q_low if slot < 16 else q_high)[there, :] = total[at(places[AT_Q + slot], 32), 0:512]
        (kv_low if slot < 16 else kv_high)[there, :] = total[at(places[AT_KV + slot], 32), 512:1024]
    gain_sum = jnp.zeros((1, n1.shape[1]), F32)
    for slot, ref in enumerate((own, side, far, last)):
        part = dot_nt(grad_pre[slot * BLOCK : (slot + 1) * BLOCK, :], w_all[...])
        value = ref[...].astype(F32)
        scale = lax.rsqrt(jnp.mean(value * value, axis=1, keepdims=True) + EPS)
        gain_sum = gain_sum + jnp.sum(part * (value * scale), axis=0, keepdims=True)
        if slot % 2 == 1:
            send[slot // 2] = part.astype(BF)
        else:
            (keep_own if slot == 0 else keep_far)[...] = part
    rows = [gain_sum[:, :512], gain_sum[:, 512:], gain_two[:, :512], gain_two[:, 512:]]
    rows += [jnp.concatenate([gain_q[...], gain_k[...], jnp.zeros((1, 256), F32)], axis=1), jnp.zeros((3, 512), F32)]
    q_high[512:528, :] = halves(jnp.concatenate(rows, axis=0))


def far_sum(part, keep, got):
    kernel = functools.partial(far_kernel, part)
    return call(kernel, [struct(keep.shape, BF)], [keep, got], 0, small=True)[0]


def call(kernel, outs, args, scalars, scratch=(), flops=0, small=False, update=False):
    space = [pl.BlockSpec(memory_space=pltpu.SMEM)] * scalars
    space += [pl.BlockSpec(memory_space=pltpu.VMEM)] * (len(args) - scalars)
    size = sum(math.prod(a.shape) * a.dtype.itemsize for a in list(args) + list(outs))
    return pl.pallas_call(
        kernel,
        out_shape=outs,
        in_specs=space,
        out_specs=[pl.BlockSpec(memory_space=pltpu.VMEM)] * len(outs),
        scratch_shapes=list(scratch),
        compiler_params=pltpu.CompilerParams(vmem_limit_bytes=SMALL_LIMIT if small else UPDATE_LIMIT if update else VMEM_LIMIT),
        cost_estimate=pl.CostEstimate(flops=flops, bytes_accessed=size, transcendentals=0),
    )(*args)


def struct(shape, dtype):
    return jax.ShapeDtypeStruct(shape, dtype)


def rms_scale(value, gain):
    return value * lax.rsqrt(jnp.mean(value * value, axis=-1, keepdims=True) + EPS) * gain


def rms_back(value, gain, grad):
    scale = lax.rsqrt(jnp.mean(value * value, axis=-1, keepdims=True) + EPS)
    scaled = grad * gain
    inner = jnp.mean(scaled * value, axis=-1, keepdims=True)
    grad_value = scale * scaled - value * (scale * scale * scale) * inner
    return grad_value, jnp.sum(grad * value * scale, axis=0)


def adamw(weight, gradient, first_moment, second_moment, rate, decay_rate):
    first_moment = BETA_ONE * first_moment + (1.0 - BETA_ONE) * gradient
    second_moment = BETA_TWO * second_moment + (1.0 - BETA_TWO) * gradient * gradient
    first_hat = first_moment / (1.0 - BETA_ONE**STEP)
    second_hat = second_moment / (1.0 - BETA_TWO**STEP)
    weight = weight - rate * (first_hat / (jnp.sqrt(second_hat) + ADAM_EPS) + decay_rate * weight)
    return (weight, first_moment, second_moment)


def rounded(value):
    return lax.reduce_precision(value.astype(F32), 8, 7)


def after(value, *others):
    return lax.optimization_barrier((value,) + others)[0]


def pick(stack, index):
    return lax.dynamic_index_in_dim(stack, index, 0, keepdims=False)


def on_device(
    tokens,
    cotangent,
    w_qkv,
    w_out,
    w_gu,
    w_down,
    gains,
    first_qkv,
    first_out,
    first_gu,
    first_down,
    first_gains,
    second_qkv,
    second_out,
    second_gu,
    second_down,
    second_gains,
):
    width = tokens.shape[-1]
    x_at = lax.axis_index("seq")
    shard_at = lax.axis_index("shard")
    replica_at = lax.axis_index("replica")
    device = (x_at * 8 + shard_at) * 4 + replica_at
    core = replica_at % 2
    quarter = jnp.where(x_at < 2, core, 3 - core)
    places = pick(jnp.asarray(PLACES), device)

    positions = jnp.arange(4 * BLOCK, dtype=F32)
    frequency = THETA ** (-jnp.arange(HD // 2, dtype=F32) / (HD // 2))
    angles = positions[:, None] * frequency[None, :]
    cos_half, sin_half = jnp.cos(angles), jnp.sin(angles)
    cos_table = jnp.concatenate([cos_half, cos_half], axis=1)
    sin_table = jnp.concatenate([-sin_half, sin_half], axis=1)

    low_qkv = w_qkv.astype(BF)
    stack_qkv = jnp.stack(
        [
            jnp.concatenate(
                [
                    low_qkv[:, 512 * n : 512 * (n + 1)],
                    low_qkv[:, 2048 + 256 * n : 2304 + 256 * n],
                    low_qkv[:, 3072 + 256 * n : 3328 + 256 * n],
                ],
                axis=1,
            )
            for n in range(4)
        ]
    )
    spot = (jnp.arange(32) == x_at * 8 + shard_at)[:, None]
    gain_vals = jnp.where(spot, gains[None, :], 0.0).reshape(1, -1)
    gain_vals = jnp.pad(gain_vals, ((0, 0), (0, 3 * 1024 - 32 * 72))).reshape(3, 1024)
    gain_rows = jnp.pad(gain_vals, ((0, 13), (0, 0))).astype(BF)

    def doubled(held, got):
        return call(double_kernel, [struct((2 * held.shape[0] - 16, 1024), BF)], [held, got], 0, small=True)[0]

    qkv_one = jnp.concatenate([gain_rows, pick(stack_qkv, quarter)], axis=0)
    sent = jnp.concatenate([gain_rows, pick(stack_qkv, 3 - quarter)], axis=0)
    qkv_two = doubled(qkv_one, swap(sent, "bb"))
    qkv_four = doubled(qkv_two, swap(qkv_two, "aa"))
    qkv_eight = doubled(qkv_four, swap(qkv_four, STEPS_Q[0]))

    low_gu = after(w_gu, qkv_four).astype(BF)
    part = FF // 4
    stack_gu = jnp.stack(
        [
            jnp.concatenate(
                [low_gu[:, part * n : part * (n + 1)], low_gu[:, FF + part * n : FF + part * (n + 1)]], axis=1
            )
            for n in range(4)
        ]
    )
    gu_one = pick(stack_gu, quarter)[None]
    gu_two = jnp.concatenate([gu_one, swap(pick(stack_gu, 3 - quarter)[None], "bb")], axis=0)

    first = rehome(jnp.concatenate([tokens[0], w_out.astype(BF), w_down.astype(BF)], axis=0))
    own_tokens = first[:BLOCK]
    out_one = first[None, BLOCK : BLOCK + 64]
    down_one = first[BLOCK + 64 :]
    far_tokens = swap(after(own_tokens, gu_two), "bb")
    side_tokens = swap(after(own_tokens, qkv_eight), "kk")

    qkv_next = swap(qkv_eight, STEPS_Q[1])
    qkv_parts = [qkv_eight, qkv_next, swap(qkv_eight, STEPS_Q[2]), swap(qkv_next, STEPS_Q[2])]
    gu_four = jnp.concatenate([gu_two, swap(after(gu_two, qkv_eight, cos_table, sin_table, places), "aa")], axis=0)
    last_tokens = swap(far_tokens, "kk")
    own_mix = rehome(after(cotangent[0], gu_four))
    far_mix = swap(after(own_mix, far_tokens), "bb")
    side_mix = swap(after(own_mix, qkv_next), "kk")
    out_two = jnp.concatenate([out_one, swap(after(out_one, qkv_eight), STEPS_ROWS[0])], axis=0)
    out_low = jnp.concatenate([out_two, swap(out_two, STEPS_ROWS[1])], axis=0)
    out_high = swap(out_low, STEPS_ROWS[2])

    last = gu_four[:, :, 1024:]
    mlp_one = jnp.concatenate(
        [
            gu_four[0, :, :1024], gu_four[1, :, :1024], jnp.concatenate([last[0], last[1]], axis=1),
            gu_four[2, :, :1024], gu_four[3, :, :1024], jnp.concatenate([last[2], last[3]], axis=1),
            down_one,
        ],
        axis=0,
    )[None]
    mlp_two = jnp.concatenate([mlp_one, swap(after(mlp_one, out_low, qkv_next), STEPS_MLP[0])], axis=0)

    total = 4 * BLOCK
    n1, gain_one, gain_two, gain_query, gain_key = call(
        norm_kernel,
        [struct((total, width), BF)] + [struct((1, width), F32)] * 2 + [struct((1, HD), F32)] * 2,
        [own_tokens, side_tokens, far_tokens, last_tokens] + [piece[:16] for piece in qkv_parts],
        0,
        small=True,
    )
    w_all, pre, queries, keys, values, att, log_total = call(
        attention_kernel,
        [
            struct((width, 1024), BF),
            struct((total, 768), F32),
            struct((2, 4, 2 * BLOCK, HD), BF),
            struct((2, total, HD), BF),
            struct((2, total, HD), BF),
            struct((total, 512), BF),
            struct((8, 2 * BLOCK), F32),
        ],
        [
            places, n1, *qkv_parts,
            cos_table, sin_table, gain_query, gain_key,
        ],
        1,
        flops=14_000_000_000,
    )
    last_mix = swap(after(far_mix, att), "kk")
    mlp_low = jnp.concatenate([mlp_two, swap(after(mlp_two, out_low), STEPS_MLP[1])], axis=0)
    mlp_high = swap(after(mlp_low, att), STEPS_MLP[2])
    w_out_all, out_own, out_keep, out_send = call(
        out_kernel,
        [struct((512, width), BF)] + [struct((BLOCK, width), F32)] * 2 + [struct((2, BLOCK, width), BF)],
        [places, after(att, mlp_low, far_mix), out_low, out_high],
        1,
        flops=4_500_000_000,
    )
    got_out = swap(out_send, "kk")
    out_far = far_sum(1, out_keep, got_out)
    state, n2 = call(
        state_kernel,
        [struct((BLOCK, width), F32), struct((BLOCK, width), BF)],
        [out_own, got_out, swap(out_far, "bb"), own_tokens, gain_two],
        0,
        small=True,
    )
    far_n2 = swap(n2, "bb")
    side_n2 = swap(n2, "kk")


    def mlp(*parts):
        return call(
            mlp_kernel,
            [
                struct((2 * BLOCK, part), BF),
                struct((2 * BLOCK, 2 * part), BF),
                struct((BLOCK, width), F32),
                struct((BLOCK, width), F32),
                struct((2, BLOCK, width), BF),
            ],
            [places, *parts, mlp_low, mlp_high],
            1,
            scratch=[pltpu.VMEM((width, 2 * part), BF), pltpu.VMEM((part, width), BF)],
            flops=10_400_000_000,
        )

    hidden_own, gu_own, mix_keep_own, back_keep_own, send_own = mlp(n2, side_n2, own_mix, side_mix)
    far_n2 = after(far_n2, send_own)
    last_n2 = swap(far_n2, "kk")
    hidden_far, gu_far, mix_keep_far, back_keep_far, send_far = mlp(
        far_n2, last_n2, far_mix, last_mix
    )
    got_far = swap(send_far, "kk")
    got_own = swap(after(send_own, got_far), "kk")
    back_far = far_sum(0, back_keep_far, got_far)
    back_arrived = swap(back_far, "bb")
    grad_mlp_parts = call(
        mlp_weights_kernel,
        [struct((4, 144, width), BF)] * 4,
        [
            places, after(n2, back_far), side_n2, far_n2, last_n2, own_mix, side_mix, far_mix, last_mix,
            hidden_own, hidden_far, gu_own, gu_far,
        ],
        1,
        scratch=[pltpu.VMEM((8, 288, width), BF), pltpu.VMEM((4, 8, 32, 2 * part), BF)],
        flops=12_200_000_000,
    )
    grad_state, low_state, grad_gain_two = call(
        state_back_kernel,
        [struct((BLOCK, width), F32), struct((BLOCK, width), BF), struct((1, width), F32)],
        [back_keep_own, got_own, after(back_arrived, grad_mlp_parts[1]), state, own_mix, gain_two],
        0,
        small=True,
    )
    far_state = swap(low_state, "bb")
    side_state = swap(low_state, "kk")
    last_state = swap(far_state, "kk")

    def fold_mlp(a_low, a_high, b_low, b_high, index, tie):
        slots = a_low.shape[0] // 2
        outs = [struct((slots, 144, width), BF)] * 4
        args = [
            a_low, after(swap(after(a_high, tie), STEPS_GRAD_A[index]), b_high),
            b_low, swap(after(b_high, tie), STEPS_GRAD_B[index]),
        ]
        if slots == 0:
            kernel, outs = fold_pair_last_kernel, [struct((96, width), BF), struct((192, width), BF)]
        else:
            kernel = fold_pair_kernel
        return call(kernel, outs, args, 0, small=True)

    mlp_grads = fold_mlp(*grad_mlp_parts, 2, low_state)

    out_grads = call(
        out_weights_kernel,
        [struct((512, 512), BF)] * 2,
        [places, att, low_state, side_state, far_state, last_state],
        1,
        scratch=[pltpu.VMEM((512, width), BF)],
        flops=3_500_000_000,
    )
    grad_low, grad_high = out_grads
    got_grad = swap(grad_high, STEPS_GRAD_OUT[2])
    mix_far = (mix_keep_far + got_far[1].astype(F32)).astype(BF)
    mix_arrived = swap(after(mix_far, last_state), "bb")
    grad_pre, grad_gain_query, grad_gain_key = call(
        attention_back_kernel,
        [struct((total, 1024), BF), struct((1, HD), F32), struct((1, HD), F32)],
        [
            places, after(low_state, grad_low, mlp_grads[0]), side_state, far_state, last_state, w_out_all, queries, keys, values, pre,
            log_total, cos_table, sin_table, gain_query, gain_key,
        ],
        1,
        scratch=[
            pltpu.VMEM((2, 4, 2 * BLOCK, HD), BF), pltpu.VMEM((total, HD), F32), pltpu.VMEM((total, HD), F32)
        ],
        flops=18_000_000_000,
    )
    grad_total = grad_low.astype(F32) + after(got_grad, grad_pre).astype(F32)
    grad_low, grad_high = grad_total[:256], grad_total[256:].astype(BF)
    got_grad = swap(grad_high, STEPS_GRAD_OUT[1])
    mlp_grads = fold_mlp(*mlp_grads, 1, mlp_grads[1])
    q_low, q_high, kv_low, kv_high, in_own, in_keep, in_send = call(
        qkv_back_kernel,
        [struct((512, 512), BF), struct((528, 512), BF), struct((512, 512), BF), struct((512, 512), BF)]
        + [struct((BLOCK, width), F32)] * 2
        + [struct((2, BLOCK, width), BF)],
        [
            places, after(n1, mix_arrived, grad_high, mlp_grads[0]), grad_pre, w_all, own_tokens, side_tokens, far_tokens, last_tokens,
            grad_gain_two, grad_gain_query, grad_gain_key,
        ],
        1,
        scratch=[pltpu.VMEM((width, 1024), BF)],
        flops=11_000_000_000,
    )
    def step(kernel, outs, *args):
        return call(kernel, [struct(*out) for out in outs], args, 0, small=True)

    def fold(rows, q, kv, index, *ties):
        q_got = swap(after(q[1], *ties) if ties else q[1], STEPS_GRAD_Q[index])
        kv_got = swap(kv[1], STEPS_GRAD_KV[index])
        half = rows // 2
        outs = [((half, 512), F32), ((half + 16, 512), BF), ((half, 512), F32), ((half, 512), BF)]
        result = step(fold_kernel, outs, q[0], q[1], q_got, kv[0], kv_got)
        return result[0:2], result[2:4]

    mlp_keep, mlp_send = fold_mlp(*mlp_grads, 0, mlp_grads[1])
    in_send = after(in_send, mlp_send, got_grad)
    kv_high = after(kv_high, mlp_send, got_grad)
    got_in = swap(in_send, "kk")
    in_far = far_sum(1, in_keep, got_in)
    in_arrived = swap(in_far, "bb")

    q, kv = fold(512, (q_low, q_high), (kv_low, kv_high), 2, got_grad, mlp_send)
    grad_total = grad_low + got_grad.astype(F32)
    grad_low, grad_high = grad_total[:128], grad_total[128:]
    got_grad = swap(grad_high.astype(BF), STEPS_GRAD_OUT[0])
    mixed = state + (mix_keep_own + got_own[1].astype(F32)) + after(mix_arrived, q[1]).astype(F32)

    mlp_send = after(mlp_send, q[1])
    mlp_got = swap(mlp_send, "aa")
    (mlp_rows,) = step(mlp_sum_kernel, [((192, width), BF)], mlp_keep, mlp_send, mlp_got)

    q, kv = fold(256, q, kv, 1, in_arrived, got_grad)
    q_got = swap(after(q[1], mlp_got), STEPS_GRAD_Q[0])
    kv_got = swap(kv[1], STEPS_GRAD_KV[0])
    keep, send = step(
        fold_last_kernel,
        [((256, 512), F32), ((272, 512), BF)],
        q[0], q[1], q_got, kv[0], kv_got, grad_low, got_grad,
    )
    mlp_got = swap(mlp_rows, "hh")
    mlp_whole, mlp_send = step(mlp_side_kernel, [((192, width), BF), ((64, width), BF)], mlp_rows, mlp_got)

    got = swap(send, "aa")
    (send_next,) = step(sum_kernel, [((272, 512), BF)], keep, send, got)
    (low_grad,) = step(
        input_back_kernel,
        [((BLOCK, width), BF)],
        in_own, got_in, in_arrived, own_tokens, grad_state, gain_one,
    )
    returned = rehome(after(jnp.concatenate([mixed.astype(BF), low_grad], axis=0), got))
    mixed_out = returned[None, :BLOCK]
    input_grad = returned[None, BLOCK:].astype(F32)
    got = swap(after(send_next, mlp_send), "hh")
    whole, send = step(side_kernel, [((272, 512), BF), ((80, 512), BF)], send_next, got)

    mlp_got = swap(mlp_send, "bb")
    (mlp_message,) = step(mlp_gather_kernel, [((192, width), BF)], mlp_whole, mlp_got)
    mlp_got = swap(mlp_message, "kk")
    upd_mlp = call(
        update_mlp_kernel,
        [struct(w_gu.shape, F32)] * 3 + [struct(w_down.shape, F32)] * 3,
        [places, mlp_message, mlp_got, w_gu, first_gu, second_gu, w_down, first_down, second_down],
        1,
        scratch=[pltpu.VMEM(w_gu.shape, F32)],
        update=True,
    )

    got = swap(after(send, low_grad, mlp_message), "bb")
    (message,) = step(gather_kernel, [((272, 512), BF)], whole, send, got)
    got = swap(after(message, upd_mlp[5]), "kk")
    own_gains = pick((joined(message) + joined(got)).reshape(-1)[: 2 * width + 2 * HD].reshape(32, 72), x_at * 8 + shard_at)
    upd_qkv = call(
        update_qkv_kernel,
        [struct(w_qkv.shape, F32)] * 3 + [struct(w_out.shape, F32)] * 3,
        [places, message, got, w_qkv, first_qkv, second_qkv, w_out, first_out, second_out],
        1,
        scratch=[pltpu.VMEM(w_qkv.shape, F32)],
        update=True,
    )
    upd_gains = adamw(gains, own_gains, first_gains, second_gains, RATES[4], DECAYS[4])
    return (mixed_out, input_grad, *upd_qkv, *upd_mlp, *upd_gains)


def solution(mesh):
    rows = P(("seq", "shard"), None)
    flat = P(("seq", "shard"))
    whole = P(("shard", "replica"), "seq", None)
    per_weight = (rows, rows, rows, rows, flat)
    return jax.shard_map(
        on_device,
        mesh=mesh,
        in_specs=(whole, whole) + per_weight * 3,
        out_specs=(whole, whole) + (rows,) * 12 + (flat,) * 3,
        check_vma=False,
    )
```
